32 devices in a mesh: dp: 8 (over z, y), mp: 4 (over x, core).
Axes of the slice: x: 2, y: 2, z: 4, core: 2. Of those that a mesh axis runs over, the one named last changes fastest.
Arguments:
- block_input: bfloat16 [12000, 768], P(('dp', 'mp')), may hold values from -6 to 6
- group_ids: int32 [12000], P(('dp', 'mp')), may hold values from 0 to 15
- intr_table: bfloat16 [16, 768], replicated, may hold values from -3 to 3
- ln1_gain: float32 [768], replicated, may hold values from 0.5 to 1.5
- ln1_bias: float32 [768], replicated, may hold values from -1 to 1
- w_qkv: bfloat16 [768, 3, 768], P(None, None, 'mp'), may hold values from -0.21875 to 0.21875
- b_qv: float32 [2, 768], P(None, 'mp'), may hold values from -1.5 to 1.5
- w_out: bfloat16 [768, 768], P('mp'), may hold values from -3.5 to 3.5
- b_out: float32 [768], replicated, may hold values from -1 to 1
- ln2_gain: float32 [768], replicated, may hold values from 0.5 to 1.5
- ln2_bias: float32 [768], replicated, may hold values from -1 to 1
- w_up: bfloat16 [768, 1536], P(None, 'mp'), may hold values from -0.21875 to 0.21875
- b_up: float32 [1536], P('mp'), may hold values from -1.5 to 1.5
- w_down: bfloat16 [1536, 768], P('mp'), may hold values from -0.21875 to 0.21875
- b_down: float32 [768], replicated, may hold values from -1 to 1
- cotangent: bfloat16 [12000, 768], P(('dp', 'mp')), may hold values from -16 to 16
Outputs:
- mixed: bfloat16 [12000, 768], P(('dp', 'mp'))
- input_grad: bfloat16 [12000, 768], P(('dp', 'mp'))
- table_grad: float32 [16, 768], replicated
- ln1_gain_grad: float32 [768], replicated
- ln1_bias_grad: float32 [768], replicated
- w_qkv_grad: float32 [768, 3, 768], P(None, None, 'mp')
- b_qv_grad: float32 [2, 768], P(None, 'mp')
- w_out_grad: float32 [768, 768], P('mp')
- b_out_grad: float32 [768], replicated
- ln2_gain_grad: float32 [768], replicated
- ln2_bias_grad: float32 [768], replicated
- w_up_grad: float32 [768, 1536], P(None, 'mp')
- b_up_grad: float32 [1536], P('mp')
- w_down_grad: float32 [1536, 768], P('mp')
- b_down_grad: float32 [768], replicated
The draws below stay inside these ranges and needn't reach their ends.
All inputs are finite; a program needn't handle non-finite values.
Results may differ from the reference program's by a relative error of at most 0.01.
Values may be sent and summed in bfloat16 or wider, within the bound.
No kernel may reach another device: no remote copies, remote signals or barrier semaphores. Data moves between devices by JAX's collectives and lax.ppermute only.
A program may use at most 128 MiB of HBM per device.

```python
import jax
import jax.numpy as jnp
from jax import lax

D = 768
HEADS = 12
FF = 1536
HEAD = 64
GROUPS = 16
SCENE_TOK = 1500
TOKENS = 12000


def draw_cotangent(key, part):
    place = jnp.arange(TOKENS, dtype=jnp.float32) / max(TOKENS - 1, 1)
    base = jnp.clip(jax.random.normal(key, (TOKENS, D), jnp.float32), -4.0, 4.0)
    scale = 1.0 + 2.0 * place
    return (base * scale[:, None]).astype(jnp.bfloat16)


def touch_ends(values, key, least, top_value):
    longest = values.shape.index(max(values.shape))
    spots = []
    for shift in (0, 1):
        where = [jax.random.randint(jax.random.fold_in(key, axis), (), 0, length) for axis, length in enumerate(values.shape)]
        where[longest] = (where[longest] + shift) % values.shape[longest]
        spots.append(tuple(where))
    return values.at[spots[0]].set(least).at[spots[1]].set(top_value)


def block_scale(key, shape, pieces, low, high):
    def one(position, blocks):
        heights = jax.random.uniform(jax.random.fold_in(jax.random.fold_in(key, 6), position), (blocks,), jnp.float32, low / len(pieces), high / len(pieces))
        return jnp.repeat(jnp.exp(heights), shape[position] // blocks).reshape((-1,) + (1,) * (len(shape) - position - 1))

    loudness = one(*pieces[0])
    for cut in pieces[1:]:
        loudness = loudness * one(*cut)
    return loudness


def gaussian(stream_key, extent, deviation, limit, pieces=(), held_as=jnp.bfloat16):
    factor_of = block_scale(stream_key, extent, pieces, -0.22, 0.18) if pieces else 1.0
    drawn = jax.random.normal(stream_key, extent, jnp.float32) * deviation * factor_of
    return jnp.minimum(jnp.maximum(drawn, -limit), limit).astype(held_as)


def setup_inputs(seed: int = 0) -> dict:
    splits = jax.random.split(jax.random.key(seed), 17)
    return {
        "block_input": gaussian(splits[0], (TOKENS, D), 1.0, 6.0, ((0, 32),)),
        "group_ids": touch_ends(jax.random.randint(splits[1], (TOKENS,), 0, GROUPS), jax.random.fold_in(splits[1], 1), 0, GROUPS - 1).astype(jnp.int32),
        "intr_table": gaussian(splits[2], (GROUPS, D), 0.5, 3.0),
        "ln1_gain": jnp.clip(1.0 + 0.1 * jax.random.normal(splits[3], (D,), jnp.float32), 0.5, 1.5),
        "ln1_bias": gaussian(splits[4], (D,), 0.2, 1.0, (), jnp.float32),
        "w_qkv": gaussian(splits[5], (D, 3, D), D ** -0.5, 0.21875, ((2, 4),)),
        "b_qv": gaussian(splits[6], (2, D), 0.3, 1.5, ((1, 4),), jnp.float32),
        "w_out": gaussian(splits[7], (D, D), (max(D // 256, 1)) ** -0.5, 3.5, ((0, 4),)),
        "b_out": gaussian(splits[8], (D,), 0.2, 1.0, (), jnp.float32),
        "ln2_gain": jnp.clip(1.0 + 0.1 * jax.random.normal(splits[9], (D,), jnp.float32), 0.5, 1.5),
        "ln2_bias": gaussian(splits[10], (D,), 0.2, 1.0, (), jnp.float32),
        "w_up": gaussian(splits[11], (D, FF), D ** -0.5, 0.21875, ((1, 4),)),
        "b_up": gaussian(splits[12], (FF,), 0.3, 1.5, ((0, 4),), jnp.float32),
        "w_down": gaussian(splits[13], (FF, D), (FF // 2) ** -0.5, 0.21875, ((0, 4),)),
        "b_down": gaussian(splits[14], (D,), 0.2, 1.0, (), jnp.float32),
        "cotangent": draw_cotangent(jax.random.fold_in(splits[16], 71), 0),
    }


@jax.custom_vjp
def low(v):
    return lax.optimization_barrier(v.astype(jnp.bfloat16)).astype(jnp.float32)

@jax.custom_vjp
def low_back(v):
    return v

def low_keep(v):
    return (low(v), None)

def low_pass(kept, grad):
    return (grad,)

def back_keep(v):
    return (v, None)

def back_low(kept, grad):
    return (low(grad),)
low.defvjp(low_keep, low_pass)
low_back.defvjp(back_keep, back_low)

def matmul(left, right):
    return jnp.dot(left, right, precision=lax.Precision.HIGHEST)

def layer_norm(rows, gain, bias):
    centre = rows - lax.optimization_barrier(jnp.mean(rows, axis=-1, keepdims=True))
    var = lax.optimization_barrier(jnp.mean(centre * centre, axis=-1, keepdims=True))
    return centre * lax.rsqrt(var + 1e-05) * gain + bias

def scene_layer(params, inputs, onehot):
    table, g1, c1, wqkv, bqv, wout, bout, g2, c2, wup, bup, wdown, bdown = params
    h0 = low(inputs + matmul(onehot, table))
    a1 = low(layer_norm(h0, g1, c1))
    qkv = jnp.einsum('td,dkh->tkh', a1, wqkv, precision=lax.Precision.HIGHEST)
    query = low_back(low(qkv[:, 0] + bqv[0]))
    keys = low_back(low(qkv[:, 1]))
    values = low_back(low(qkv[:, 2] + bqv[1]))
    length = inputs.shape[0]

    def split_heads(arr):
        return arr.reshape(length, HEADS, HEAD).transpose(1, 0, 2)
    qh, kh, vh = (split_heads(query), split_heads(keys), split_heads(values))
    scores = low_back(jnp.einsum('hqd,hkd->hqk', qh, kh, precision=lax.Precision.HIGHEST) * 0.125)
    top = lax.optimization_barrier(jnp.max(scores, axis=-1, keepdims=True))
    lse = top + jnp.log(lax.optimization_barrier(jnp.sum(jnp.exp(scores - top), axis=-1, keepdims=True)))
    probs = low(jnp.exp(scores - lse))
    heads_out = jnp.einsum('hqk,hkd->hqd', probs, vh, precision=lax.Precision.HIGHEST)
    attended = low_back(low(heads_out.transpose(1, 0, 2).reshape(length, D)))
    branch = low_back(matmul(attended, wout) + bout)
    h1 = h0 + branch
    a2 = low(layer_norm(h1, g2, c2))
    hidden = low_back(matmul(a2, wup) + bup)
    act = low(jax.nn.gelu(hidden))
    return h1 + matmul(act, wdown) + bdown

def reference(block_input, group_ids, intr_table, ln1_gain, ln1_bias, w_qkv, b_qv, w_out, b_out, ln2_gain, ln2_bias, w_up, b_up, w_down, b_down, cotangent):
    params = tuple((p.astype(jnp.float32) for p in (intr_table, ln1_gain, ln1_bias, w_qkv, b_qv, w_out, b_out, ln2_gain, ln2_bias, w_up, b_up, w_down, b_down)))
    scenes = TOKENS // SCENE_TOK
    inputs = block_input.astype(jnp.float32).reshape(scenes, SCENE_TOK, D)
    idents = group_ids.reshape(scenes, SCENE_TOK)
    grads_in = cotangent.astype(jnp.float32).reshape(scenes, SCENE_TOK, D)
    zeros = tuple((jnp.zeros_like(p) for p in params))
    levels = jnp.arange(GROUPS, dtype=jnp.int32)

    def step(total, item):
        rows, ident, grad = item
        onehot = (ident[:, None] == levels[None, :]).astype(jnp.float32)
        result, pull = jax.vjp(lambda p, h: scene_layer(p, h, onehot), params, rows)
        dparams, drows = pull(grad)
        total = tuple((a + b for a, b in zip(total, dparams)))
        return (total, (result.astype(jnp.bfloat16), drows.astype(jnp.bfloat16)))
    total, (mixed, input_grad) = lax.scan(step, zeros, (inputs, idents, grads_in))
    return (mixed.reshape(TOKENS, D), input_grad.reshape(TOKENS, D), total[0], total[1], total[2], total[3], total[4], total[5], total[6], total[7], total[8], total[9], total[10], total[11], total[12])
```

```python
import jax
import jax.numpy as jnp
from jax import lax
from jax.experimental import pallas as pl
from jax.experimental.pallas import tpu as pltpu
from jax.sharding import PartitionSpec as P

HEAD = 64
BF = jnp.bfloat16
F32 = jnp.float32
LOG2E = 1.4426950408889634
NN = (((1,), (0,)), ((), ()))
NT = (((1,), (1,)), ((), ()))
TN = (((0,), (0,)), ((), ()))
QB = 256


def mm(a, b, dims):
    return lax.dot_general(a, b, dims, preferred_element_type=F32)


def three_parts(v):
    hi = v.astype(BF)
    rest = v - hi.astype(F32)
    mid = rest.astype(BF)
    low = (rest - mid.astype(F32)).astype(BF)
    return hi, mid, low


def norm_rows(rows):
    centre = rows - jnp.mean(rows, axis=-1, keepdims=True)
    var = jnp.mean(centre * centre, axis=-1, keepdims=True)
    rstd = lax.rsqrt(var + 1e-05)
    return centre * rstd, rstd


def norm_back(grad, normed, rstd, gain):
    scaled = grad * gain
    return rstd * (
        scaled
        - jnp.mean(scaled, axis=-1, keepdims=True)
        - normed * jnp.mean(scaled * normed, axis=-1, keepdims=True)
    )


def onehot_rows(ids_row, groups):
    levels = lax.broadcasted_iota(jnp.int32, (groups, ids_row.shape[1]), 0).astype(F32)
    return (levels == ids_row).astype(F32).astype(BF)


def onehot_sum(hot, rows):
    hi = rows.astype(BF)
    low = (rows - hi.astype(F32)).astype(BF)
    return mm(hot, hi, NN) + mm(hot, low, NN)


def attend_kernel(
    rows_own, h_0, h_1, h_2, h_3, gain, bias, w_t, b_t,
    a1, qkv, probs, o32, rl, o_0, o_1, o_2, o_3, p_buf, p_sem,
):
    padded = h_0.shape[0]
    tokens = 4 * padded
    feat = w_t.shape[0] // 3
    heads = feat // HEAD
    for j, h in enumerate((h_0, h_1, h_2, h_3)):
        normed, _ = norm_rows(h[...].astype(F32))
        a1[j * padded : (j + 1) * padded, :] = (normed * gain[...] + bias[...]).astype(BF)
    qkv[...] = (mm(w_t[...], a1[...], NT) + b_t[...]).astype(BF)
    lane = lax.broadcasted_iota(jnp.int32, (16, tokens), 1)
    sub = lax.broadcasted_iota(jnp.int32, (16, tokens), 0)
    valid = jnp.zeros((16, tokens), jnp.bool_)
    for j in range(4):
        valid = valid | ((lane >= j * padded) & (lane < j * padded + rows_own))
    first = sub == 0
    mask = jnp.where(first & ~valid, -1e30, 0.0).astype(BF)
    ones = jnp.where(first, 1.0, 0.0).astype(BF)
    copies = [None, None]
    step = 0
    for h in range(heads):
        at = h * HEAD
        scaled = qkv[at : at + HEAD, :].astype(F32) * (0.125 * LOG2E)
        hi = scaled.astype(BF)
        low = (scaled - hi.astype(F32)).astype(BF)
        q_x = jnp.concatenate((hi, low, ones), axis=0)
        k_h = qkv[feat + at : feat + at + HEAD, :]
        k_x = jnp.concatenate((k_h, k_h, mask), axis=0)
        v_x = jnp.concatenate((qkv[2 * feat + at : 2 * feat + at + HEAD, :], ones), axis=0)
        for b in range(tokens // QB):
            cols = slice(b * QB, (b + 1) * QB)
            scores = mm(q_x[:, cols], k_x, TN)
            top = jnp.max(scores, axis=-1, keepdims=True)
            slot = step % 2
            if copies[slot] is not None:
                copies[slot].wait()
            p_block = jnp.exp2(scores - top).astype(BF)
            p_buf[slot] = p_block
            copies[slot] = pltpu.make_async_copy(
                p_buf.at[slot], probs.at[h, cols, :], p_sem.at[slot]
            )
            copies[slot].start()
            out = mm(v_x, p_block, NT)
            inv = 1.0 / out[HEAD : HEAD + 1, :]
            o32[at : at + HEAD, cols] = out[:HEAD, :] * inv
            rl[h : h + 1, cols] = inv
            step += 1
    for j, o in enumerate((o_0, o_1, o_2, o_3)):
        o[...] = o32[:, j * padded : (j + 1) * padded].astype(BF)
    copies[0].wait()
    copies[1].wait()


def attend(rows_own, hs, gain, bias, w_t, b_t):
    padded, width = hs[0].shape
    tokens = 4 * padded
    feat = w_t.shape[0] // 3
    heads = feat // HEAD
    vm = pl.BlockSpec(memory_space=pltpu.VMEM)
    sd = jax.ShapeDtypeStruct
    return pl.pallas_call(
        lambda *refs: attend_kernel(rows_own, *refs),
        out_shape=(
            sd((tokens, width), BF),
            sd((3 * feat, tokens), BF),
            sd((heads, tokens, tokens), BF),
            sd((feat, tokens), F32),
            sd((8, tokens), F32),
        )
        + (sd((feat, padded), BF),) * 4,
        in_specs=[vm] * 8,
        out_specs=(vm, vm, pl.BlockSpec(memory_space=pl.ANY), vm, vm, vm, vm, vm, vm),
        scratch_shapes=[pltpu.VMEM((2, QB, tokens), BF), pltpu.SemaphoreType.DMA((2,))],
        compiler_params=pltpu.CompilerParams(vmem_limit_bytes=48 * 2**20),
        cost_estimate=pl.CostEstimate(
            flops=10_000_000_000, bytes_accessed=25_000_000, transcendentals=7_000_000
        ),
        name="attend",
    )(*hs, gain, bias, w_t, b_t)


def own_kernel(
    rows_own, groups, sizes,
    o_0, o_1, o_2, o_3, h0, dy, w_0, w_1, w_2, w_3, b_out, gain, bias, b_down,
    mixed, dh1, do_0, do_1, do_2, do_3, g_0, g_1, g_2, g_3, small, db_up,
):
    hid, feat = sizes
    outs_t = (o_0, o_1, o_2, o_3)
    packs = (w_0, w_1, w_2, w_3)
    grads = (g_0, g_1, g_2, g_3)
    up, down, out = slice(0, hid), slice(hid, 2 * hid), slice(2 * hid, 2 * hid + feat)
    extra = 2 * hid + feat
    padded, width = h0.shape
    attn = b_out[...]
    for o_t, pack in zip(outs_t, packs):
        attn = attn + mm(o_t[...], pack[out, :], TN)
    h1 = h0[...].astype(F32) + attn
    normed, rstd = norm_rows(h1)
    a2 = (normed * gain[...] + bias[...]).astype(BF)
    dy_b = dy[...]
    acc = h1 + b_down[...]
    da2 = jnp.zeros((padded, width), F32)
    for j, pack in enumerate(packs):
        rows = pack[extra : extra + 16, :].astype(F32)
        b_up = (rows[0:1] + rows[1:2] + rows[2:3])[:, :hid]
        u = mm(a2, pack[up, :], NT) + b_up
        cube = u * u
        t = jnp.tanh(0.7978845608028654 * (u + 0.044715 * (u * cube)))
        half = 0.5 * (1.0 + t)
        act = (u * half).astype(BF)
        slope = half + 0.5 * u * (1.0 - t * t) * (
            0.7978845608028654 + (3 * 0.044715 * 0.7978845608028654) * cube
        )
        acc = acc + mm(act, pack[down, :], NN)
        du_f = mm(dy_b, pack[down, :], NT) * slope
        du = du_f.astype(BF)
        da2 = da2 + mm(du, pack[up, :], NN)
        grads[j][down, :] = mm(act, dy_b, TN).astype(BF)
        grads[j][up, :] = mm(du, a2, TN).astype(BF)
        db_up[j : j + 1, :] = jnp.sum(du.astype(F32), axis=0, keepdims=True)
    mixed[...] = acc[:rows_own].astype(BF)
    dyf = dy_b.astype(F32)
    total = dyf + norm_back(da2, normed, rstd, gain[...])
    dh1[...] = total
    dattn = total.astype(BF)
    for o_t, pack, d_o, g in zip(outs_t, packs, (do_0, do_1, do_2, do_3), grads):
        d_o[...] = mm(pack[out, :], dattn, NT).astype(BF)
        g[out, :] = mm(o_t[...], dattn, NN).astype(BF)
    ids_row = h0[padded - 16 :, :].astype(F32)[rows_own - padded + 16 : rows_own - padded + 17, :padded]
    hot = onehot_rows(ids_row, groups)
    small[0:groups, :] = onehot_sum(hot, total)
    small[groups : groups + 8, :] = jnp.concatenate(
        (
            jnp.sum(dattn.astype(F32), axis=0, keepdims=True),
            jnp.sum(da2 * normed, axis=0, keepdims=True),
            jnp.sum(da2, axis=0, keepdims=True),
            jnp.sum(dyf, axis=0, keepdims=True),
            jnp.zeros((4, width), F32),
        ),
        axis=0,
    )


def own_part(rows_own, groups, sizes, outs_t, h0, dy, packs, b_out, gain, bias, b_down):
    hid, feat = sizes
    padded, width = h0.shape
    vm = pl.BlockSpec(memory_space=pltpu.VMEM)
    sd = jax.ShapeDtypeStruct
    shapes = (
        (sd((rows_own, width), BF), sd((padded, width), F32))
        + (sd((feat, padded), BF),) * 4
        + (sd((2 * hid + feat, width), BF),) * 4
        + (sd((groups + 8, width), F32), sd((4, hid), F32))
    )
    return pl.pallas_call(
        lambda *refs: own_kernel(rows_own, groups, sizes, *refs),
        out_shape=shapes,
        in_specs=[vm] * 14,
        out_specs=(vm,) * len(shapes),
        compiler_params=pltpu.CompilerParams(vmem_limit_bytes=56 * 2**20),
        cost_estimate=pl.CostEstimate(
            flops=8_000_000_000, bytes_accessed=18_000_000, transcendentals=600_000
        ),
        name="own_part",
    )(*outs_t, h0, dy, *packs, b_out, gain, bias, b_down)


def attend_back_kernel(
    rows_own, groups,
    do_0, do_1, do_2, do_3, h_0, h_1, h_2, h_3, a1, qkv, probs, o32, rl, gain, w_t,
    dh_0, dh_1, dh_2, dh_3, dw, small, db,
    dqkv, d_s, p_all, p_sem,
):
    padded, width = h_0.shape
    tokens = 4 * padded
    feat = w_t.shape[0] // 3
    heads = feat // HEAD

    def fetch(h):
        return pltpu.make_async_copy(probs.at[h], p_all.at[h % 2], p_sem.at[h % 2])

    fetch(0).start()
    d_out = jnp.concatenate((do_0[...], do_1[...], do_2[...], do_3[...]), axis=1)
    sub = lax.broadcasted_iota(jnp.int32, (16, tokens), 0)
    ones = jnp.where(sub < 3, 1.0, 0.0).astype(BF)
    zero = jnp.zeros((13, tokens), F32)
    for h in range(heads):
        at = h * HEAD
        if h + 1 < heads:
            fetch(h + 1).start()
        do_s = (d_out[at : at + HEAD, :].astype(F32) * rl[h : h + 1, :]).astype(BF)
        delta = -jnp.sum(do_s.astype(F32) * o32[at : at + HEAD, :], axis=0, keepdims=True)
        d_hi = delta.astype(BF).astype(F32)
        d_mid = (delta - d_hi).astype(BF).astype(F32)
        d_low = delta - d_hi - d_mid
        tail = jnp.concatenate((d_hi, d_mid, d_low, zero), axis=0).astype(BF)
        do_x = jnp.concatenate((do_s, tail), axis=0)
        v_x = jnp.concatenate((qkv[2 * feat + at : 2 * feat + at + HEAD, :], ones), axis=0)
        q_h = qkv[at : at + HEAD, :]
        k_h = qkv[feat + at : feat + at + HEAD, :]
        fetch(h).wait()
        for b in range(tokens // QB):
            cols = slice(b * QB, (b + 1) * QB)
            dp = mm(do_x[:, cols], v_x, TN)
            ds = (p_all[h % 2, cols, :].astype(F32) * dp).astype(BF)
            d_s[cols, :] = ds
            dqkv[at : at + HEAD, cols] = (0.125 * mm(k_h, ds, NT)).astype(BF)
        dqkv[feat + at : feat + at + HEAD, :] = (0.125 * mm(q_h, d_s[...], NN)).astype(BF)
        dqkv[2 * feat + at : 2 * feat + at + HEAD, :] = mm(do_s, p_all[h % 2], NN).astype(BF)
    dw[...] = mm(dqkv[...], a1[...], NN).astype(BF)
    db[...] = mm(jnp.ones((8, tokens), BF), dqkv[...], NT)
    g = gain[...]
    table = jnp.zeros((groups, width), F32)
    dgain = jnp.zeros((1, width), F32)
    dbias = jnp.zeros((1, width), F32)
    for j, (h, dh) in enumerate(zip((h_0, h_1, h_2, h_3), (dh_0, dh_1, dh_2, dh_3))):
        rows = slice(j * padded, (j + 1) * padded)
        da1 = mm(dqkv[:, rows], w_t[...], TN)
        normed, rstd = norm_rows(h[...].astype(F32))
        back = norm_back(da1, normed, rstd, g)
        dh[...] = back.astype(BF)
        dgain = dgain + jnp.sum(da1 * normed, axis=0, keepdims=True)
        dbias = dbias + jnp.sum(da1, axis=0, keepdims=True)
        ids_row = h[padded - 16 :, :].astype(F32)[rows_own - padded + 16 : rows_own - padded + 17, :padded]
        table = table + onehot_sum(onehot_rows(ids_row, groups), back)
    small[0:groups, :] = table
    small[groups : groups + 8, :] = jnp.concatenate(
        (dgain, dbias, jnp.zeros((6, width), F32)), axis=0
    )


def attend_back(rows_own, groups, dos, hs, a1, qkv, probs, o32, rl, gain, w_t):
    padded, width = hs[0].shape
    tokens = 4 * padded
    feat = w_t.shape[0] // 3
    vm = pl.BlockSpec(memory_space=pltpu.VMEM)
    sd = jax.ShapeDtypeStruct
    shapes = (sd((padded, width), BF),) * 4 + (
        sd((3 * feat, width), BF),
        sd((groups + 8, width), F32),
        sd((8, 3 * feat), F32),
    )
    return pl.pallas_call(
        lambda *refs: attend_back_kernel(rows_own, groups, *refs),
        out_shape=shapes,
        in_specs=[vm] * 10 + [pl.BlockSpec(memory_space=pl.ANY)] + [vm] * 4,
        out_specs=(vm,) * len(shapes),
        scratch_shapes=[
            pltpu.VMEM((3 * feat, tokens), BF),
            pltpu.VMEM((tokens, tokens), BF),
            pltpu.VMEM((2, tokens, tokens), BF),
            pltpu.SemaphoreType.DMA((2,)),
        ],
        compiler_params=pltpu.CompilerParams(vmem_limit_bytes=56 * 2**20),
        cost_estimate=pl.CostEstimate(
            flops=20_000_000_000, bytes_accessed=30_000_000, transcendentals=10_000
        ),
        name="attend_back",
    )(*dos, *hs, a1, qkv, probs, o32, rl, gain, w_t)


def swap(arr, axis, bit):
    size = lax.axis_size(axis)
    return lax.ppermute(arr, axis, [(i, i ^ bit) for i in range(size)])


def add(a, b):
    return (a.astype(F32) + b.astype(F32)).astype(a.dtype)


def reduce_dp(arr):
    size = lax.axis_size("dp")
    me = lax.axis_index("dp")
    bits = []
    bit = 1
    while bit < size:
        bits.append(bit)
        bit *= 2
    for bit in bits:
        half = arr.shape[0] // 2
        side = (me // bit) % 2
        sent = lax.dynamic_slice_in_dim(arr, (1 - side) * half, half, 0)
        kept = lax.dynamic_slice_in_dim(arr, side * half, half, 0)
        arr = add(kept, swap(sent, "dp", bit))
    for bit in reversed(bits):
        other = swap(arr, "dp", bit)
        side = (me // bit) % 2
        arr = jnp.where(
            side == 0,
            jnp.concatenate((arr, other), axis=0),
            jnp.concatenate((other, arr), axis=0),
        )
    return arr


def reduce_small(arr):
    bit = 1
    while bit < lax.axis_size("mp"):
        arr = arr + swap(arr, "mp", bit)
        bit *= 2
    bit = 1
    while bit < lax.axis_size("dp"):
        arr = arr + swap(arr, "dp", bit)
        bit *= 2
    return arr


def per_device(
    block_input, group_ids, intr_table, ln1_gain, ln1_bias, w_qkv, b_qv, w_out, b_out,
    ln2_gain, ln2_bias, w_up, b_up, w_down, b_down, cotangent,
):
    rows_own, width = block_input.shape
    padded = -(-rows_own // 128) * 128
    groups = intr_table.shape[0]
    feat, hid = w_out.shape[0], w_down.shape[0]
    me = lax.axis_index("mp")
    onehot = (group_ids[:, None] == jnp.arange(groups, dtype=jnp.int32)[None, :]).astype(BF)
    h0_rows = (
        block_input.astype(F32) + jnp.dot(onehot, intr_table, preferred_element_type=F32)
    ).astype(BF)
    ids_row = jnp.pad(group_ids.astype(BF)[None, :], ((0, 0), (0, width - rows_own)))
    h0 = jnp.concatenate(
        (h0_rows, ids_row, jnp.zeros((padded - rows_own - 1, width), BF)), axis=0
    )
    h_x = swap(h0, "mp", 2)
    h_c = swap(h0, "mp", 1)
    h_xc = swap(h_x, "mp", 1)
    hs = (h0, h_c, h_x, h_xc)

    b_rows = jnp.stack(three_parts(b_up), axis=0)
    pack = jnp.concatenate(
        (w_up.T, w_down, w_out, jnp.pad(b_rows, ((0, 13), (0, width - hid)))), axis=0
    )
    pack, _ = lax.optimization_barrier((pack, h_x))
    w_x = swap(pack, "mp", 2)
    w_c = swap(pack, "mp", 1)
    w_xc = swap(w_x, "mp", 1)
    packs = (pack, w_c, w_x, w_xc)
    dy = jnp.pad(cotangent, ((0, padded - rows_own), (0, 0)))

    w_t = w_qkv.transpose(1, 2, 0).reshape(3 * feat, width)
    b_t = jnp.concatenate((b_qv[0], jnp.zeros((feat,), F32), b_qv[1]))[:, None]
    row = lambda v: v.reshape(1, -1)
    a1, qkv, probs, o32, rl, *o_ts = attend(rows_own, hs, row(ln1_gain), row(ln1_bias), w_t, b_t)
    o_ts = [o_ts[0]] + [swap(o_ts[j], "mp", j) for j in (1, 2, 3)]
    mixed, dh1, *rest = own_part(
        rows_own, groups, (hid, feat), o_ts, h0, dy, packs,
        row(b_out), row(ln2_gain), row(ln2_bias), row(b_down),
    )
    do_ts, grads, (small_own, db_up) = rest[:4], rest[4:8], rest[8:]
    do_ts = [do_ts[0]] + [swap(do_ts[j], "mp", j) for j in (1, 2, 3)]
    sum_0 = add(grads[0], swap(grads[1], "mp", 1))
    sum_2 = add(grads[2], swap(grads[3], "mp", 1))
    g_mlp = add(sum_0, swap(sum_2, "mp", 2))
    g_mlp = reduce_dp(g_mlp)

    *dhs, dw, small_att, db = attend_back(
        rows_own, groups, do_ts, hs, a1, qkv, probs, o32, rl, row(ln1_gain), w_t
    )
    part_0 = add(dhs[0], swap(dhs[1], "mp", 1))
    part_2 = add(dhs[2], swap(dhs[3], "mp", 1))
    dh0 = dh1 + part_0.astype(F32) + swap(part_2, "mp", 2).astype(F32)
    input_grad = dh0[:rows_own].astype(BF)

    g_qkv = reduce_dp(dw)

    up_rows = jnp.zeros((4, hid), F32)
    for j in range(4):
        up_rows = lax.dynamic_update_slice(up_rows, db_up[j : j + 1], (me ^ j, 0))
    qv_rows = jnp.zeros((2, 4, feat), F32)
    qv_own = jnp.stack((db[0, :feat], db[0, 2 * feat :]), axis=0)[:, None, :]
    qv_rows = lax.dynamic_update_slice(qv_rows, qv_own, (0, me, 0))
    small = jnp.concatenate(
        (
            small_own[:groups] + small_att[:groups],
            small_own[groups : groups + 4],
            small_att[groups : groups + 2],
            up_rows.reshape(-1, width),
            qv_rows.reshape(-1, width),
        ),
        axis=0,
    )
    small = reduce_small(small)
    at = groups
    up_at = at + 6
    qv_at = up_at + 4 * hid // width
    b_up_grad = lax.dynamic_slice(small[up_at:qv_at].reshape(4, hid), (me, 0), (1, hid))[0]
    b_qv_grad = lax.dynamic_slice(
        small[qv_at:].reshape(2, 4, feat), (0, me, 0), (2, 1, feat)
    ).reshape(2, feat)
    w_qkv_grad = g_qkv.astype(F32).reshape(3, feat, width).transpose(2, 0, 1)
    return (
        mixed,
        input_grad,
        small[:groups],
        small[at + 4],
        small[at + 5],
        w_qkv_grad,
        b_qv_grad,
        g_mlp[2 * hid :].astype(F32),
        small[at],
        small[at + 1],
        small[at + 2],
        g_mlp[:hid].astype(F32).T,
        b_up_grad,
        g_mlp[hid : 2 * hid].astype(F32),
        small[at + 3],
    )


def solution(mesh):
    rows = P(("dp", "mp"), None)
    return jax.shard_map(
        per_device,
        mesh=mesh,
        in_specs=(
            rows, P(("dp", "mp")), P(), P(), P(), P(None, None, "mp"), P(None, "mp"), P("mp", None),
            P(), P(), P(), P(None, "mp"), P("mp"), P("mp", None), P(), rows,
        ),
        out_specs=(
            rows, rows, P(), P(), P(), P(None, None, "mp"), P(None, "mp"), P("mp", None),
            P(), P(), P(), P(None, "mp"), P("mp"), P("mp", None), P(),
        ),
        check_vma=False,
    )
```

```python
import jax
import jax.numpy as jnp
from jax import lax
from jax.experimental import pallas as pl
from jax.experimental.pallas import tpu as pltpu
from jax.sharding import PartitionSpec as P

HEAD = 64
BF = jnp.bfloat16
F32 = jnp.float32
LOG2E = 1.4426950408889634
NN = (((1,), (0,)), ((), ()))
NT = (((1,), (1,)), ((), ()))
TN = (((0,), (0,)), ((), ()))
QB = 256
VM = pl.BlockSpec(memory_space=pltpu.VMEM)
ANY = pl.BlockSpec(memory_space=pl.ANY)
SM = pl.BlockSpec(memory_space=pltpu.SMEM)
SD = jax.ShapeDtypeStruct
SAFE = 3000.0


def mm(a, b, dims):
    return lax.dot_general(a, b, dims, preferred_element_type=F32)


def three_parts(v):
    hi = v.astype(BF)
    rest = v - hi.astype(F32)
    mid = rest.astype(BF)
    low = (rest - mid.astype(F32)).astype(BF)
    return hi, mid, low


def norm_rows(rows):
    centre = rows - jnp.mean(rows, axis=-1, keepdims=True)
    var = jnp.mean(centre * centre, axis=-1, keepdims=True)
    rstd = lax.rsqrt(var + 1e-05)
    return centre * rstd, rstd


def norm_back(grad, normed, rstd, gain):
    scaled = grad * gain
    return rstd * (
        scaled
        - jnp.mean(scaled, axis=-1, keepdims=True)
        - normed * jnp.mean(scaled * normed, axis=-1, keepdims=True)
    )


def onehot_rows(ids_row, groups):
    levels = lax.broadcasted_iota(jnp.int32, (groups, ids_row.shape[1]), 0).astype(F32)
    return (levels == ids_row).astype(F32).astype(BF)


def onehot_sum(hot, rows):
    hi = rows.astype(BF)
    low = (rows - hi.astype(F32)).astype(BF)
    return mm(hot, hi, NN) + mm(hot, low, NN)


def ids_of(h, rows_own, padded):
    tail = h[padded - 16 :, :].astype(F32)
    at = rows_own - padded + 16
    return tail[at : at + 1, :padded]


def call(kernel, name, ins, outs, scratch, args, limit, flops, nbytes):
    return pl.pallas_call(
        kernel,
        out_shape=tuple(s for s, _ in outs),
        in_specs=ins,
        out_specs=tuple(o for _, o in outs),
        scratch_shapes=scratch,
        compiler_params=pltpu.CompilerParams(vmem_limit_bytes=limit * 2**20),
        cost_estimate=pl.CostEstimate(flops=flops, bytes_accessed=nbytes, transcendentals=0),
        name=name,
    )(*args)


def attend_kernel(
    rows_own, h_0, h_1, h_2, h_3, gain, bias, w_t, b_t,
    a1, qkv, probs, o32, rl, o_0, o_1, o_2, o_3, a1_v, qkv_v, p_buf, p_sem, sem,
):
    padded = h_0.shape[0]
    tokens = 4 * padded
    heads = w_t.shape[0] // (3 * HEAD)
    for j, h in enumerate((h_0, h_1, h_2, h_3)):
        normed, _ = norm_rows(h[...].astype(F32))
        a1_v[j * padded : (j + 1) * padded, :] = (normed * gain[...] + bias[...]).astype(BF)
    out_a1 = pltpu.make_async_copy(a1_v, a1, sem.at[0])
    out_a1.start()
    qkv_v[...] = (mm(w_t[...], a1_v[...], NT) + b_t[...]).astype(BF)
    out_qkv = pltpu.make_async_copy(qkv_v, qkv, sem.at[1])
    out_qkv.start()
    lane = lax.broadcasted_iota(jnp.int32, (16, tokens), 1)
    sub = lax.broadcasted_iota(jnp.int32, (16, tokens), 0)
    valid = jnp.zeros((16, tokens), jnp.bool_)
    for j in range(4):
        valid = valid | ((lane >= j * padded) & (lane < j * padded + rows_own))
    first = sub == 0
    mask = jnp.where(first & ~valid, -1e30, 0.0).astype(BF)
    ones = jnp.where(first, 1.0, 0.0).astype(BF)
    half = tokens // 2
    slots = p_buf.shape[0]
    copies = [None] * slots
    step = 0
    for h in range(heads):
        at = 3 * h * HEAD
        scaled = qkv_v[at : at + HEAD, :].astype(F32) * (0.125 * LOG2E)
        hi = scaled.astype(BF)
        low = (scaled - hi.astype(F32)).astype(BF)
        q_x = jnp.concatenate((hi, low, ones), axis=0)
        k_h = qkv_v[at + HEAD : at + 2 * HEAD, :]
        k_f = k_h.astype(F32)
        k_x = jnp.concatenate((k_h, k_h, mask), axis=0)
        v_x = jnp.concatenate((qkv_v[at + 2 * HEAD : at + 3 * HEAD, :], ones), axis=0)
        bound = jnp.max(jnp.sum(scaled * scaled, axis=0, keepdims=True)) * jnp.max(
            jnp.sum(k_f * k_f, axis=0, keepdims=True)
        )
        small = bound < SAFE
        for part in range(2):
            slot = step % slots
            if copies[slot] is not None:
                copies[slot].wait()

            def block(b, exact, slot=slot, h=h, part=part, q_x=q_x, k_x=k_x, v_x=v_x):
                cols = slice(part * half + b * QB, part * half + (b + 1) * QB)
                scores = mm(q_x[:, cols], k_x, TN)
                if exact:
                    scores = scores - jnp.max(scores, axis=-1, keepdims=True)
                p_block = jnp.exp2(scores).astype(BF)
                p_buf[slot, b * QB : (b + 1) * QB, :] = p_block
                out = mm(v_x, p_block, NT)
                inv = 1.0 / out[HEAD : HEAD + 1, :]
                o32[h * HEAD : (h + 1) * HEAD, cols] = out[:HEAD, :] * inv
                rl[h : h + 1, cols] = inv

            @pl.when(small)
            def _():
                for b in range(half // QB):
                    block(b, False)

            @pl.when(jnp.logical_not(small))
            def _():
                for b in range(half // QB):
                    block(b, True)

            copies[slot] = pltpu.make_async_copy(
                p_buf.at[slot], probs.at[h, part * half : (part + 1) * half, :], p_sem.at[slot]
            )
            copies[slot].start()
            step += 1
    for j, o in enumerate((o_0, o_1, o_2, o_3)):
        o[...] = o32[:, j * padded : (j + 1) * padded].astype(BF)
    out_a1.wait()
    out_qkv.wait()
    for copy in copies:
        if copy is not None:
            copy.wait()


def attend(rows_own, hs, gain, bias, w_t, b_t):
    padded, width = hs[0].shape
    tokens = 4 * padded
    rows = w_t.shape[0]
    feat = rows // 3
    heads = feat // HEAD
    return call(
        lambda *refs: attend_kernel(rows_own, *refs),
        "attend",
        [VM] * 8,
        [
            (SD((tokens, width), BF), ANY),
            (SD((rows, tokens), BF), ANY),
            (SD((heads, tokens, tokens), BF), ANY),
            (SD((feat, tokens), F32), VM),
            (SD((8, tokens), F32), VM),
        ]
        + [(SD((feat, padded), BF), VM)] * 4,
        [
            pltpu.VMEM((tokens, width), BF),
            pltpu.VMEM((rows, tokens), BF),
            pltpu.VMEM((3, tokens // 2, tokens), BF),
            pltpu.SemaphoreType.DMA((3,)),
            pltpu.SemaphoreType.DMA((2,)),
        ],
        (*hs, gain, bias, w_t, b_t),
        40, 12_000_000_000, 25_000_000,
    )


def own_a_kernel(
    rows_own, groups, sizes, cuts,
    side, o_0, o_1, o_2, o_3, h0, dy, w_own, w_c, x_00, x_01, x_10, x_11,
    xc_00, xc_01, xc_10, xc_11, b_out, gain, bias, b_down,
    mixed, dh1, do_0, do_1, do_2, do_3, act_h, du_h, a2_h, dattn_h, small, db_up,
    w_v, act_v, du_v, a2_v, w_sem, sem,
):
    hid, feat = sizes
    cut = cuts[0]
    outs_t = (o_0, o_1, o_2, o_3)
    up_at = feat + 32
    out, up = slice(0, feat), slice(up_at, up_at + hid)
    down = slice(up_at + hid, up_at + 2 * hid)
    padded, width = h0.shape
    me = side[0]
    loads = [[], []]
    for c in range(2):
        base, size = (0, cuts[0]) if c == 0 else (cuts[0], cuts[1])
        n = size // 2
        near = pl.multiple_of(base + me * n, 16)
        far = pl.multiple_of(base + (1 - me) * n, 16)
        for src, j, at, num in (
            (w_own.at[base : base + size], 0, base, size),
            (w_c.at[base : base + size], 1, base, size),
            ((x_00, x_10)[c], 2, near, n),
            ((x_01, x_11)[c], 2, far, n),
            ((xc_00, xc_10)[c], 3, near, n),
            ((xc_01, xc_11)[c], 3, far, n),
        ):
            copy = pltpu.make_async_copy(
                src, w_v.at[j, pl.ds(at, num), :], w_sem.at[c * 6 + len(loads[c])]
            )
            copy.start()
            loads[c].append(copy)
    for copy in loads[0]:
        copy.wait()
    attn = b_out[...]
    for j, o_t in enumerate(outs_t):
        attn = attn + mm(o_t[...], w_v[j, out, :], TN)
    h1 = h0[...].astype(F32) + attn
    normed, rstd = norm_rows(h1)
    a2 = (normed * gain[...] + bias[...]).astype(BF)
    a2_v[...] = a2
    saves = [pltpu.make_async_copy(a2_v, a2_h, sem.at[0])]
    saves[0].start()
    dy_b = dy[...]
    acc = h1 + b_down[...]
    da2 = jnp.zeros((padded, width), F32)
    for copy in loads[1]:
        copy.wait()
    for j in range(4):
        rows = w_v[j, feat : feat + 16, :].astype(F32)
        b_up = (rows[0:1] + rows[1:2] + rows[2:3])[:, :hid]
        u = mm(a2, w_v[j, up, :], NT) + b_up
        cube = u * u
        t = jnp.tanh(0.7978845608028654 * (u + 0.044715 * (u * cube)))
        half = 0.5 * (1.0 + t)
        act = (u * half).astype(BF)
        slope = half + 0.5 * u * (1.0 - t * t) * (
            0.7978845608028654 + (3 * 0.044715 * 0.7978845608028654) * cube
        )
        acc = acc + mm(act, w_v[j, down, :], NN)
        du = (mm(dy_b, w_v[j, down, :], NT) * slope).astype(BF)
        da2 = da2 + mm(du, w_v[j, up, :], NN)
        act_v[j] = act
        du_v[j] = du
        for k, (src, dst) in enumerate(((act_v, act_h), (du_v, du_h))):
            copy = pltpu.make_async_copy(src.at[j], dst.at[j], sem.at[1 + 2 * j + k])
            copy.start()
            saves.append(copy)
        db_up[j : j + 1, :] = jnp.sum(du.astype(F32), axis=0, keepdims=True)
    mixed[...] = acc[:rows_own].astype(BF)
    dyf = dy_b.astype(F32)
    total = dyf + norm_back(da2, normed, rstd, gain[...])
    dh1[...] = total
    dattn = total.astype(BF)
    dattn_h[...] = dattn
    for j, d_o in enumerate((do_0, do_1, do_2, do_3)):
        d_o[...] = mm(w_v[j, out, :], dattn, NT).astype(BF)
    hot = onehot_rows(ids_of(h0, rows_own, padded), groups)
    small[0:groups, :] = onehot_sum(hot, total)
    small[groups : groups + 8, :] = jnp.concatenate(
        (
            jnp.sum(dattn.astype(F32), axis=0, keepdims=True),
            jnp.sum(da2 * normed, axis=0, keepdims=True),
            jnp.sum(da2, axis=0, keepdims=True),
            jnp.sum(dyf, axis=0, keepdims=True),
            jnp.zeros((4, width), F32),
        ),
        axis=0,
    )
    for copy in saves:
        copy.wait()


def own_a(rows_own, groups, sizes, cuts, side, o_ts, h0, dy, weights, b_out, gain, bias, b_down):
    hid, feat = sizes
    padded, width = h0.shape
    return call(
        lambda *refs: own_a_kernel(rows_own, groups, sizes, cuts, *refs),
        "own_a",
        [SM] + [VM] * 6 + [ANY] * 10 + [VM] * 4,
        [(SD((rows_own, width), BF), VM), (SD((padded, width), F32), VM)]
        + [(SD((feat, padded), BF), VM)] * 4
        + [(SD((4, padded, hid), BF), ANY)] * 2
        + [
            (SD((padded, width), BF), ANY),
            (SD((padded, width), BF), VM),
            (SD((groups + 8, width), F32), VM),
            (SD((4, hid), F32), VM),
        ],
        [
            pltpu.VMEM((4, sum(cuts), width), BF),
            pltpu.VMEM((4, padded, hid), BF),
            pltpu.VMEM((4, padded, hid), BF),
            pltpu.VMEM((padded, width), BF),
            pltpu.SemaphoreType.DMA((12,)),
            pltpu.SemaphoreType.DMA((9,)),
        ],
        (side, *o_ts, h0, dy, *weights, b_out, gain, bias, b_down),
        40, 6_000_000_000, 16_000_000,
    )


def own_b_kernel(
    cut, act_h, du_h, a2, dattn, dy, o_0, o_1, o_2, o_3, keep_a, send_a, keep_b, send_b,
    act_v, du_v, ka_v, sa_v, kb_v, sb_v, in_sem, sem,
):
    hid = act_h.shape[2]
    loads = []
    for j in range(4):
        pair = []
        for k, (src, dst) in enumerate(((act_h, act_v), (du_h, du_v))):
            copy = pltpu.make_async_copy(src.at[j], dst.at[j], in_sem.at[2 * j + k])
            copy.start()
            pair.append(copy)
        loads.append(pair)
    saves = []
    for j, o_t in enumerate((o_0, o_1, o_2, o_3)):
        a_v, a_h = ((ka_v, keep_a), (sa_v, send_a))[j % 2]
        b_v, b_h = ((kb_v, keep_b), (sb_v, send_b))[j % 2]
        d_out = mm(o_t[...], dattn[...], NN).astype(BF)
        a_v[j // 2, hid:, :] = d_out[:cut]
        b_v[j // 2, hid:, :] = d_out[cut:]
        for copy in loads[j]:
            copy.wait()
        a_v[j // 2, :hid, :] = mm(du_v[j], a2[...], TN).astype(BF)
        b_v[j // 2, :hid, :] = mm(act_v[j], dy[...], TN).astype(BF)
        for k, (src, dst) in enumerate(((a_v, a_h), (b_v, b_h))):
            copy = pltpu.make_async_copy(src.at[j // 2], dst.at[j // 2], sem.at[2 * j + k])
            copy.start()
            saves.append(copy)
    for copy in saves:
        copy.wait()


def own_b(cut, act, du, a2, dattn, dy, o_ts):
    _, padded, hid = act.shape
    width = a2.shape[1]
    feat = o_ts[0].shape[0]
    a, b = (2, hid + cut, width), (2, hid + feat - cut, width)
    return call(
        lambda *refs: own_b_kernel(cut, *refs),
        "own_b",
        [ANY] * 2 + [VM] * 7,
        [(SD(s, BF), ANY) for s in (a, a, b, b)],
        [pltpu.VMEM((4, padded, hid), BF)] * 2
        + [pltpu.VMEM(s, BF) for s in (a, a, b, b)]
        + [pltpu.SemaphoreType.DMA((8,)), pltpu.SemaphoreType.DMA((8,))],
        (act, du, a2, dattn, dy, *o_ts),
        24, 3_000_000_000, 10_000_000,
    )


def back_heads(heads, first, d_out, qkv, probs, o32, rl, dqkv, d_s, p_all, p_sem, q_v, q_sem):
    tokens = o32.shape[1]
    half = tokens // 2

    def fetch(i):
        h, part = divmod(i, 2)
        return pltpu.make_async_copy(
            probs.at[first + h, part * half : (part + 1) * half, :],
            p_all.at[h % 2, part * half : (part + 1) * half, :],
            p_sem.at[i % 4],
        )

    rows = heads * 3 * HEAD
    at0 = first * 3 * HEAD
    get_q = pltpu.make_async_copy(qkv.at[at0 : at0 + rows, :], q_v, q_sem)
    get_q.start()
    for i in range(2):
        fetch(i).start()
    sub = lax.broadcasted_iota(jnp.int32, (16, tokens), 0)
    ones = jnp.where(sub < 3, 1.0, 0.0).astype(BF)
    zero = jnp.zeros((13, tokens), F32)
    get_q.wait()
    for h in range(heads):
        at = h * 3 * HEAD
        src = (first + h) * HEAD
        do_s = (d_out[src : src + HEAD, :].astype(F32) * rl[first + h : first + h + 1, :]).astype(BF)
        delta = -jnp.sum(do_s.astype(F32) * o32[src : src + HEAD, :], axis=0, keepdims=True)
        d_hi = delta.astype(BF).astype(F32)
        d_mid = (delta - d_hi).astype(BF).astype(F32)
        d_low = delta - d_hi - d_mid
        tail = jnp.concatenate((d_hi, d_mid, d_low, zero), axis=0).astype(BF)
        do_x = jnp.concatenate((do_s, tail), axis=0)
        q_h = q_v[at : at + HEAD, :]
        k_h = q_v[at + HEAD : at + 2 * HEAD, :]
        v_x = jnp.concatenate((q_v[at + 2 * HEAD : at + 3 * HEAD, :], ones), axis=0)
        if h + 1 < heads:
            fetch(2 * h + 2).start()
            fetch(2 * h + 3).start()
        for b in range(tokens // QB):
            cols = slice(b * QB, (b + 1) * QB)
            if b * QB in (0, half):
                fetch(2 * h + b * QB // half).wait()
            dp = mm(do_x[:, cols], v_x, TN)
            ds = (p_all[h % 2, cols, :].astype(F32) * dp).astype(BF)
            d_s[cols, :] = ds
            dqkv[at : at + HEAD, cols] = (0.125 * mm(k_h, ds, NT)).astype(BF)
        dqkv[at + HEAD : at + 2 * HEAD, :] = (0.125 * mm(q_h, d_s[...], NN)).astype(BF)
        dqkv[at + 2 * HEAD : at + 3 * HEAD, :] = mm(do_s, p_all[h % 2], NN).astype(BF)


def back_1_kernel(
    heads, do_0, do_1, do_2, do_3, a1, qkv, probs, o32, rl, dqkv, dw,
    d_s, p_all, p_sem, q_v, a1_v, sem,
):
    get_a1 = pltpu.make_async_copy(a1, a1_v, sem.at[0])
    d_out = jnp.concatenate((do_0[...], do_1[...], do_2[...], do_3[...]), axis=1)
    back_heads(heads, 0, d_out, qkv, probs, o32, rl, dqkv, d_s, p_all, p_sem, q_v, sem.at[1])
    get_a1.start()
    get_a1.wait()
    dw[...] = mm(dqkv[...], a1_v[...], NN).astype(BF)


def back_1(heads, dos, a1, qkv, probs, o32, rl):
    tokens, width = a1.shape
    rows = heads * 3 * HEAD
    return call(
        lambda *refs: back_1_kernel(heads, *refs),
        "back_1",
        [VM] * 4 + [ANY] * 3 + [VM] * 2,
        [(SD((rows, tokens), BF), VM), (SD((rows, width), BF), VM)],
        [
            pltpu.VMEM((tokens, tokens), BF),
            pltpu.VMEM((2, tokens, tokens), BF),
            pltpu.SemaphoreType.DMA((4,)),
            pltpu.VMEM((rows, tokens), BF),
            pltpu.VMEM((tokens, width), BF),
            pltpu.SemaphoreType.DMA((2,)),
        ],
        (*dos, a1, qkv, probs, o32, rl),
        40, 14_000_000_000, 18_000_000,
    )


def back_2_kernel(
    heads, rows_own, groups,
    do_0, do_1, do_2, do_3, h_0, h_1, h_2, h_3, a1, qkv, probs, o32, rl, gain, w_t, dqkv_1,
    keep, send, dw, small, db,
    dqkv, d_s, p_all, p_sem, q_v, a1_v, h_v, w_v, d1_v, sem,
):
    padded, width = h_0.shape
    done = dqkv_1.shape[0] // (3 * HEAD)
    gets = [
        pltpu.make_async_copy(src, dst, sem.at[2 + i])
        for i, (src, dst) in enumerate(
            [(a1, a1_v), (dqkv_1, d1_v), (w_t, w_v)]
            + [(h, h_v.at[j]) for j, h in enumerate((h_0, h_1, h_2, h_3))]
        )
    ]
    d_out = jnp.concatenate((do_0[...], do_1[...], do_2[...], do_3[...]), axis=1)
    back_heads(
        heads - done, done, d_out, qkv, probs, o32, rl, dqkv, d_s, p_all, p_sem, q_v, sem.at[1]
    )
    for get in gets:
        get.start()
    for get in gets:
        get.wait()
    dw[...] = mm(dqkv[...], a1_v[...], NN).astype(BF)
    ones = jnp.ones((8, dqkv.shape[1]), BF)
    db[:, : d1_v.shape[0]] = mm(ones, d1_v[...], NT)
    db[:, d1_v.shape[0] :] = mm(ones, dqkv[...], NT)
    cut = d1_v.shape[0]
    g = gain[...]
    table = jnp.zeros((groups, width), F32)
    dgain = jnp.zeros((1, width), F32)
    dbias = jnp.zeros((1, width), F32)
    for j in (3, 1, 2, 0):
        rows = slice(j * padded, (j + 1) * padded)
        da1 = mm(d1_v[:, rows], w_v[:cut, :], TN) + mm(dqkv[:, rows], w_v[cut:, :], TN)
        normed, rstd = norm_rows(h_v[j].astype(F32))
        back = norm_back(da1, normed, rstd, g)
        (keep, send)[j % 2][j // 2] = back.astype(BF)
        dgain = dgain + jnp.sum(da1 * normed, axis=0, keepdims=True)
        dbias = dbias + jnp.sum(da1, axis=0, keepdims=True)
        hot = onehot_rows(ids_of(h_v.at[j], rows_own, padded), groups)
        table = table + onehot_sum(hot, back)
    small[0:groups, :] = table
    small[groups : groups + 8, :] = jnp.concatenate(
        (dgain, dbias, jnp.zeros((6, width), F32)), axis=0
    )


def back_2(rows_own, groups, dos, hs, a1, qkv, probs, o32, rl, gain, w_t, dqkv_1):
    tokens, width = a1.shape
    padded = hs[0].shape[0]
    heads = w_t.shape[0] // (3 * HEAD)
    rows = w_t.shape[0] - dqkv_1.shape[0]
    return call(
        lambda *refs: back_2_kernel(heads, rows_own, groups, *refs),
        "back_2",
        [VM] * 4 + [ANY] * 7 + [VM] * 3 + [ANY] * 2,
        [
            (SD((2, padded, width), BF), VM),
            (SD((2, padded, width), BF), VM),
            (SD((rows, width), BF), VM),
            (SD((groups + 8, width), F32), VM),
            (SD((8, w_t.shape[0]), F32), VM),
        ],
        [
            pltpu.VMEM((rows, tokens), BF),
            pltpu.VMEM((tokens, tokens), BF),
            pltpu.VMEM((2, tokens, tokens), BF),
            pltpu.SemaphoreType.DMA((4,)),
            pltpu.VMEM((rows, tokens), BF),
            pltpu.VMEM((tokens, width), BF),
            pltpu.VMEM((4, padded, width), BF),
            pltpu.VMEM(w_t.shape, BF),
            pltpu.VMEM(dqkv_1.shape, BF),
            pltpu.SemaphoreType.DMA((9,)),
        ],
        (*dos, *hs, a1, qkv, probs, o32, rl, gain, w_t, dqkv_1),
        44, 9_000_000_000, 16_000_000,
    )


def swap(arr, axis, bit):
    size = lax.axis_size(axis)
    return lax.ppermute(arr, axis, [(i, i ^ bit) for i in range(size)])


def add(a, b):
    return (a.astype(F32) + b.astype(F32)).astype(a.dtype)


def after(value, *others):
    return lax.optimization_barrier((value, others))[0]


def side_of(bit):
    return (lax.axis_index("dp") // bit) % 2


def dp_bits():
    bits, bit = [], 1
    while bit < lax.axis_size("dp"):
        bits.append(bit)
        bit *= 2
    return bits


def halve(arr, bit):
    axis = arr.ndim - 3
    half = arr.shape[axis] // 2
    side = side_of(bit)
    kept = lax.dynamic_slice_in_dim(arr, side * half, half, axis)
    sent = lax.dynamic_slice_in_dim(arr, (1 - side) * half, half, axis)
    return kept, sent


def scatter(arr, bits):
    for bit in bits:
        kept, sent = halve(arr, bit)
        arr = add(kept, swap(sent, "dp", bit))
    return arr


def gather(arr, bits):
    for bit in reversed(bits):
        other = swap(arr, "dp", bit)
        arr = jnp.where(
            side_of(bit) == 0,
            jnp.concatenate((arr, other), axis=0),
            jnp.concatenate((other, arr), axis=0),
        )
    return arr


def pieces(arr):
    n = lax.axis_size("dp")
    return arr.reshape(*arr.shape[:-2], n, arr.shape[-2] // n, arr.shape[-1])


def rows_of(arr):
    return arr.reshape(-1, arr.shape[-1])


def reduce_small(arr):
    bit = 1
    while bit < lax.axis_size("mp"):
        arr = arr + swap(arr, "mp", bit)
        bit *= 2
    for bit in dp_bits():
        arr = arr + swap(arr, "dp", bit)
    return arr


def per_device(
    block_input, group_ids, intr_table, ln1_gain, ln1_bias, w_qkv, b_qv, w_out, b_out,
    ln2_gain, ln2_bias, w_up, b_up, w_down, b_down, cotangent,
):
    rows_own, width = block_input.shape
    padded = -(-rows_own // 128) * 128
    groups = intr_table.shape[0]
    feat, hid = w_out.shape[0], w_down.shape[0]
    heads = feat // HEAD
    me = lax.axis_index("mp")
    bits = dp_bits()
    row = lambda v: v.reshape(1, -1)

    onehot = (group_ids[:, None] == jnp.arange(groups, dtype=jnp.int32)[None, :]).astype(BF)
    h0_rows = (
        block_input.astype(F32) + jnp.dot(onehot, intr_table, preferred_element_type=F32)
    ).astype(BF)
    ids_row = jnp.pad(group_ids.astype(BF)[None, :], ((0, 0), (0, width - rows_own)))
    h0 = jnp.concatenate(
        (h0_rows, ids_row, jnp.zeros((padded - rows_own - 1, width), BF)), axis=0
    )
    h_x = swap(h0, "mp", 2)
    h_c = swap(h0, "mp", 1)
    h_xc = swap(h_x, "mp", 1)
    hs = (h0, h_c, h_x, h_xc)

    b_rows = jnp.stack(three_parts(b_up), axis=0)
    pack = jnp.concatenate(
        (w_out, jnp.pad(b_rows, ((0, 29), (0, width - hid))), w_up.T, w_down), axis=0
    )
    cut_0 = pack.shape[0] // 64 * 32
    cuts = (cut_0, pack.shape[0] - cut_0)
    side = side_of(1)
    w_c = swap(pack, "mp", 1)
    x_parts = []
    ready = h_x
    for base, size in ((0, cuts[0]), (cuts[0], cuts[1])):
        sent = lax.dynamic_slice_in_dim(pack, base + side * (size // 2), size // 2, 0)
        near = swap(after(sent, ready), "mp", 2)
        ready = near
        x_parts.append(near)
    dy = jnp.pad(cotangent, ((0, padded - rows_own), (0, 0)))

    w_t = (
        w_qkv.reshape(width, 3, heads, HEAD).transpose(2, 1, 3, 0).reshape(3 * feat, width)
    )
    b_three = jnp.stack((b_qv[0], jnp.zeros((feat,), F32), b_qv[1]), axis=0)
    b_t = b_three.reshape(3, heads, HEAD).transpose(1, 0, 2).reshape(3 * feat, 1)
    a1, qkv, probs, o32, rl, *o_ts = attend(rows_own, hs, row(ln1_gain), row(ln1_bias), w_t, b_t)

    x_near = [after(p, o_ts[0]) for p in x_parts]
    x_all = []
    for near in x_near:
        x_all += [near, swap(near, "dp", 1)]
    xc_all = [swap(p, "mp", 1) for p in x_all]
    o_ts = [o_ts[0]] + [swap(o_ts[j], "mp", j) for j in (1, 2, 3)]
    (
        mixed, dh1, *do_ts, act, du, a2, dattn, small_own, db_up,
    ) = own_a(
        rows_own, groups, (hid, feat), cuts, side.reshape(1), o_ts, h0, dy,
        (pack, w_c, *x_all, *xc_all),
        row(b_out), row(ln2_gain), row(ln2_bias), row(b_down),
    )
    do_ts = [do_ts[0]] + [swap(do_ts[j], "mp", j) for j in (1, 2, 3)]
    cut = feat // 3
    keep_a, send_a, keep_b, send_b = own_b(cut, act, du, a2, dattn, dy, o_ts)
    sum_a = add(keep_a, swap(send_a, "mp", 1))
    sum_b = add(keep_b, swap(send_b, "mp", 1))

    g_a = pieces(add(sum_a[0], swap(sum_a[1], "mp", 2)))
    g_a = gather(scatter(g_a, bits), bits)
    g_b = scatter(pieces(sum_b), bits)
    g_b = gather(add(g_b[0], swap(g_b[1], "mp", 2)), bits)
    g_a, g_b = rows_of(g_a), rows_of(g_b)

    dqkv_1, dw_1 = back_1(heads - 1, do_ts, a1, qkv, probs, o32, rl)
    keep, send, dw_2, small_att, db = back_2(
        rows_own, groups, do_ts, hs, a1, qkv, probs, o32, rl, row(ln1_gain), w_t, dqkv_1
    )
    part = add(keep, swap(send, "mp", 1))
    dh0 = dh1 + part[0].astype(F32) + swap(part[1], "mp", 2).astype(F32)
    input_grad = dh0[:rows_own].astype(BF)

    g_1 = rows_of(gather(scatter(pieces(dw_1), bits), bits))
    g_2 = rows_of(gather(scatter(pieces(dw_2), bits), bits))

    up_rows = jnp.zeros((4, hid), F32)
    for j in range(4):
        up_rows = lax.dynamic_update_slice(up_rows, db_up[j : j + 1], (me ^ j, 0))
    db_3 = db[0].reshape(heads, 3, HEAD)
    qv_own = jnp.stack((db_3[:, 0].reshape(feat), db_3[:, 2].reshape(feat)), axis=0)[:, None, :]
    qv_rows = lax.dynamic_update_slice(jnp.zeros((2, 4, feat), F32), qv_own, (0, me, 0))
    small = jnp.concatenate(
        (
            small_own[:groups] + small_att[:groups],
            small_own[groups : groups + 4],
            small_att[groups : groups + 2],
            up_rows.reshape(-1, width),
            qv_rows.reshape(-1, width),
        ),
        axis=0,
    )
    small = reduce_small(small)
    at = groups
    up_at = at + 6
    qv_at = up_at + 4 * hid // width
    b_up_grad = lax.dynamic_slice(small[up_at:qv_at].reshape(4, hid), (me, 0), (1, hid))[0]
    b_qv_grad = lax.dynamic_slice(
        small[qv_at:].reshape(2, 4, feat), (0, me, 0), (2, 1, feat)
    ).reshape(2, feat)
    g_qkv = jnp.concatenate((g_1, g_2), axis=0).astype(F32)
    w_qkv_grad = (
        g_qkv.reshape(heads, 3, HEAD, width).transpose(3, 1, 0, 2).reshape(width, 3, feat)
    )
    return (
        mixed,
        input_grad,
        small[:groups],
        small[at + 4],
        small[at + 5],
        w_qkv_grad,
        b_qv_grad,
        jnp.concatenate((g_a[hid:], g_b[hid:]), axis=0).astype(F32),
        small[at],
        small[at + 1],
        small[at + 2],
        g_a[:hid].astype(F32).T,
        b_up_grad,
        g_b[:hid].astype(F32),
        small[at + 3],
    )


def solution(mesh):
    rows = P(("dp", "mp"), None)
    return jax.shard_map(
        per_device,
        mesh=mesh,
        in_specs=(
            rows, P(("dp", "mp")), P(), P(), P(), P(None, None, "mp"), P(None, "mp"), P("mp", None),
            P(), P(), P(), P(None, "mp"), P("mp"), P("mp", None), P(), rows,
        ),
        out_specs=(
            rows, rows, P(), P(), P(), P(None, None, "mp"), P(None, "mp"), P("mp", None),
            P(), P(), P(), P(None, "mp"), P("mp"), P("mp", None), P(),
        ),
        check_vma=False,
    )
```

```python
import jax
import jax.numpy as jnp
from jax import lax
from jax.experimental import pallas as pl
from jax.experimental.pallas import tpu as pltpu
from jax.sharding import PartitionSpec as P

HEAD = 64
BF = jnp.bfloat16
F32 = jnp.float32
LOG2E = 1.4426950408889634
NN = (((1,), (0,)), ((), ()))
NT = (((1,), (1,)), ((), ()))
TN = (((0,), (0,)), ((), ()))
QB = 256
SD = jax.ShapeDtypeStruct
SAFE = 3000.0
EXTRA = 32


def mm(a, b, dims):
    return lax.dot_general(a, b, dims, preferred_element_type=F32)


def three_parts(v):
    hi = v.astype(BF)
    rest = v - hi.astype(F32)
    mid = rest.astype(BF)
    low = (rest - mid.astype(F32)).astype(BF)
    return hi, mid, low


def norm_rows(rows):
    centre = rows - jnp.mean(rows, axis=-1, keepdims=True)
    var = jnp.mean(centre * centre, axis=-1, keepdims=True)
    rstd = lax.rsqrt(var + 1e-05)
    return centre * rstd, rstd


def norm_back(grad, normed, rstd, gain):
    scaled = grad * gain
    return rstd * (
        scaled
        - jnp.mean(scaled, axis=-1, keepdims=True)
        - normed * jnp.mean(scaled * normed, axis=-1, keepdims=True)
    )


def gelu_parts(u):
    square = u * u
    t = jnp.tanh(0.7978845608028654 * (u + 0.044715 * (u * square)))
    half = 0.5 * (1.0 + t)
    slope = half + 0.5 * u * (1.0 - t * t) * (
        0.7978845608028654 + (3 * 0.044715 * 0.7978845608028654) * square
    )
    return u * half, slope


def onehot_rows(ids_row, groups):
    levels = lax.broadcasted_iota(jnp.int32, (groups, ids_row.shape[1]), 0).astype(F32)
    return (levels == ids_row).astype(F32).astype(BF)


def onehot_sum(hot, rows):
    hi = rows.astype(BF)
    low = (rows - hi.astype(F32)).astype(BF)
    return mm(hot, hi, NN) + mm(hot, low, NN)


def ids_of(h, rows_own, padded):
    tail = h[padded - 16 :, :].astype(F32)
    at = rows_own - padded + 16
    return tail[at : at + 1, :padded]


class Copy:
    def __init__(self, src, dst, sem, near):
        self.copy = pltpu.make_async_copy(src, dst, sem)
        self.ref = near
        self.begun = False
        self.ended = False

    def start(self):
        if not self.begun:
            self.begun = True
            self.copy.start()
        return self

    def wait(self):
        self.start()
        if not self.ended:
            self.ended = True
            self.copy.wait()
        return self.ref


def hbm_call(
    name, body, ins, outs, *, raw_ins=(), raw_outs=(), smem=(), scratch=(), limit, flops, nbytes,
    eager=True,
):
    hbm = pl.BlockSpec(memory_space=pltpu.HBM)
    n_i, n_o = len(ins), len(outs)

    def kernel(*refs):
        rest = list(refs)

        def take(n):
            got = rest[:n]
            del rest[:n]
            return got

        small = take(len(smem))
        far_i, raw_i = take(n_i), take(len(raw_ins))
        far_o, raw_o = take(n_o), take(len(raw_outs))
        near_i, near_o = take(n_i), take(n_o)
        own = take(len(scratch))
        sem_i, sem_o = take(2)
        feeds = [Copy(f, n, sem_i.at[k], n) for k, (f, n) in enumerate(zip(far_i, near_i))]
        sinks = [Copy(n, f, sem_o.at[k], n) for k, (f, n) in enumerate(zip(far_o, near_o))]
        if eager:
            for feed in feeds:
                feed.start()
        body(small, feeds, raw_i, sinks, raw_o, own)
        for sink in sinks:
            sink.start()
        for sink in sinks:
            sink.wait()
        for feed in feeds:
            feed.wait()

    vmem = lambda a: pltpu.VMEM(a.shape, a.dtype)
    return pl.pallas_call(
        kernel,
        out_shape=tuple(outs) + tuple(raw_outs),
        in_specs=[pl.BlockSpec(memory_space=pltpu.SMEM)] * len(smem)
        + [hbm] * (n_i + len(raw_ins)),
        out_specs=(hbm,) * (n_o + len(raw_outs)),
        scratch_shapes=[vmem(a) for a in ins]
        + [vmem(a) for a in outs]
        + list(scratch)
        + [pltpu.SemaphoreType.DMA((n_i,)), pltpu.SemaphoreType.DMA((n_o,))],
        compiler_params=pltpu.CompilerParams(vmem_limit_bytes=limit * 2**20),
        cost_estimate=pl.CostEstimate(flops=flops, bytes_accessed=nbytes, transcendentals=0),
        name=name,
    )(*smem, *ins, *raw_ins)


def forward_heads(heads, first, rows_own, qkv, probs, o32, rl, p_buf, p_sem):
    tokens = qkv.shape[1]
    padded = tokens // 4
    lane = lax.broadcasted_iota(jnp.int32, (16, tokens), 1)
    sub = lax.broadcasted_iota(jnp.int32, (16, tokens), 0)
    valid = jnp.zeros((16, tokens), jnp.bool_)
    for j in range(4):
        valid = valid | ((lane >= j * padded) & (lane < j * padded + rows_own))
    top_row = sub == 0
    mask = jnp.where(top_row & ~valid, -1e30, 0.0).astype(BF)
    ones = jnp.where(top_row, 1.0, 0.0).astype(BF)
    half = tokens // 2
    slots = p_buf.shape[0]
    copies = [None] * slots
    step = 0
    for h in range(heads):
        at = 3 * (first + h) * HEAD
        scaled = qkv[at : at + HEAD, :].astype(F32) * (0.125 * LOG2E)
        hi = scaled.astype(BF)
        low = (scaled - hi.astype(F32)).astype(BF)
        q_x = jnp.concatenate((hi, low, ones), axis=0)
        k_h = qkv[at + HEAD : at + 2 * HEAD, :]
        k_f = k_h.astype(F32)
        k_x = jnp.concatenate((k_h, k_h, mask), axis=0)
        v_x = jnp.concatenate((qkv[at + 2 * HEAD : at + 3 * HEAD, :], ones), axis=0)
        bound = jnp.max(jnp.sum(scaled * scaled, axis=0, keepdims=True)) * jnp.max(
            jnp.sum(k_f * k_f, axis=0, keepdims=True)
        )
        small = bound < SAFE
        for part in range(2):
            slot = step % slots
            if copies[slot] is not None:
                copies[slot].wait()

            def block(b, exact, slot=slot, h=h, part=part, q_x=q_x, k_x=k_x, v_x=v_x):
                cols = slice(part * half + b * QB, part * half + (b + 1) * QB)
                scores = mm(q_x[:, cols], k_x, TN)
                if exact:
                    scores = scores - jnp.max(scores, axis=-1, keepdims=True)
                p_block = jnp.exp2(scores).astype(BF)
                p_buf[slot, b * QB : (b + 1) * QB, :] = p_block
                out = mm(v_x, p_block, NT)
                inv = 1.0 / out[HEAD : HEAD + 1, :]
                o32[h * HEAD : (h + 1) * HEAD, cols] = out[:HEAD, :] * inv
                rl[h : h + 1, cols] = inv

            @pl.when(small)
            def _():
                for b in range(half // QB):
                    block(b, False)

            @pl.when(jnp.logical_not(small))
            def _():
                for b in range(half // QB):
                    block(b, True)

            copies[slot] = pltpu.make_async_copy(
                p_buf.at[slot], probs.at[h, part * half : (part + 1) * half, :], p_sem.at[slot]
            )
            copies[slot].start()
            step += 1
    return [c for c in copies if c is not None]


def attend_1(rows_own, heads, hs, params, w_t, b_t):
    padded, width = hs[0].shape
    tokens = 4 * padded
    rows = w_t.shape[0]

    def body(_, ins, raw_i, outs, raw_o, own):
        a1, qkv, o32, rl, o_b = outs
        p_buf, p_sem = own
        par = ins[5].wait()
        for pair in range(2):
            for j in (2 * pair, 2 * pair + 1):
                normed, _ = norm_rows(ins[j].wait()[...].astype(F32))
                a1.ref[j * padded : (j + 1) * padded, :] = (
                    normed * par[0:1, :] + par[1:2, :]
                ).astype(BF)
            cols = slice(2 * pair * padded, 2 * (pair + 1) * padded)
            w_v, b_v = ins[4].wait(), ins[6].wait()
            qkv.ref[:, cols] = (mm(w_v[...], a1.ref[cols, :], NT) + b_v[...]).astype(BF)
        a1.start()
        qkv.start()
        copies = forward_heads(heads, 0, rows_own, qkv.ref, raw_o[0], o32.ref, rl.ref, p_buf, p_sem)
        o_b.ref[...] = o32.ref[...].astype(BF)
        for sink in (o32, rl, o_b):
            sink.start()
        for copy in copies:
            copy.wait()

    return hbm_call(
        "attend_1", body, (*hs, w_t, params, b_t),
        (
            SD((tokens, width), BF), SD((rows, tokens), BF), SD((heads * HEAD, tokens), F32),
            SD((8, tokens), F32), SD((heads * HEAD, tokens), BF),
        ),
        raw_outs=(SD((heads, tokens, tokens), BF),),
        scratch=[pltpu.VMEM((3, tokens // 2, tokens), BF), pltpu.SemaphoreType.DMA((3,))],
        limit=48, flops=9_000_000_000, nbytes=20_000_000,
    )


def attend_2(rows_own, heads, qkv, o_b):
    rows, tokens = qkv.shape
    padded = tokens // 4
    feat = rows // 3
    done = o_b.shape[0] // HEAD

    def body(_, ins, raw_i, outs, raw_o, own):
        o32, rl = outs[:2]
        p_buf, p_sem, q_v, q_sem = own
        get = pltpu.make_async_copy(raw_i[0].at[3 * done * HEAD :, :], q_v, q_sem.at[0])
        get.start()
        get.wait()
        copies = forward_heads(heads, 0, rows_own, q_v, raw_o[0], o32.ref, rl.ref, p_buf, p_sem)
        o_1 = ins[0].wait()
        for j, o in enumerate(outs[2:]):
            cols = slice(j * padded, (j + 1) * padded)
            o.ref[: done * HEAD, :] = o_1[:, cols]
            o.ref[done * HEAD :, :] = o32.ref[:, cols].astype(BF)
        for sink in outs:
            sink.start()
        for copy in copies:
            copy.wait()

    return hbm_call(
        "attend_2", body, (o_b,),
        (SD((heads * HEAD, tokens), F32), SD((8, tokens), F32)) + (SD((feat, padded), BF),) * 4,
        raw_ins=(qkv,),
        raw_outs=(SD((heads, tokens, tokens), BF),),
        scratch=[
            pltpu.VMEM((2, tokens // 2, tokens), BF), pltpu.SemaphoreType.DMA((2,)),
            pltpu.VMEM((3 * heads * HEAD, tokens), BF), pltpu.SemaphoreType.DMA((1,)),
        ],
        limit=48, flops=4_000_000_000, nbytes=6_000_000,
    )


def own_0(o_ts, h0, w_outs, params):
    padded, width = h0.shape

    def body(_, ins, raw_i, outs, raw_o, own):
        par = ins[9].wait()
        attn = par[2:3, :]
        for j in range(4):
            attn = attn + mm(ins[j].wait()[...], ins[5 + j].wait()[...], TN)
        h1 = ins[4].wait()[...].astype(F32) + attn
        outs[1].ref[...] = h1
        outs[1].start()
        normed, _ = norm_rows(h1)
        outs[0].ref[...] = (normed * par[3:4, :] + par[4:5, :]).astype(BF)

    return hbm_call(
        "own_0", body, (*o_ts, h0, *w_outs, params),
        (SD((padded, width), BF), SD((padded, width), F32)),
        limit=32, flops=900_000_000, nbytes=4_500_000,
    )


def own_1(rows_own, groups, sizes, side, h1, a2, dy, h0, w_outs, params, ups, downs):
    hid, feat = sizes
    padded, width = h1.shape
    up_rows, down_rows = hid + EXTRA, hid

    def body(smem, ins, raw_i, outs, raw_o, own):
        w_v, w_sem = own
        me = smem[0][0]
        loads = []
        for c, (base, size) in enumerate(((0, up_rows), (up_rows, down_rows))):
            n = size // 2
            near = pl.multiple_of(base + me * n, 16)
            far = pl.multiple_of(base + (1 - me) * n, 16)
            part = raw_i[6 * c : 6 * c + 6]
            for k, (j, at, num) in enumerate(
                ((0, base, size), (1, base, size), (2, near, n), (2, far, n), (3, near, n), (3, far, n))
            ):
                loads.append(
                    pltpu.make_async_copy(part[k], w_v.at[j, pl.ds(at, num), :], w_sem.at[6 * c + k])
                )
        order = (0, 6, 1, 7, 2, 3, 8, 9, 4, 5, 10, 11)
        need = ((0, 6), (1, 7), (2, 3, 8, 9), (4, 5, 10, 11))
        for k in order:
            loads[k].start()
        par = ins[4].wait()
        h1_v, a2_v = ins[0].wait()[...], ins[1].wait()[...]
        dy_b = ins[2].wait()[...]
        normed, rstd = norm_rows(h1_v)
        acc = h1_v + par[5:6, :]
        da2 = jnp.zeros((padded, width), F32)
        up, down = slice(EXTRA, up_rows), slice(up_rows, up_rows + hid)
        for j in range(4):
            for k in need[j]:
                loads[k].wait()
            rows = w_v[j, 0:16, :].astype(F32)
            b_up = (rows[0:1] + rows[1:2] + rows[2:3])[:, :hid]
            value, slope = gelu_parts(mm(a2_v, w_v[j, up, :], NT) + b_up)
            acc = acc + mm(value.astype(BF), w_v[j, down, :], NN)
            du = (mm(dy_b, w_v[j, down, :], NT) * slope).astype(BF)
            da2 = da2 + mm(du, w_v[j, up, :], NN)
        mixed, dh1, dattn_o, small = outs[:4]
        dyf = dy_b.astype(F32)
        total = dyf + norm_back(da2, normed, rstd, par[3:4, :])
        dattn = total.astype(BF)
        for j in range(4):
            outs[4 + j].ref[...] = mm(ins[5 + j].wait()[...], dattn, NT).astype(BF)
            outs[4 + j].start()
        mixed.ref[...] = acc[:rows_own].astype(BF)
        mixed.start()
        dh1.ref[...] = total
        dh1.start()
        dattn_o.ref[...] = dattn
        dattn_o.start()
        hot = onehot_rows(ids_of(ins[3].wait(), rows_own, padded), groups)
        small.ref[0:groups, :] = onehot_sum(hot, total)
        small.ref[groups : groups + 8, :] = jnp.concatenate(
            (
                jnp.sum(dattn.astype(F32), axis=0, keepdims=True),
                jnp.sum(da2 * normed, axis=0, keepdims=True),
                jnp.sum(da2, axis=0, keepdims=True),
                jnp.sum(dyf, axis=0, keepdims=True),
                jnp.zeros((4, width), F32),
            ),
            axis=0,
        )

    return hbm_call(
        "own_1", body, (h1, a2, dy, h0, params, *w_outs),
        (
            SD((rows_own, width), BF), SD((padded, width), F32), SD((padded, width), BF),
            SD((groups + 8, width), F32),
        )
        + (SD((feat, padded), BF),) * 4,
        raw_ins=(*ups, *downs),
        smem=(side,),
        scratch=[pltpu.VMEM((4, up_rows + down_rows, width), BF), pltpu.SemaphoreType.DMA((12,))],
        limit=48, flops=5_000_000_000, nbytes=14_000_000,
    )


def weight_grads(a2s, dys, up_pack, down, o_ts, dattn):
    padded, width = a2s[0].shape
    hid = down.shape[0]
    feat = o_ts[0].shape[0]
    tokens = 4 * padded

    def body(_, ins, raw_i, outs, raw_o, own):
        act, du, a2, dy, sem = own
        gets = []
        for j in range(4):
            rows = slice(j * padded, (j + 1) * padded)
            gets.append(
                (
                    pltpu.make_async_copy(raw_i[j], a2.at[rows, :], sem.at[2 * j]),
                    pltpu.make_async_copy(raw_i[4 + j], dy.at[rows, :], sem.at[2 * j + 1]),
                )
            )
            for get in gets[j]:
                get.start()
        dattn_v = ins[6].wait()[...]
        for j in range(4):
            (outs[1], outs[2])[j % 2].ref[j // 2] = mm(ins[2 + j].wait()[...], dattn_v, NN).astype(BF)
        outs[1].start()
        outs[2].start()
        up_v, down_v = ins[0].wait(), ins[1].wait()
        rows = up_v[0:16, :].astype(F32)
        b_up = (rows[0:1] + rows[1:2] + rows[2:3])[:, :hid]
        db = jnp.zeros((1, hid), F32)
        for j in range(4):
            at = slice(j * padded, (j + 1) * padded)
            for get in gets[j]:
                get.wait()
            value, slope = gelu_parts(mm(a2[at, :], up_v[EXTRA:, :], NT) + b_up)
            act[at, :] = value.astype(BF)
            du_j = (mm(dy[at, :], down_v[...], NT) * slope).astype(BF)
            du[at, :] = du_j
            db = db + jnp.sum(du_j.astype(F32), axis=0, keepdims=True)
        outs[3].ref[...] = jnp.broadcast_to(db, (8, hid))
        outs[0].ref[:hid, :] = mm(du[...], a2[...], TN).astype(BF)
        outs[0].ref[hid:, :] = mm(act[...], dy[...], TN).astype(BF)

    return hbm_call(
        "weight_grads", body, (up_pack, down, *o_ts, dattn),
        (
            SD((2 * hid, width), BF), SD((2, feat, width), BF), SD((2, feat, width), BF),
            SD((8, hid), F32),
        ),
        raw_ins=(*a2s, *dys),
        scratch=[pltpu.VMEM((tokens, hid), BF)] * 2
        + [pltpu.VMEM((tokens, width), BF)] * 2
        + [pltpu.SemaphoreType.DMA((8,))],
        limit=40, flops=5_000_000_000, nbytes=10_000_000,
    )


def back_heads(heads, first, dos, q_v, probs, o32, rl, dqkv, d_s, p_all, p_sem, ready):
    tokens = q_v.shape[1]
    half = tokens // 2

    def fetch(i):
        h, part = divmod(i, 2)
        return pltpu.make_async_copy(
            probs.at[h, part * half : (part + 1) * half, :],
            p_all.at[h, part * half : (part + 1) * half, :],
            p_sem.at[i],
        )

    fetches = [fetch(i) for i in range(2 * heads)]
    for f in fetches[:2]:
        f.start()
    ready()
    for f in fetches[2:]:
        f.start()
    d_out = jnp.concatenate([d[...] for d in dos], axis=1)
    sub = lax.broadcasted_iota(jnp.int32, (16, tokens), 0)
    ones = jnp.where(sub < 3, 1.0, 0.0).astype(BF)
    zero = jnp.zeros((13, tokens), F32)
    for h in range(heads):
        at = h * 3 * HEAD
        src = (first + h) * HEAD
        do_s = (d_out[src : src + HEAD, :].astype(F32) * rl[h : h + 1, :]).astype(BF)
        delta = -jnp.sum(
            do_s.astype(F32) * o32[h * HEAD : (h + 1) * HEAD, :], axis=0, keepdims=True
        )
        d_hi = delta.astype(BF).astype(F32)
        d_mid = (delta - d_hi).astype(BF).astype(F32)
        d_low = delta - d_hi - d_mid
        tail = jnp.concatenate((d_hi, d_mid, d_low, zero), axis=0).astype(BF)
        do_x = jnp.concatenate((do_s, tail), axis=0)
        q_h = q_v[at : at + HEAD, :]
        k_h = q_v[at + HEAD : at + 2 * HEAD, :]
        v_x = jnp.concatenate((q_v[at + 2 * HEAD : at + 3 * HEAD, :], ones), axis=0)
        for b in range(tokens // QB):
            cols = slice(b * QB, (b + 1) * QB)
            if b * QB in (0, half):
                fetches[2 * h + b * QB // half].wait()
            dp = mm(do_x[:, cols], v_x, TN)
            ds = (p_all[h, cols, :].astype(F32) * dp).astype(BF)
            d_s[cols, :] = ds
            dqkv[at : at + HEAD, cols] = (0.125 * mm(k_h, ds, NT)).astype(BF)
        dqkv[at + HEAD : at + 2 * HEAD, :] = (0.125 * mm(q_h, d_s[...], NN)).astype(BF)
        dqkv[at + 2 * HEAD : at + 3 * HEAD, :] = mm(do_s, p_all[h], NN).astype(BF)


def back_scratch(heads, tokens):
    return [
        pltpu.VMEM((tokens, tokens), BF),
        pltpu.VMEM((heads, tokens, tokens), BF),
        pltpu.SemaphoreType.DMA((2 * heads,)),
        pltpu.VMEM((3 * heads * HEAD, tokens), BF),
        pltpu.SemaphoreType.DMA((1,)),
    ]


def back_1(heads, dos, a1, qkv, probs, o32, rl):
    tokens, width = a1.shape
    rows = heads * 3 * HEAD

    def body(_, ins, raw_i, outs, raw_o, own):
        d_s, p_all, p_sem, q_v, q_sem = own
        get = pltpu.make_async_copy(raw_i[1].at[:rows, :], q_v, q_sem.at[0])

        def ready():
            get.start()
            for feed in ins[:6]:
                feed.start()
            get.wait()
            for feed in ins[:6]:
                feed.wait()

        dqkv, dw = outs
        back_heads(
            heads, 0, [f.ref for f in ins[:4]], q_v, raw_i[0], ins[4].ref, ins[5].ref, dqkv.ref,
            d_s, p_all, p_sem, ready,
        )
        dqkv.start()
        dw.ref[...] = mm(dqkv.ref[...], ins[6].wait()[...], NN).astype(BF)

    return hbm_call(
        "back_1", body, (*dos, o32, rl, a1), (SD((rows, tokens), BF), SD((rows, width), BF)),
        raw_ins=(probs, qkv),
        scratch=back_scratch(heads, tokens),
        limit=48, flops=14_000_000_000, nbytes=18_000_000, eager=False,
    )


def back_2(rows_own, groups, heads, dos, hs, a1, qkv, probs, o32, rl, params, w_t, dqkv_1):
    tokens, width = a1.shape
    padded = hs[0].shape[0]
    cut = dqkv_1.shape[0]
    rows = w_t.shape[0] - cut

    def body(_, ins, raw_i, outs, raw_o, own):
        d_s, p_all, p_sem, q_v, q_sem, dqkv = own
        get = pltpu.make_async_copy(raw_i[1].at[cut:, :], q_v, q_sem.at[0])

        def ready():
            get.start()
            for feed in ins[:6]:
                feed.start()
            get.wait()
            for feed in ins[:6]:
                feed.wait()
            for feed in ins[6:]:
                feed.start()

        back_heads(
            heads, cut // (3 * HEAD), [f.ref for f in ins[:4]], q_v, raw_i[0], ins[4].ref,
            ins[5].ref, dqkv, d_s, p_all, p_sem, ready,
        )
        dw, send, keep, small, db = outs
        dw.ref[...] = mm(dqkv[...], ins[6].wait()[...], NN).astype(BF)
        dw.start()
        w_v, d1, par = ins[7].wait(), ins[8].wait(), ins[9].wait()
        ones = jnp.ones((8, tokens), BF)
        db.ref[:, :cut] = mm(ones, d1[...], NT)
        db.ref[:, cut:] = mm(ones, dqkv[...], NT)
        db.start()
        gain = par[0:1, :]
        table = jnp.zeros((groups, width), F32)
        dgain = jnp.zeros((1, width), F32)
        dbias = jnp.zeros((1, width), F32)
        for j in (3, 1, 2, 0):
            at = slice(j * padded, (j + 1) * padded)
            da1 = mm(d1[:, at], w_v[:cut, :], TN) + mm(dqkv[:, at], w_v[cut:, :], TN)
            h = ins[10 + j].wait()
            normed, rstd = norm_rows(h[...].astype(F32))
            back = norm_back(da1, normed, rstd, gain)
            (keep, send)[j % 2].ref[j // 2] = back.astype(BF)
            dgain = dgain + jnp.sum(da1 * normed, axis=0, keepdims=True)
            dbias = dbias + jnp.sum(da1, axis=0, keepdims=True)
            table = table + onehot_sum(onehot_rows(ids_of(h, rows_own, padded), groups), back)
            if j == 1:
                send.start()
        keep.start()
        small.ref[0:groups, :] = table
        small.ref[groups : groups + 8, :] = jnp.concatenate(
            (dgain, dbias, jnp.zeros((6, width), F32)), axis=0
        )

    return hbm_call(
        "back_2", body, (*dos, o32, rl, a1, w_t, dqkv_1, params, *hs),
        (
            SD((rows, width), BF), SD((2, padded, width), BF), SD((2, padded, width), BF),
            SD((groups + 8, width), F32), SD((8, w_t.shape[0]), F32),
        ),
        raw_ins=(probs, qkv),
        scratch=back_scratch(heads, tokens) + [pltpu.VMEM((rows, tokens), BF)],
        limit=48, flops=10_000_000_000, nbytes=18_000_000, eager=False,
    )


def swap(arr, axis, bit):
    size = lax.axis_size(axis)
    return lax.ppermute(arr, axis, [(i, i ^ bit) for i in range(size)])


def add(a, b):
    return (a.astype(F32) + b.astype(F32)).astype(a.dtype)


def after(value, *others):
    return lax.optimization_barrier((value, others))[0]


def side_of(bit):
    return (lax.axis_index("dp") // bit) % 2


def dp_bits():
    bits, bit = [], 1
    while bit < lax.axis_size("dp"):
        bits.append(bit)
        bit *= 2
    return bits


def reduce_dp(arr, bits):
    pieces = 2 ** (len(bits) - 1)
    width = arr.shape[1]
    cur = arr.reshape(pieces, arr.shape[0] // pieces, width)
    for bit in bits[:-1]:
        half = cur.shape[0] // 2
        side = side_of(bit)
        kept = lax.dynamic_slice_in_dim(cur, side * half, half, 0)
        sent = lax.dynamic_slice_in_dim(cur, (1 - side) * half, half, 0)
        cur = add(kept, swap(sent, "dp", bit))
    cur = add(cur, swap(cur, "dp", bits[-1]))
    for bit in reversed(bits[:-1]):
        other = swap(cur, "dp", bit)
        cur = jnp.where(
            side_of(bit) == 0,
            jnp.concatenate((cur, other), axis=0),
            jnp.concatenate((other, cur), axis=0),
        )
    return cur.reshape(-1, width)


def reduce_small(arr):
    bit = 1
    while bit < lax.axis_size("mp"):
        arr = arr + swap(arr, "mp", bit)
        bit *= 2
    for bit in dp_bits():
        arr = arr + swap(arr, "dp", bit)
    return arr


def per_device(
    block_input, group_ids, intr_table, ln1_gain, ln1_bias, w_qkv, b_qv, w_out, b_out,
    ln2_gain, ln2_bias, w_up, b_up, w_down, b_down, cotangent,
):
    rows_own, width = block_input.shape
    padded = -(-rows_own // 128) * 128
    groups = intr_table.shape[0]
    feat, hid = w_out.shape[0], w_down.shape[0]
    heads = feat // HEAD
    me = lax.axis_index("mp")
    bits = dp_bits()

    onehot = (group_ids[:, None] == jnp.arange(groups, dtype=jnp.int32)[None, :]).astype(BF)
    h0_rows = (
        block_input.astype(F32) + jnp.dot(onehot, intr_table, preferred_element_type=F32)
    ).astype(BF)
    ids_row = jnp.pad(group_ids.astype(BF)[None, :], ((0, 0), (0, width - rows_own)))
    h0 = jnp.concatenate(
        (h0_rows, ids_row, jnp.zeros((padded - rows_own - 1, width), BF)), axis=0
    )
    h_x = swap(h0, "mp", 2)
    h_c = swap(h0, "mp", 1)
    h_xc = swap(h_x, "mp", 1)
    hs = (h0, h_c, h_x, h_xc)

    zero_row = jnp.zeros((width,), F32)
    params = jnp.stack(
        (ln1_gain, ln1_bias, b_out, ln2_gain, ln2_bias, b_down, zero_row, zero_row), axis=0
    )
    w_t = (
        w_qkv.reshape(width, 3, heads, HEAD).transpose(2, 1, 3, 0).reshape(3 * feat, width)
    )
    b_three = jnp.stack((b_qv[0], jnp.zeros((feat,), F32), b_qv[1]), axis=0)
    b_t = b_three.reshape(3, heads, HEAD).transpose(1, 0, 2).reshape(3 * feat, 1)

    b_rows = jnp.stack(three_parts(b_up), axis=0)
    up_pack = jnp.concatenate(
        (jnp.pad(b_rows, ((0, EXTRA - 3), (0, width - hid))), w_up.T), axis=0
    )
    side = side_of(1)

    def half_of(arr):
        n = arr.shape[0] // 2
        return lax.dynamic_slice_in_dim(arr, side * n, n, 0)

    out_x = swap(after(w_out, h_x), "mp", 2)
    out_c = swap(w_out, "mp", 1)
    up_c = swap(up_pack, "mp", 1)
    down_c = swap(w_down, "mp", 1)
    up_near = swap(after(half_of(up_pack), h_x), "mp", 2)
    dy = jnp.pad(cotangent, ((0, padded - rows_own), (0, 0)))

    a1, qkv, o32_1, rl_1, o_b, probs_1 = attend_1(rows_own, heads - 1, hs, params, w_t, b_t)

    up_near, out_x, down_half = lax.optimization_barrier((up_near, out_x, half_of(w_down), o_b))[:3]
    out_xc = swap(out_x, "mp", 1)
    down_near = swap(down_half, "mp", 2)
    up_far = swap(up_near, "dp", 1)
    o32_2, rl_2, *o_ts, probs_2 = attend_2(rows_own, 1, qkv, o_b)
    o_ts = [o_ts[0]] + [swap(o_ts[j], "mp", j) for j in (1, 2, 3)]
    down_near, up_far = lax.optimization_barrier((down_near, up_far, o32_2))[:2]
    down_far = swap(down_near, "dp", 1)
    up_xc = [swap(p, "mp", 1) for p in (up_near, up_far)]
    down_xc = [swap(p, "mp", 1) for p in (down_near, down_far)]

    dy_x = swap(after(dy, o_ts[2]), "mp", 2)
    dy_c = swap(dy, "mp", 1)
    w_outs = (w_out, out_c, out_x, out_xc)
    a2, h1 = own_0(o_ts, h0, w_outs, params)
    a2_x = swap(a2, "mp", 2)
    a2_c = swap(a2, "mp", 1)
    mixed, dh1, dattn, small_own, *do_ts = own_1(
        rows_own, groups, (hid, feat), side.reshape(1), h1, a2, dy, h0, w_outs, params,
        (up_pack, up_c, up_near, up_far, *up_xc),
        (w_down, down_c, down_near, down_far, *down_xc),
    )
    do_ts = [do_ts[0]] + [swap(do_ts[j], "mp", j) for j in (1, 2, 3)]
    dy_x, a2_x = lax.optimization_barrier((dy_x, a2_x, dattn))[:2]
    a2_xc = swap(a2_x, "mp", 1)
    dy_xc = swap(dy_x, "mp", 1)
    g_mlp, keep_o, send_o, db_up = weight_grads(
        (a2, a2_c, a2_x, a2_xc), (dy, dy_c, dy_x, dy_xc), up_pack, w_down, o_ts, dattn
    )
    g_mlp = lax.psum(g_mlp, "dp")
    sum_o = add(keep_o, swap(send_o, "mp", 1))
    other_o = swap(sum_o[1], "mp", 2)

    do_ts = lax.optimization_barrier((*do_ts, db_up))[:4]
    dqkv_1, dw_1 = back_1(heads - 1, do_ts, a1, qkv, probs_1, o32_1, rl_1)
    g_o = add(sum_o[0], after(other_o, dw_1))
    g_1 = reduce_dp(jnp.concatenate((dw_1, g_o), axis=0), bits)
    dw_2, send, keep, small_att, db = back_2(
        rows_own, groups, 1, do_ts, hs, a1, qkv, probs_2, o32_2, rl_2, params, w_t, dqkv_1
    )
    part = add(keep, swap(send, "mp", 1))
    dh0 = dh1 + part[0].astype(F32) + swap(part[1], "mp", 2).astype(F32)
    input_grad = dh0[:rows_own].astype(BF)
    g_2 = reduce_dp(dw_2, bits)

    up_rows = lax.dynamic_update_slice(jnp.zeros((4, hid), F32), db_up[:1], (me, 0))
    db_3 = db[0].reshape(heads, 3, HEAD)
    qv_own = jnp.stack((db_3[:, 0].reshape(feat), db_3[:, 2].reshape(feat)), axis=0)[:, None, :]
    qv_rows = lax.dynamic_update_slice(jnp.zeros((2, 4, feat), F32), qv_own, (0, me, 0))
    small = jnp.concatenate(
        (
            small_own[:groups] + small_att[:groups],
            small_own[groups : groups + 4],
            small_att[groups : groups + 2],
            up_rows.reshape(-1, width),
            qv_rows.reshape(-1, width),
        ),
        axis=0,
    )
    small = reduce_small(small)
    at = groups
    up_at = at + 6
    qv_at = up_at + 4 * hid // width
    b_up_grad = lax.dynamic_slice(small[up_at:qv_at].reshape(4, hid), (me, 0), (1, hid))[0]
    b_qv_grad = lax.dynamic_slice(
        small[qv_at:].reshape(2, 4, feat), (0, me, 0), (2, 1, feat)
    ).reshape(2, feat)
    cut = dw_1.shape[0]
    g_qkv = jnp.concatenate((g_1[:cut], g_2), axis=0).astype(F32)
    w_qkv_grad = (
        g_qkv.reshape(heads, 3, HEAD, width).transpose(3, 1, 0, 2).reshape(width, 3, feat)
    )
    return (
        mixed,
        input_grad,
        small[:groups],
        small[at + 4],
        small[at + 5],
        w_qkv_grad,
        b_qv_grad,
        g_1[cut:].astype(F32),
        small[at],
        small[at + 1],
        small[at + 2],
        g_mlp[:hid].astype(F32).T,
        b_up_grad,
        g_mlp[hid:].astype(F32),
        small[at + 3],
    )


def solution(mesh):
    rows = P(("dp", "mp"), None)
    return jax.shard_map(
        per_device,
        mesh=mesh,
        in_specs=(
            rows, P(("dp", "mp")), P(), P(), P(), P(None, None, "mp"), P(None, "mp"), P("mp", None),
            P(), P(), P(), P(None, "mp"), P("mp"), P("mp", None), P(), rows,
        ),
        out_specs=(
            rows, rows, P(), P(), P(), P(None, None, "mp"), P(None, "mp"), P("mp", None),
            P(), P(), P(), P(None, "mp"), P("mp"), P("mp", None), P(),
        ),
        check_vma=False,
    )
```

```python
import jax
import jax.numpy as jnp
from jax import lax
from jax.experimental import pallas as pl
from jax.experimental.pallas import tpu as pltpu
from jax.sharding import PartitionSpec as P

HEAD = 64
BF = jnp.bfloat16
F32 = jnp.float32
LOG2E = 1.4426950408889634
NN = (((1,), (0,)), ((), ()))
NT = (((1,), (1,)), ((), ()))
TN = (((0,), (0,)), ((), ()))
QB = 256
SD = jax.ShapeDtypeStruct
SAFE = 3000.0
EXTRA = 32


def mm(a, b, dims):
    return lax.dot_general(a, b, dims, preferred_element_type=F32)


def three_parts(v):
    hi = v.astype(BF)
    rest = v - hi.astype(F32)
    mid = rest.astype(BF)
    low = (rest - mid.astype(F32)).astype(BF)
    return hi, mid, low


def norm_rows(rows):
    centre = rows - jnp.mean(rows, axis=-1, keepdims=True)
    var = jnp.mean(centre * centre, axis=-1, keepdims=True)
    rstd = lax.rsqrt(var + 1e-05)
    return centre * rstd, rstd


def norm_back(grad, normed, rstd, gain):
    scaled = grad * gain
    return rstd * (
        scaled
        - jnp.mean(scaled, axis=-1, keepdims=True)
        - normed * jnp.mean(scaled * normed, axis=-1, keepdims=True)
    )


def gelu_parts(u):
    square = u * u
    t = jnp.tanh(0.7978845608028654 * (u + 0.044715 * (u * square)))
    half = 0.5 * (1.0 + t)
    slope = half + 0.5 * u * (1.0 - t * t) * (
        0.7978845608028654 + (3 * 0.044715 * 0.7978845608028654) * square
    )
    return u * half, slope


def onehot_rows(ids_row, groups):
    levels = lax.broadcasted_iota(jnp.int32, (groups, ids_row.shape[1]), 0).astype(F32)
    return (levels == ids_row).astype(F32).astype(BF)


def onehot_sum(hot, rows):
    hi = rows.astype(BF)
    low = (rows - hi.astype(F32)).astype(BF)
    return mm(hot, hi, NN) + mm(hot, low, NN)


def ids_of(h, rows_own, padded):
    tail = h[padded - 16 :, :].astype(F32)
    at = rows_own - padded + 16
    return tail[at : at + 1, :padded]


class Copy:
    def __init__(self, src, dst, sem, near):
        self.copy = pltpu.make_async_copy(src, dst, sem)
        self.ref = near
        self.begun = False
        self.ended = False

    def start(self):
        if not self.begun:
            self.begun = True
            self.copy.start()
        return self

    def wait(self):
        self.start()
        if not self.ended:
            self.ended = True
            self.copy.wait()
        return self.ref


def hbm_call(
    name, body, ins, outs, *, raw_ins=(), raw_outs=(), near_ins=(), smem=(), scratch=(),
    limit, flops, nbytes, eager=True,
):
    hbm = pl.BlockSpec(memory_space=pltpu.HBM)
    n_i, n_o = len(ins), len(outs)

    def kernel(*refs):
        rest = list(refs)

        def take(n):
            got = rest[:n]
            del rest[:n]
            return got

        small = take(len(smem))
        far_i, raw_i = take(n_i), take(len(raw_ins))
        raw_i = raw_i + take(len(near_ins))
        far_o, raw_o = take(n_o), take(len(raw_outs))
        near_i, near_o = take(n_i), take(n_o)
        own = take(len(scratch))
        sem_i, sem_o = take(2)
        feeds = [Copy(f, n, sem_i.at[k], n) for k, (f, n) in enumerate(zip(far_i, near_i))]
        sinks = [Copy(n, f, sem_o.at[k], n) for k, (f, n) in enumerate(zip(far_o, near_o))]
        if eager:
            for feed in feeds:
                feed.start()
        body(small, feeds, raw_i, sinks, raw_o, own)
        for sink in sinks:
            sink.start()
        for sink in sinks:
            sink.wait()
        for feed in feeds:
            feed.wait()

    vmem = lambda a: pltpu.VMEM(a.shape, a.dtype)
    return pl.pallas_call(
        kernel,
        out_shape=tuple(pltpu.HBM(s.shape, s.dtype) for s in (*outs, *raw_outs)),
        in_specs=[pl.BlockSpec(memory_space=pltpu.SMEM)] * len(smem)
        + [hbm] * (n_i + len(raw_ins))
        + [pl.BlockSpec(memory_space=pltpu.VMEM)] * len(near_ins),
        out_specs=(hbm,) * (n_o + len(raw_outs)),
        scratch_shapes=[vmem(a) for a in ins]
        + [vmem(a) for a in outs]
        + list(scratch)
        + [pltpu.SemaphoreType.DMA((n_i,)), pltpu.SemaphoreType.DMA((n_o,))],
        compiler_params=pltpu.CompilerParams(vmem_limit_bytes=limit * 2**20),
        cost_estimate=pl.CostEstimate(flops=flops, bytes_accessed=nbytes, transcendentals=0),
        name=name,
    )(*smem, *[pltpu.with_memory_space_constraint(a, pltpu.HBM) for a in (*ins, *raw_ins)], *near_ins)


def forward_heads(heads, first, rows_own, qkv, probs, o32, rl, p_buf, p_sem):
    tokens = qkv.shape[1]
    padded = tokens // 4
    lane = lax.broadcasted_iota(jnp.int32, (16, tokens), 1)
    sub = lax.broadcasted_iota(jnp.int32, (16, tokens), 0)
    valid = jnp.zeros((16, tokens), jnp.bool_)
    for j in range(4):
        valid = valid | ((lane >= j * padded) & (lane < j * padded + rows_own))
    top_row = sub == 0
    mask = jnp.where(top_row & ~valid, -1e30, 0.0).astype(BF)
    ones = jnp.where(top_row, 1.0, 0.0).astype(BF)
    half = tokens // 2
    slots = p_buf.shape[0]
    copies = [None] * slots
    step = 0
    for h in range(heads):
        at = 3 * (first + h) * HEAD
        scaled = qkv[at : at + HEAD, :].astype(F32) * (0.125 * LOG2E)
        hi = scaled.astype(BF)
        low = (scaled - hi.astype(F32)).astype(BF)
        q_x = jnp.concatenate((hi, low, ones), axis=0)
        k_h = qkv[at + HEAD : at + 2 * HEAD, :]
        k_f = k_h.astype(F32)
        k_x = jnp.concatenate((k_h, k_h, mask), axis=0)
        v_x = jnp.concatenate((qkv[at + 2 * HEAD : at + 3 * HEAD, :], ones), axis=0)
        bound = jnp.max(jnp.sum(scaled * scaled, axis=0, keepdims=True)) * jnp.max(
            jnp.sum(k_f * k_f, axis=0, keepdims=True)
        )
        small = bound < SAFE
        for part in range(2):
            slot = step % slots
            if copies[slot] is not None:
                copies[slot].wait()

            def block(b, exact, slot=slot, h=h, part=part, q_x=q_x, k_x=k_x, v_x=v_x):
                cols = slice(part * half + b * QB, part * half + (b + 1) * QB)
                scores = mm(q_x[:, cols], k_x, TN)
                if exact:
                    scores = scores - jnp.max(scores, axis=-1, keepdims=True)
                p_block = jnp.exp2(scores).astype(BF)
                p_buf[slot, b * QB : (b + 1) * QB, :] = p_block
                out = mm(v_x, p_block, NT)
                inv = 1.0 / out[HEAD : HEAD + 1, :]
                o32[h * HEAD : (h + 1) * HEAD, cols] = out[:HEAD, :] * inv
                rl[h : h + 1, cols] = inv

            @pl.when(small)
            def _():
                for b in range(half // QB):
                    block(b, False)

            @pl.when(jnp.logical_not(small))
            def _():
                for b in range(half // QB):
                    block(b, True)

            copies[slot] = pltpu.make_async_copy(
                p_buf.at[slot], probs.at[h, part * half : (part + 1) * half, :], p_sem.at[slot]
            )
            copies[slot].start()
            step += 1
    return [c for c in copies if c is not None]


def attend(rows_own, h0, others, params, w_t, b_t):
    padded, width = h0.shape
    tokens = 4 * padded
    rows = w_t.shape[0]
    feat = rows // 3
    heads = feat // HEAD

    def body(_, ins, raw_i, outs, raw_o, own):
        a1, qkv, o32, rl = outs[:4]
        p_buf, p_sem = own
        par = ins[2].wait()
        for pair in range(2):
            for j in (2 * pair, 2 * pair + 1):
                h = ins[0].wait() if j == 0 else raw_i[j - 1]
                normed, _ = norm_rows(h[...].astype(F32))
                a1.ref[j * padded : (j + 1) * padded, :] = (
                    normed * par[0:1, :] + par[1:2, :]
                ).astype(BF)
            cols = slice(2 * pair * padded, 2 * (pair + 1) * padded)
            w_v, b_v = ins[1].wait(), ins[3].wait()
            qkv.ref[:, cols] = (mm(w_v[...], a1.ref[cols, :], NT) + b_v[...]).astype(BF)
        a1.start()
        qkv.start()
        copies = forward_heads(heads, 0, rows_own, qkv.ref, raw_o[0], o32.ref, rl.ref, p_buf, p_sem)
        for j, o in enumerate(outs[4:]):
            o.ref[...] = o32.ref[:, j * padded : (j + 1) * padded].astype(BF)
        for sink in outs:
            sink.start()
        for copy in copies:
            copy.wait()

    return hbm_call(
        "attend", body, (h0, w_t, params, b_t),
        (
            SD((tokens, width), BF), SD((rows, tokens), BF), SD((feat, tokens), F32),
            SD((8, tokens), F32),
        )
        + (SD((feat, padded), BF),) * 4,
        raw_outs=(SD((heads, tokens, tokens), BF),),
        near_ins=others,
        scratch=[pltpu.VMEM((3, tokens // 2, tokens), BF), pltpu.SemaphoreType.DMA((3,))],
        limit=44, flops=12_000_000_000, nbytes=25_000_000,
    )


def own_part(rows_own, groups, sizes, split, side, h0, dy, params, packs, pieces, o_ts):
    hid, feat = sizes
    padded, width = h0.shape
    rows = packs[0].shape[0]
    cut = pieces[0].shape[0]
    half = pieces[1].shape[0]
    a, b = SD((2, hid + split, width), BF), SD((2, hid + feat - split, width), BF)
    blocks = 2
    step = padded // blocks

    def body(smem, ins, raw_i, outs, raw_o, own):
        w_v, w_sem, act_v, du_v, s_sem = own[:5]
        bufs = own[5:]
        o_r = raw_i[8:]
        me = smem[0][0]
        near = pl.multiple_of(cut + me * half, 16)
        far = pl.multiple_of(cut + (1 - me) * half, 16)
        loads = []
        for k, (j, at, num) in enumerate(
            ((0, 0, rows), (1, 0, rows), (2, 0, cut), (2, near, half), (2, far, half),
             (3, 0, cut), (3, near, half), (3, far, half))
        ):
            copy = pltpu.make_async_copy(raw_i[k], w_v.at[j, pl.ds(at, num), :], w_sem.at[k])
            copy.start()
            loads.append(copy)
        out, up = slice(0, feat), slice(feat + EXTRA, feat + EXTRA + hid)
        down = slice(feat + EXTRA + hid, rows)
        par = ins[2].wait()
        attn = par[2:3, :]
        for j, first in enumerate(((0,), (1,), (2, 3, 4), (5, 6, 7))):
            for k in first:
                loads[k].wait()
            attn = attn + mm(o_r[j][...], w_v[j, out, :], TN)
        h1 = ins[0].wait()[...].astype(F32) + attn
        normed, rstd = norm_rows(h1)
        a2 = (normed * par[3:4, :] + par[4:5, :]).astype(BF)
        mixed, dh1, small, db_up = outs[:4]
        dy_b = ins[1].wait()[...]
        acc = [h1[r * step : (r + 1) * step] + par[5:6, :] for r in range(blocks)]
        da2 = [jnp.zeros((step, width), F32) for _ in range(blocks)]
        for j in range(4):
            b_rows = w_v[j, feat : feat + 16, :].astype(F32)
            b_up = (b_rows[0:1] + b_rows[1:2] + b_rows[2:3])[:, :hid]
            db = jnp.zeros((1, hid), F32)
            for r in range(blocks):
                at = slice(r * step, (r + 1) * step)
                value, slope = gelu_parts(mm(a2[at], w_v[j, up, :], NT) + b_up)
                act = value.astype(BF)
                acc[r] = acc[r] + mm(act, w_v[j, down, :], NN)
                du = (mm(dy_b[at], w_v[j, down, :], NT) * slope).astype(BF)
                da2[r] = da2[r] + mm(du, w_v[j, up, :], NN)
                act_v[j, at, :] = act
                du_v[j, at, :] = du
                db = db + jnp.sum(du.astype(F32), axis=0, keepdims=True)
            db_up.ref[j : j + 1, :] = db
        da2 = jnp.concatenate(da2, axis=0)
        dyf = dy_b.astype(F32)
        total = dyf + norm_back(da2, normed, rstd, par[3:4, :])
        dattn = total.astype(BF)
        for j in range(4):
            outs[4 + j].ref[...] = mm(w_v[j, out, :], dattn, NT).astype(BF)
            outs[4 + j].start()
        dh1.ref[...] = total
        dh1.start()
        mixed.ref[...] = jnp.concatenate(acc, axis=0)[:rows_own].astype(BF)
        mixed.start()
        saves = []
        for j in (1, 3, 0, 2):
            d_out = mm(o_r[j][...], dattn, NN).astype(BF)
            a_v, b_v = bufs[j % 2], bufs[2 + j % 2]
            a_v[j // 2, hid:, :] = d_out[:split]
            b_v[j // 2, hid:, :] = d_out[split:]
            a_v[j // 2, :hid, :] = mm(du_v[j], a2, TN).astype(BF)
            b_v[j // 2, :hid, :] = mm(act_v[j], dy_b, TN).astype(BF)
            for k in (j % 2, 2 + j % 2):
                copy = pltpu.make_async_copy(
                    bufs[k].at[j // 2], raw_o[k].at[j // 2], s_sem.at[2 * (k // 2) + 4 * (k % 2) + j // 2]
                )
                copy.start()
                saves.append(copy)
        hot = onehot_rows(ids_of(ins[0].ref, rows_own, padded), groups)
        small.ref[0:groups, :] = onehot_sum(hot, total)
        small.ref[groups : groups + 8, :] = jnp.concatenate(
            (
                jnp.sum(dattn.astype(F32), axis=0, keepdims=True),
                jnp.sum(da2 * normed, axis=0, keepdims=True),
                jnp.sum(da2, axis=0, keepdims=True),
                jnp.sum(dyf, axis=0, keepdims=True),
                jnp.zeros((4, width), F32),
            ),
            axis=0,
        )
        for copy in saves:
            copy.wait()

    return hbm_call(
        "own_part", body, (h0, dy, params),
        (
            SD((rows_own, width), BF), SD((padded, width), F32), SD((groups + 8, width), F32),
            SD((8, hid), F32),
        )
        + (SD((feat, padded), BF),) * 4,
        raw_ins=packs,
        near_ins=(*pieces, *o_ts),
        raw_outs=(a, a, b, b),
        smem=(side,),
        scratch=[
            pltpu.VMEM((4, rows, width), BF), pltpu.SemaphoreType.DMA((8,)),
            pltpu.VMEM((4, padded, hid), BF), pltpu.VMEM((4, padded, hid), BF),
            pltpu.SemaphoreType.DMA((8,)),
        ]
        + [pltpu.VMEM(s.shape, BF) for s in (a, a, b, b)],
        limit=48, flops=10_000_000_000, nbytes=16_000_000,
    )


def mark(value):
    def body(_, ins, raw_i, outs, raw_o, own):
        outs[0].ref[...] = jnp.zeros_like(outs[0].ref)

    (out,) = hbm_call(
        "mark", body, (value[:8, :128].astype(F32),), (SD((8, 128), F32),),
        limit=4, flops=20_000_000_000, nbytes=1_000,
    )
    return out


def back_heads(heads, first, dos, q_v, probs, o32, rl, dqkv, d_s, p_all, p_sem, ready):
    tokens = q_v.shape[1]
    half = tokens // 2

    def fetch(i):
        h, part = divmod(i, 2)
        return pltpu.make_async_copy(
            probs.at[first + h, part * half : (part + 1) * half, :],
            p_all.at[h, part * half : (part + 1) * half, :],
            p_sem.at[i],
        )

    fetches = [fetch(i) for i in range(2 * heads)]
    for f in fetches[:2]:
        f.start()
    ready()
    for f in fetches[2:]:
        f.start()
    d_out = jnp.concatenate([d[...] for d in dos], axis=1)
    sub = lax.broadcasted_iota(jnp.int32, (16, tokens), 0)
    ones = jnp.where(sub < 3, 1.0, 0.0).astype(BF)
    zero = jnp.zeros((13, tokens), F32)
    for h in range(heads):
        at = h * 3 * HEAD
        src = (first + h) * HEAD
        do_s = (d_out[src : src + HEAD, :].astype(F32) * rl[first + h : first + h + 1, :]).astype(BF)
        delta = -jnp.sum(
            do_s.astype(F32) * o32[src : src + HEAD, :], axis=0, keepdims=True
        )
        d_hi = delta.astype(BF).astype(F32)
        d_mid = (delta - d_hi).astype(BF).astype(F32)
        d_low = delta - d_hi - d_mid
        tail = jnp.concatenate((d_hi, d_mid, d_low, zero), axis=0).astype(BF)
        do_x = jnp.concatenate((do_s, tail), axis=0)
        q_h = q_v[at : at + HEAD, :]
        k_h = q_v[at + HEAD : at + 2 * HEAD, :]
        v_x = jnp.concatenate((q_v[at + 2 * HEAD : at + 3 * HEAD, :], ones), axis=0)
        for b in range(tokens // QB):
            cols = slice(b * QB, (b + 1) * QB)
            if b * QB in (0, half):
                fetches[2 * h + b * QB // half].wait()
            dp = mm(do_x[:, cols], v_x, TN)
            ds = (p_all[h, cols, :].astype(F32) * dp).astype(BF)
            d_s[cols, :] = ds
            dqkv[at : at + HEAD, cols] = (0.125 * mm(k_h, ds, NT)).astype(BF)
        dqkv[at + HEAD : at + 2 * HEAD, :] = (0.125 * mm(q_h, d_s[...], NN)).astype(BF)
        dqkv[at + 2 * HEAD : at + 3 * HEAD, :] = mm(do_s, p_all[h], NN).astype(BF)


def back_scratch(heads, tokens):
    return [
        pltpu.VMEM((tokens, tokens), BF),
        pltpu.VMEM((heads, tokens, tokens), BF),
        pltpu.SemaphoreType.DMA((2 * heads,)),
        pltpu.VMEM((3 * heads * HEAD, tokens), BF),
        pltpu.SemaphoreType.DMA((1,)),
    ]


def back_1(heads, dos, a1, qkv, probs, o32, rl):
    tokens, width = a1.shape
    rows = heads * 3 * HEAD

    def body(_, ins, raw_i, outs, raw_o, own):
        d_s, p_all, p_sem, q_v, q_sem = own
        get = pltpu.make_async_copy(raw_i[1].at[:rows, :], q_v, q_sem.at[0])

        def ready():
            get.start()
            for feed in ins[:2]:
                feed.start()
            get.wait()
            for feed in ins[:2]:
                feed.wait()
            ins[2].start()

        dqkv, dw = outs
        back_heads(
            heads, 0, raw_i[2:], q_v, raw_i[0], ins[0].ref, ins[1].ref, dqkv.ref,
            d_s, p_all, p_sem, ready,
        )
        dqkv.start()
        dw.ref[...] = mm(dqkv.ref[...], ins[2].wait()[...], NN).astype(BF)

    return hbm_call(
        "back_1", body, (o32, rl, a1), (SD((rows, tokens), BF), SD((rows, width), BF)),
        raw_ins=(probs, qkv),
        near_ins=dos,
        scratch=back_scratch(heads, tokens),
        limit=48, flops=14_000_000_000, nbytes=18_000_000, eager=False,
    )


def back_2(rows_own, groups, heads, dos, hs, a1, qkv, probs, o32, rl, params, w_t, dqkv_1):
    tokens, width = a1.shape
    padded = hs[0].shape[0]
    cut = dqkv_1.shape[0]
    rows = w_t.shape[0] - cut

    def body(_, ins, raw_i, outs, raw_o, own):
        d_s, p_all, p_sem, q_v, q_sem, dqkv = own
        get = pltpu.make_async_copy(raw_i[1].at[cut:, :], q_v, q_sem.at[0])

        def ready():
            get.start()
            for feed in ins[:2]:
                feed.start()
            get.wait()
            for feed in ins[:2]:
                feed.wait()
            for feed in ins[2:]:
                feed.start()

        back_heads(
            heads, cut // (3 * HEAD), raw_i[2:], q_v, raw_i[0], ins[0].ref,
            ins[1].ref, dqkv, d_s, p_all, p_sem, ready,
        )
        dw, send, keep, small, db = outs
        dw.ref[...] = mm(dqkv[...], ins[2].wait()[...], NN).astype(BF)
        dw.start()
        w_v, d1, par = ins[3].wait(), ins[4].wait(), ins[5].wait()
        ones = jnp.ones((8, tokens), BF)
        db.ref[:, :cut] = mm(ones, d1[...], NT)
        db.ref[:, cut:] = mm(ones, dqkv[...], NT)
        db.start()
        gain = par[0:1, :]
        table = jnp.zeros((groups, width), F32)
        dgain = jnp.zeros((1, width), F32)
        dbias = jnp.zeros((1, width), F32)
        for j in (3, 1, 2, 0):
            at = slice(j * padded, (j + 1) * padded)
            da1 = mm(d1[:, at], w_v[:cut, :], TN) + mm(dqkv[:, at], w_v[cut:, :], TN)
            h = ins[6 + j].wait()
            normed, rstd = norm_rows(h[...].astype(F32))
            back = norm_back(da1, normed, rstd, gain)
            (keep, send)[j % 2].ref[j // 2] = back.astype(BF)
            dgain = dgain + jnp.sum(da1 * normed, axis=0, keepdims=True)
            dbias = dbias + jnp.sum(da1, axis=0, keepdims=True)
            table = table + onehot_sum(onehot_rows(ids_of(h, rows_own, padded), groups), back)
            if j == 1:
                send.start()
        keep.start()
        small.ref[0:groups, :] = table
        small.ref[groups : groups + 8, :] = jnp.concatenate(
            (dgain, dbias, jnp.zeros((6, width), F32)), axis=0
        )

    return hbm_call(
        "back_2", body, (o32, rl, a1, w_t, dqkv_1, params, *hs),
        (
            SD((rows, width), BF), SD((2, padded, width), BF), SD((2, padded, width), BF),
            SD((groups + 8, width), F32), SD((8, w_t.shape[0]), F32),
        ),
        raw_ins=(probs, qkv),
        near_ins=dos,
        scratch=back_scratch(heads, tokens) + [pltpu.VMEM((rows, tokens), BF)],
        limit=48, flops=10_000_000_000, nbytes=18_000_000, eager=False,
    )


def swap(arr, axis, bit):
    size = lax.axis_size(axis)
    return lax.ppermute(arr, axis, [(i, i ^ bit) for i in range(size)])


def add(a, b):
    return (a.astype(F32) + b.astype(F32)).astype(a.dtype)


def after(value, *others):
    return lax.optimization_barrier((value, others))[0]


def side_of(bit):
    return (lax.axis_index("dp") // bit) % 2


def dp_bits():
    bits, bit = [], 1
    while bit < lax.axis_size("dp"):
        bits.append(bit)
        bit *= 2
    return bits


def sync(*values):
    return lax.optimization_barrier(values)


class Sum:
    def __init__(self, arr, bits):
        self.bits = bits[:-1]
        self.rows = arr.shape[-2]
        lead = arr.shape[:-2]
        self.lead = len(lead)
        cuts = (2,) * len(self.bits)
        self.cur = arr.reshape(*lead, *cuts, self.rows // 2 ** len(cuts), arr.shape[-1])

    def axis(self, bit):
        return self.lead + self.bits.index(bit)

    def halve(self, bit):
        axis, side = self.axis(bit), side_of(bit)
        self.kept = lax.dynamic_slice_in_dim(self.cur, side, 1, axis)
        return swap(lax.dynamic_slice_in_dim(self.cur, 1 - side, 1, axis), "dp", bit)

    def halved(self, got):
        self.cur = add(self.kept, got)

    def whole(self, bit):
        return swap(self.cur, "dp", bit)

    def added(self, got):
        self.cur = add(self.cur, got)

    def double(self, bit):
        return swap(self.cur, "dp", bit)

    def doubled(self, bit, got):
        axis = self.axis(bit)
        self.cur = jnp.where(
            side_of(bit) == 0,
            jnp.concatenate((self.cur, got), axis=axis),
            jnp.concatenate((got, self.cur), axis=axis),
        )

    def result(self):
        return self.cur.reshape(self.rows, self.cur.shape[-1])


def per_device(
    block_input, group_ids, intr_table, ln1_gain, ln1_bias, w_qkv, b_qv, w_out, b_out,
    ln2_gain, ln2_bias, w_up, b_up, w_down, b_down, cotangent,
):
    rows_own, width = block_input.shape
    padded = -(-rows_own // 128) * 128
    groups = intr_table.shape[0]
    feat, hid = w_out.shape[0], w_down.shape[0]
    heads = feat // HEAD
    me = lax.axis_index("mp")
    bits = dp_bits()

    onehot = (group_ids[:, None] == jnp.arange(groups, dtype=jnp.int32)[None, :]).astype(BF)
    h0_rows = (
        block_input.astype(F32) + jnp.dot(onehot, intr_table, preferred_element_type=F32)
    ).astype(BF)
    ids_row = jnp.pad(group_ids.astype(BF)[None, :], ((0, 0), (0, width - rows_own)))
    h0 = jnp.concatenate(
        (h0_rows, ids_row, jnp.zeros((padded - rows_own - 1, width), BF)), axis=0
    )
    h_x = swap(h0, "mp", 2)
    h_c = swap(h0, "mp", 1)

    zero_row = jnp.zeros((width,), F32)
    params = jnp.stack(
        (ln1_gain, ln1_bias, b_out, ln2_gain, ln2_bias, b_down, zero_row, zero_row), axis=0
    )
    w_t = (
        w_qkv.reshape(width, 3, heads, HEAD).transpose(2, 1, 3, 0).reshape(3 * feat, width)
    )
    b_three = jnp.stack((b_qv[0], jnp.zeros((feat,), F32), b_qv[1]), axis=0)
    b_t = b_three.reshape(3, heads, HEAD).transpose(1, 0, 2).reshape(3 * feat, 1)

    b_rows = jnp.stack(three_parts(b_up), axis=0)
    pack = jnp.concatenate(
        (w_out, jnp.pad(b_rows, ((0, EXTRA - 3), (0, width - hid))), w_up.T, w_down), axis=0
    )
    side = side_of(1)
    half = pack.shape[0] // 64 * 16
    cut = pack.shape[0] - 2 * half
    pack_c = swap(pack, "mp", 1)
    dy = jnp.pad(cotangent, ((0, padded - rows_own), (0, 0)))
    h_x, params, w_t, b_t, near, whole, dy, _ = sync(
        h_x, params, w_t, b_t,
        lax.dynamic_slice_in_dim(pack, cut + side * half, half, 0), pack[:cut], dy, mark(pack),
    )
    h_xc = swap(h_x, "mp", 1)
    hs = (h0, h_c, h_x, h_xc)
    near, whole = swap(near, "mp", 2), swap(whole, "mp", 2)

    a1, qkv, o32, rl, *o_ts, probs = attend(rows_own, h0, hs[1:], params, w_t, b_t)
    o_own = o_ts[0]
    near = after(near, o_own)
    o_c, o_x, o_xc, far, near_c, whole, _ = sync(
        *(swap(o_ts[j], "mp", j) for j in (1, 2, 3)),
        swap(near, "dp", bits[0]), swap(near, "mp", 1), whole, mark(rl),
    )
    o_ts = (o_own, o_c, o_x, o_xc)
    whole_c, far_c = swap(whole, "mp", 1), swap(far, "mp", 1)
    part = feat // 3
    mixed, dh1, small_own, db_up, *do_ts, keep_a, send_a, keep_b, send_b = own_part(
        rows_own, groups, (hid, feat), part, side.reshape(1), h0, dy, params, (pack, pack_c),
        (whole, near, far, whole_c, near_c, far_c), o_ts,
    )
    do_own = do_ts[0]
    first, full, others = bits[0], bits[-1], bits[1:-1]
    do_c, do_x, do_xc, got_a, got_b, _ = sync(
        *(swap(do_ts[j], "mp", j) for j in (1, 2, 3)), swap(send_a, "mp", 1), swap(send_b, "mp", 1),
        mark(small_own),
    )

    sum_a, sum_b = add(keep_a, got_a), Sum(add(keep_b, got_b), bits)
    got_a, got_b = swap(sum_a[1], "mp", 2), sum_b.halve(first)
    do_own, do_c, do_x, do_xc, kept_a, sum_b.kept = sync(
        do_own, do_c, do_x, do_xc, sum_a[0], sum_b.kept
    )
    do_ts = (do_own, do_c, do_x, do_xc)
    dqkv_1, dw_1 = back_1(heads - 1, do_ts, a1, qkv, probs, o32, rl)
    got_a, got_b, dqkv_1, dw_1 = sync(got_a, got_b, dqkv_1, dw_1)

    sum_a = Sum(add(kept_a, got_a), bits)
    sum_b.halved(got_b)
    got_a, got_b = sum_a.halve(first), sum_b.halve(others[0])
    sum_a.kept, sum_b.kept, dqkv_1 = sync(sum_a.kept, sum_b.kept, dqkv_1)
    dw_2, send, keep, small_att, db = back_2(
        rows_own, groups, 1, do_ts, hs, a1, qkv, probs, o32, rl, params, w_t, dqkv_1
    )
    got_a, got_b, dw_2, send, keep, small_att, db, small_own, db_up, dw_1 = sync(
        got_a, got_b, dw_2, send, keep, small_att, db, small_own, db_up, dw_1
    )
    up_rows = jnp.zeros((4, hid), F32)
    for j in range(4):
        up_rows = lax.dynamic_update_slice(up_rows, db_up[j : j + 1], (me ^ j, 0))
    db_3 = db[0].reshape(heads, 3, HEAD)
    qv_own = jnp.stack((db_3[:, 0].reshape(feat), db_3[:, 2].reshape(feat)), axis=0)[:, None, :]
    qv_rows = lax.dynamic_update_slice(jnp.zeros((2, 4, feat), F32), qv_own, (0, me, 0))
    small = jnp.concatenate(
        (
            small_own[:groups] + small_att[:groups],
            small_own[groups : groups + 4],
            small_att[groups : groups + 2],
            up_rows.reshape(-1, width),
            qv_rows.reshape(-1, width),
        ),
        axis=0,
    )

    sum_a.halved(got_a)
    sum_b.halved(got_b)
    sum_q = Sum(jnp.concatenate((dw_1, dw_2), axis=0), bits)
    got_a, got_x, got_q, got_c, got_s = sync(
        sum_a.halve(others[0]), swap(sum_b.cur[1], "mp", 2), sum_q.halve(first), swap(send, "mp", 1),
        swap(small, "mp", 1),
    )
    sum_a.halved(got_a)
    sum_b.cur = add(sum_b.cur[0], got_x)
    sum_b.lead = 0
    sum_q.halved(got_q)
    total = add(keep, got_c)
    small = small + got_s
    for bit in others[1:]:
        for part_sum in (sum_a, sum_b, sum_q):
            part_sum.halved(part_sum.halve(bit))
    got_a, got_b, got_q, got_x, got_s = sync(
        sum_a.whole(full), sum_b.whole(full), sum_q.halve(others[0]), swap(total[1], "mp", 2),
        swap(small, "mp", 2),
    )
    sum_a.added(got_a)
    sum_b.added(got_b)
    sum_q.halved(got_q)
    dh0 = dh1 + total[0].astype(F32) + got_x.astype(F32)
    input_grad = dh0[:rows_own].astype(BF)
    small = small + got_s
    got_a, got_b, got_q, got_s = sync(
        sum_a.double(first), sum_b.double(others[0]), sum_q.whole(full), swap(small, "dp", first)
    )
    sum_a.doubled(first, got_a)
    sum_b.doubled(others[0], got_b)
    sum_q.added(got_q)
    small = small + got_s
    for bit in others[1:]:
        for part_sum in (sum_a, sum_b, sum_q):
            part_sum.doubled(bit, part_sum.double(bit))
        small = small + swap(small, "dp", bit)
    got_a, got_b, got_q, got_s = sync(
        sum_a.double(others[0]), sum_b.double(first), sum_q.double(first),
        swap(small, "dp", others[0]),
    )
    sum_a.doubled(others[0], got_a)
    sum_b.doubled(first, got_b)
    sum_q.doubled(first, got_q)
    small = small + got_s
    got_q, got_s = sync(sum_q.double(others[0]), swap(small, "dp", full))
    sum_q.doubled(others[0], got_q)
    small = small + got_s
    g_a, g_b, g_qkv = sum_a.result(), sum_b.result(), sum_q.result()
    at = groups
    up_at = at + 6
    qv_at = up_at + 4 * hid // width
    b_up_grad = lax.dynamic_slice(small[up_at:qv_at].reshape(4, hid), (me, 0), (1, hid))[0]
    b_qv_grad = lax.dynamic_slice(
        small[qv_at:].reshape(2, 4, feat), (0, me, 0), (2, 1, feat)
    ).reshape(2, feat)
    g_qkv = g_qkv.astype(F32)
    w_qkv_grad = (
        g_qkv.reshape(heads, 3, HEAD, width).transpose(3, 1, 0, 2).reshape(width, 3, feat)
    )
    return (
        mixed,
        input_grad,
        small[:groups],
        small[at + 4],
        small[at + 5],
        w_qkv_grad,
        b_qv_grad,
        jnp.concatenate((g_a[hid:], g_b[hid:]), axis=0).astype(F32),
        small[at],
        small[at + 1],
        small[at + 2],
        g_a[:hid].astype(F32).T,
        b_up_grad,
        g_b[:hid].astype(F32),
        small[at + 3],
    )


def solution(mesh):
    rows = P(("dp", "mp"), None)
    return jax.shard_map(
        per_device,
        mesh=mesh,
        in_specs=(
            rows, P(("dp", "mp")), P(), P(), P(), P(None, None, "mp"), P(None, "mp"), P("mp", None),
            P(), P(), P(), P(None, "mp"), P("mp"), P("mp", None), P(), rows,
        ),
        out_specs=(
            rows, rows, P(), P(), P(), P(None, None, "mp"), P(None, "mp"), P("mp", None),
            P(), P(), P(), P(None, "mp"), P("mp"), P("mp", None), P(),
        ),
        check_vma=False,
    )
```

```python
import jax
import jax.numpy as jnp
from jax import lax
from jax.experimental import pallas as pl
from jax.experimental.pallas import tpu as pltpu
from jax.sharding import PartitionSpec as P

HEAD = 64
BF = jnp.bfloat16
F32 = jnp.float32
LOG2E = 1.4426950408889634
NN = (((1,), (0,)), ((), ()))
NT = (((1,), (1,)), ((), ()))
TN = (((0,), (0,)), ((), ()))
QB = 256
SD = jax.ShapeDtypeStruct
SAFE = 3000.0
EXTRA = 32


def mm(a, b, dims):
    return lax.dot_general(a, b, dims, preferred_element_type=F32)


def three_parts(v):
    hi = v.astype(BF)
    rest = v - hi.astype(F32)
    mid = rest.astype(BF)
    low = (rest - mid.astype(F32)).astype(BF)
    return hi, mid, low


def two_parts(v):
    hi = v.astype(BF)
    return jnp.concatenate((hi, (v - hi.astype(F32)).astype(BF)), axis=0)


def joined(parts):
    n = parts.shape[0] // 2
    return parts[:n].astype(F32) + parts[n:].astype(F32)


def norm_rows(rows):
    centre = rows - jnp.mean(rows, axis=-1, keepdims=True)
    var = jnp.mean(centre * centre, axis=-1, keepdims=True)
    rstd = lax.rsqrt(var + 1e-05)
    return centre * rstd, rstd


def norm_back(grad, normed, rstd, gain):
    scaled = grad * gain
    return rstd * (
        scaled
        - jnp.mean(scaled, axis=-1, keepdims=True)
        - normed * jnp.mean(scaled * normed, axis=-1, keepdims=True)
    )


def gelu_parts(u):
    square = u * u
    t = jnp.tanh(0.7978845608028654 * (u + 0.044715 * (u * square)))
    half = 0.5 * (1.0 + t)
    slope = half + 0.5 * u * (1.0 - t * t) * (
        0.7978845608028654 + (3 * 0.044715 * 0.7978845608028654) * square
    )
    return u * half, slope


def onehot_rows(ids_row, groups):
    levels = lax.broadcasted_iota(jnp.int32, (groups, ids_row.shape[1]), 0).astype(F32)
    return (levels == ids_row).astype(F32).astype(BF)


def onehot_sum(hot, rows):
    hi = rows.astype(BF)
    low = (rows - hi.astype(F32)).astype(BF)
    return mm(hot, hi, NN) + mm(hot, low, NN)


class Copy:
    def __init__(self, src, dst, sem, near):
        self.copy = pltpu.make_async_copy(src, dst, sem)
        self.ref = near
        self.begun = False
        self.ended = False

    def start(self):
        if not self.begun:
            self.begun = True
            self.copy.start()
        return self

    def wait(self):
        self.start()
        if not self.ended:
            self.ended = True
            self.copy.wait()
        return self.ref


def hbm_call(
    name, body, ins, outs, *, raw_ins=(), raw_outs=(), near_ins=(), near_outs=(), smem=(), scratch=(),
    limit, flops, nbytes, eager=True,
):
    hbm = pl.BlockSpec(memory_space=pltpu.HBM)
    n_i, n_o = len(ins), len(outs)

    def kernel(*refs):
        rest = list(refs)

        def take(n):
            got = rest[:n]
            del rest[:n]
            return got

        small = take(len(smem))
        far_i, raw_i = take(n_i), take(len(raw_ins))
        raw_i = raw_i + take(len(near_ins))
        far_o, raw_o = take(n_o), take(len(raw_outs) + len(near_outs))
        near_i, near_o = take(n_i), take(n_o)
        own = take(len(scratch))
        sem_i, sem_o = take(2)
        feeds = [Copy(f, n, sem_i.at[k], n) for k, (f, n) in enumerate(zip(far_i, near_i))]
        sinks = [Copy(n, f, sem_o.at[k], n) for k, (f, n) in enumerate(zip(far_o, near_o))]
        if eager:
            for feed in feeds:
                feed.start()
        body(small, feeds, raw_i, sinks, raw_o, own)
        for sink in sinks:
            sink.start()
        for sink in sinks:
            sink.wait()
        for feed in feeds:
            feed.wait()

    vmem = lambda a: pltpu.VMEM(a.shape, a.dtype)
    return pl.pallas_call(
        kernel,
        out_shape=tuple(pltpu.HBM(s.shape, s.dtype) for s in (*outs, *raw_outs)) + tuple(near_outs),
        in_specs=[pl.BlockSpec(memory_space=pltpu.SMEM)] * len(smem)
        + [hbm] * (n_i + len(raw_ins))
        + [pl.BlockSpec(memory_space=pltpu.VMEM)] * len(near_ins),
        out_specs=(hbm,) * (n_o + len(raw_outs))
        + (pl.BlockSpec(memory_space=pltpu.VMEM),) * len(near_outs),
        scratch_shapes=[vmem(a) for a in ins]
        + [vmem(a) for a in outs]
        + list(scratch)
        + [pltpu.SemaphoreType.DMA((n_i,)), pltpu.SemaphoreType.DMA((max(n_o, 1),))],
        compiler_params=pltpu.CompilerParams(vmem_limit_bytes=limit * 2**20),
        cost_estimate=pl.CostEstimate(flops=flops, bytes_accessed=nbytes, transcendentals=0),
        name=name,
    )(*smem, *[pltpu.with_memory_space_constraint(a, pltpu.HBM) for a in (*ins, *raw_ins)], *near_ins)


def forward_heads(heads, first, rows_own, qkv, probs, o32, rl, p_buf, p_sem):
    tokens = qkv.shape[1]
    padded = tokens // 4
    lane = lax.broadcasted_iota(jnp.int32, (16, tokens), 1)
    sub = lax.broadcasted_iota(jnp.int32, (16, tokens), 0)
    valid = jnp.zeros((16, tokens), jnp.bool_)
    for j in range(4):
        valid = valid | ((lane >= j * padded) & (lane < j * padded + rows_own))
    top_row = sub == 0
    mask = jnp.where(top_row & ~valid, -1e30, 0.0).astype(BF)
    ones = jnp.where(top_row, 1.0, 0.0).astype(BF)
    parts = []
    bound = jnp.float32(0.0)
    for h in range(heads):
        at = 3 * (first + h) * HEAD
        scaled = qkv[at : at + HEAD, :].astype(F32) * (0.125 * LOG2E)
        hi = scaled.astype(BF)
        low = (scaled - hi.astype(F32)).astype(BF)
        k_h = qkv[at + HEAD : at + 2 * HEAD, :]
        k_f = k_h.astype(F32)
        q_x = jnp.concatenate((hi, low, ones), axis=0)
        k_x = jnp.concatenate((k_h, k_h, mask), axis=0)
        v_x = jnp.concatenate((qkv[at + 2 * HEAD : at + 3 * HEAD, :], ones), axis=0)
        parts.append((q_x, k_x, v_x))
        bound = jnp.maximum(
            bound,
            jnp.max(jnp.sum(scaled * scaled, axis=0, keepdims=True))
            * jnp.max(jnp.sum(k_f * k_f, axis=0, keepdims=True)),
        )
    copies = [
        pltpu.make_async_copy(p_buf.at[h], probs.at[h], p_sem.at[h]) for h in range(heads)
    ]

    def run(exact):
        for h, (q_x, k_x, v_x) in enumerate(parts):
            for b in range(tokens // QB):
                cols = slice(b * QB, (b + 1) * QB)
                scores = mm(q_x[:, cols], k_x, TN)
                if exact:
                    scores = scores - jnp.max(scores, axis=-1, keepdims=True)
                p_block = jnp.exp2(scores).astype(BF)
                p_buf[h, cols, :] = p_block
                out = mm(v_x, p_block, NT)
                inv = 1.0 / out[HEAD : HEAD + 1, :]
                o32[h * HEAD : (h + 1) * HEAD, cols] = out[:HEAD, :] * inv
                rl[h : h + 1, cols] = inv
            copies[h].start()

    small = bound < SAFE

    @pl.when(small)
    def _():
        run(False)

    @pl.when(jnp.logical_not(small))
    def _():
        run(True)

    return copies


def attend(padded, x0, others, ids, table, params, w_t):
    rows_own, width = x0.shape
    tokens = 4 * padded
    rows = w_t.shape[0]
    feat = rows // 3
    heads = feat // HEAD
    groups = table.shape[0]

    def body(_, ins, raw_i, outs, raw_o, own):
        a1, qkv, h_all, o32, rl = outs[:5]
        p_buf, p_sem, x_v = own
        par = ins[2].wait()
        bias = jnp.transpose(par[...])[:rows, 6:7]
        table_v = ins[3].wait()[...]
        for pair in range(2):
            for j in (2 * pair, 2 * pair + 1):
                at = slice(j * padded, (j + 1) * padded)
                x = ins[0].wait() if j == 0 else raw_i[j - 1]
                x_v[j, padded - 16 :, :] = jnp.zeros((16, width), F32)
                x_v[j, :rows_own, :] = x[...].astype(F32)
                hot = onehot_rows(raw_i[3 + j][0:1, :], groups)
                h = (x_v[j] + mm(hot, table_v, TN)).astype(BF)
                h_all.ref[at, :] = h
                normed, _ = norm_rows(h.astype(F32))
                a1.ref[at, :] = (normed * par[0:1, :] + par[1:2, :]).astype(BF)
            cols = slice(2 * pair * padded, 2 * (pair + 1) * padded)
            qkv.ref[:, cols] = (mm(ins[1].wait()[...], a1.ref[cols, :], NT) + bias).astype(BF)
        for sink in (a1, qkv, h_all):
            sink.start()
        copies = forward_heads(heads, 0, rows_own, qkv.ref, raw_o[0], o32.ref, rl.ref, p_buf, p_sem)
        for j in range(4):
            o = o32.ref[:, j * padded : (j + 1) * padded].astype(BF)
            if j < 2:
                outs[5 + j].ref[...] = o
            else:
                outs[7].ref[j - 2] = o
        for sink in outs:
            sink.start()
        for copy in copies:
            copy.wait()

    return hbm_call(
        "attend", body, (x0, w_t, params, table),
        (
            SD((tokens, width), BF), SD((rows, tokens), BF), SD((tokens, width), BF),
            SD((feat, tokens), F32), SD((8, tokens), F32), SD((feat, padded), BF),
            SD((feat, padded), BF), SD((2, feat, padded), BF),
        ),
        raw_outs=(SD((heads, tokens, tokens), BF),),
        near_ins=(*others, *ids),
        scratch=[
            pltpu.VMEM((heads, tokens, tokens), BF), pltpu.SemaphoreType.DMA((heads,)),
            pltpu.VMEM((4, padded, width), F32),
        ],
        limit=40, flops=12_000_000_000, nbytes=25_000_000,
    )


def own_part(rows_own, groups, sizes, split, sides, h_all, ids, dy, params, packs, pieces, o_ts):
    hid, feat = sizes
    padded, width = dy.shape
    rows = packs[0].shape[0]
    half = hid // 2
    a, b = SD((2, hid + split, width), BF), SD((2, hid + feat - split, width), BF)
    blocks = 2
    step = padded // blocks

    def body(smem, ins, raw_i, outs, raw_o, own):
        w_v, w_sem, act_v, du_v, h_v, h_sem = own
        bufs = (raw_o[0], raw_o[1], raw_o[2], raw_o[3])
        get_h = pltpu.make_async_copy(raw_i[0].at[:padded, :], h_v, h_sem.at[0])
        get_h.start()
        raw_i = raw_i[1:]
        o_r, ids_r = raw_i[12:16], raw_i[16]
        up_at, down_at = feat + EXTRA, feat + EXTRA + hid
        ends = [
            (pl.multiple_of(at + s * half, 16), pl.multiple_of(at + (1 - s) * half, 16))
            for at, s in ((up_at, smem[0][0]), (down_at, smem[0][1]))
        ]
        places = [(0, 0, rows), (1, 0, rows)]
        for j in (2, 3):
            places += [(j, 0, up_at)] + [(j, at, half) for pair in ends for at in pair]
        loads = []
        for k, (j, at, num) in enumerate(places):
            copy = pltpu.make_async_copy(raw_i[k], w_v.at[j, pl.ds(at, num), :], w_sem.at[k])
            copy.start()
            loads.append(copy)
        out, up = slice(0, feat), slice(up_at, down_at)
        down = slice(down_at, rows)
        par = ins[1].wait()
        attn = par[2:3, :]
        for copy in loads:
            copy.wait()
        for j in range(4):
            attn = attn + mm(o_r[j][...], w_v[j, out, :], TN)
        get_h.wait()
        h1 = h_v[...].astype(F32) + attn
        normed, rstd = norm_rows(h1)
        a2 = (normed * par[3:4, :] + par[4:5, :]).astype(BF)
        mixed, dh1, small, db_up = outs[:4]
        dy_b = ins[0].wait()[...]
        acc = [h1[r * step : (r + 1) * step] + par[5:6, :] for r in range(blocks)]
        da2 = [jnp.zeros((step, width), F32) for _ in range(blocks)]
        parts = [slice(r * step, (r + 1) * step) for r in range(blocks)]

        def shard_grads(j):
            for k, left, right in ((j % 2, du_v, a2), (2 + j % 2, act_v, dy_b)):
                bufs[k][j // 2, :hid, :] = mm(left[j], right, TN).astype(BF)

        for n, j in enumerate((1, 3, 0, 2)):
            b_rows = w_v[j, feat : feat + 16, :].astype(F32)
            b_up = (b_rows[0:1] + b_rows[1:2] + b_rows[2:3])[:, :hid]
            us = [mm(a2[at], w_v[j, up, :], NT) + b_up for at in parts]
            dacts = [mm(dy_b[at], w_v[j, down, :], NT) for at in parts]
            if n:
                shard_grads((1, 3, 0)[n - 1])
            db = jnp.zeros((1, hid), F32)
            for r, at in enumerate(parts):
                value, slope = gelu_parts(us[r])
                act = value.astype(BF)
                acc[r] = acc[r] + mm(act, w_v[j, down, :], NN)
                du = (dacts[r] * slope).astype(BF)
                da2[r] = da2[r] + mm(du, w_v[j, up, :], NN)
                act_v[j, at, :] = act
                du_v[j, at, :] = du
                db = db + jnp.sum(du.astype(F32), axis=0, keepdims=True)
            db_up.ref[j : j + 1, :] = db
        shard_grads(2)
        da2 = jnp.concatenate(da2, axis=0)
        dyf = dy_b.astype(F32)
        total = dyf + norm_back(da2, normed, rstd, par[3:4, :])
        dattn = total.astype(BF)
        for j in range(4):
            outs[4 + j].ref[...] = mm(w_v[j, out, :], dattn, NT).astype(BF)
            outs[4 + j].start()
        dh1.ref[...] = total
        dh1.start()
        mixed.ref[...] = jnp.concatenate(acc, axis=0)[:rows_own].astype(BF)
        mixed.start()
        for j in (1, 3, 0, 2):
            d_out = mm(o_r[j][...], dattn, NN).astype(BF)
            bufs[j % 2][j // 2, hid:, :] = d_out[:split]
            bufs[2 + j % 2][j // 2, hid:, :] = d_out[split:]
        hot = onehot_rows(ids_r[0:1, :], groups)
        small.ref[0:groups, :] = onehot_sum(hot, total)
        small.ref[groups : groups + 8, :] = jnp.concatenate(
            (
                jnp.sum(dattn.astype(F32), axis=0, keepdims=True),
                jnp.sum(da2 * normed, axis=0, keepdims=True),
                jnp.sum(da2, axis=0, keepdims=True),
                jnp.sum(dyf, axis=0, keepdims=True),
                jnp.zeros((4, width), F32),
            ),
            axis=0,
        )
    return hbm_call(
        "own_part", body, (dy, params),
        (
            SD((rows_own, width), BF), SD((padded, width), F32), SD((groups + 8, width), F32),
            SD((8, hid), F32),
        )
        + (SD((feat, padded), BF),) * 4,
        raw_ins=(h_all, *packs),
        near_ins=(*pieces, *o_ts, ids),
        near_outs=(a, a, b, b),
        smem=(sides,),
        scratch=[
            pltpu.VMEM((4, rows, width), BF), pltpu.SemaphoreType.DMA((12,)),
            pltpu.VMEM((4, padded, hid), BF), pltpu.VMEM((4, padded, hid), BF),
            pltpu.VMEM((padded, width), BF), pltpu.SemaphoreType.DMA((1,)),
        ],
        limit=40, flops=10_000_000_000, nbytes=16_000_000,
    )


def mark(value):
    def body(_, ins, raw_i, outs, raw_o, own):
        outs[0].ref[...] = jnp.zeros_like(outs[0].ref)

    (out,) = hbm_call(
        "mark", body, (value[:8, :128].astype(F32),), (SD((8, 128), F32),),
        limit=4, flops=20_000_000_000, nbytes=1_000,
    )
    return out


def back_heads(heads, first, dos, q_v, probs, o32, rl, dqkv, d_s, p_all, p_sem, ready, late):
    tokens = q_v.shape[1]
    spans = [(h, at) for h in range(heads) for at in ((slice(0, tokens),) if h == 0 else (slice(0, tokens),))]
    fetches = [
        pltpu.make_async_copy(probs.at[first + h, at, :], p_all.at[h, at, :], p_sem.at[i])
        for i, (h, at) in enumerate(spans)
    ]
    begins = {(h, at.start): f for (h, at), f in zip(spans, fetches)}
    fetches[0].start()
    ready(lambda: [f.start() for f in fetches[1:]])
    d_out = jnp.concatenate([d[...] for d in dos], axis=1)
    sub = lax.broadcasted_iota(jnp.int32, (16, tokens), 0)
    ones = jnp.where(sub < 3, 1.0, 0.0).astype(BF)
    zero = jnp.zeros((13, tokens), F32)
    for h in range(heads):
        at = h * 3 * HEAD
        src = (first + h) * HEAD
        do_s = (d_out[src : src + HEAD, :].astype(F32) * rl[first + h : first + h + 1, :]).astype(BF)
        delta = -jnp.sum(
            do_s.astype(F32) * o32[h * HEAD : (h + 1) * HEAD, :], axis=0, keepdims=True
        )
        d_hi = delta.astype(BF).astype(F32)
        d_mid = (delta - d_hi).astype(BF).astype(F32)
        d_low = delta - d_hi - d_mid
        tail = jnp.concatenate((d_hi, d_mid, d_low, zero), axis=0).astype(BF)
        do_x = jnp.concatenate((do_s, tail), axis=0)
        q_h = q_v[at : at + HEAD, :]
        k_h = q_v[at + HEAD : at + 2 * HEAD, :]
        v_x = jnp.concatenate((q_v[at + 2 * HEAD : at + 3 * HEAD, :], ones), axis=0)
        for b in range(tokens // QB):
            cols = slice(b * QB, (b + 1) * QB)
            if (h, b * QB) in begins:
                begins[h, b * QB].wait()
                if h == 0:
                    late()
            dp = mm(do_x[:, cols], v_x, TN)
            ds = (p_all[h, cols, :].astype(F32) * dp).astype(BF)
            d_s[cols, :] = ds
            dqkv[at : at + HEAD, cols] = (0.125 * mm(k_h, ds, NT)).astype(BF)
        dqkv[at + HEAD : at + 2 * HEAD, :] = (0.125 * mm(q_h, d_s[...], NN)).astype(BF)
        dqkv[at + 2 * HEAD : at + 3 * HEAD, :] = mm(do_s, p_all[h], NN).astype(BF)


def back_scratch(heads, tokens):
    return [
        pltpu.VMEM((tokens, tokens), BF),
        pltpu.VMEM((heads, tokens, tokens), BF),
        pltpu.SemaphoreType.DMA((heads + 1,)),
        pltpu.VMEM((3 * heads * HEAD, tokens), BF),
        pltpu.SemaphoreType.DMA((2,)),
        pltpu.VMEM((heads * HEAD, tokens), F32),
    ]


def back_1(heads, dos, a1, qkv, probs, o32, rl):
    tokens, width = a1.shape
    rows = heads * 3 * HEAD

    def body(_, ins, raw_i, outs, raw_o, own):
        d_s, p_all, p_sem, q_v, q_sem, o_v = own
        gets = (
            pltpu.make_async_copy(raw_i[1].at[:rows, :], q_v, q_sem.at[0]),
            pltpu.make_async_copy(raw_i[2].at[: heads * HEAD, :], o_v, q_sem.at[1]),
        )

        def ready(more):
            ins[0].start()
            for get in gets:
                get.start()
            more()
            ins[0].wait()
            for get in gets:
                get.wait()

        dqkv, dw = outs[0], raw_o[0]
        back_heads(
            heads, 0, raw_i[3:], q_v, raw_i[0], o_v, ins[0].ref, dqkv.ref, d_s, p_all, p_sem, ready,
            ins[1].start,
        )
        dqkv.start()
        dw[...] = mm(dqkv.ref[...], ins[1].wait()[...], NN).astype(BF)

    return hbm_call(
        "back_1", body, (rl, a1), (SD((rows, tokens), BF),),
        near_outs=(SD((rows, width), BF),),
        raw_ins=(probs, qkv, o32),
        near_ins=dos,
        scratch=back_scratch(heads, tokens),
        limit=40, flops=14_000_000_000, nbytes=18_000_000, eager=False,
    )


def back_2(me, groups, heads, dos, ids, h_all, a1, qkv, probs, o32, rl, params, w_t, dqkv_1, small_own, db_up):
    tokens, width = a1.shape
    padded = tokens // 4
    cut = dqkv_1.shape[0]
    rows = w_t.shape[0] - cut

    def body(smem, ins, raw_i, outs, raw_o, own):
        d_s, p_all, p_sem, q_v, q_sem, o_v, dqkv, small = own
        gets = (
            pltpu.make_async_copy(raw_i[1].at[cut:, :], q_v, q_sem.at[0]),
            pltpu.make_async_copy(raw_i[2].at[cut // 3 :, :], o_v, q_sem.at[1]),
        )

        def ready(more):
            ins[0].start()
            for get in gets:
                get.start()
            more()
            ins[0].wait()
            for get in gets:
                get.wait()

        back_heads(
            heads, cut // (3 * HEAD), raw_i[3:7], q_v, raw_i[0], o_v, ins[0].ref, dqkv,
            d_s, p_all, p_sem, ready, lambda: [feed.start() for feed in ins[1:]],
        )
        dw, send, keep = raw_o
        shard = smem[0][0]
        dw[...] = mm(dqkv[...], ins[1].wait()[...], NN).astype(BF)
        w_v, d1, par = ins[2].wait(), ins[3].wait(), ins[4].wait()
        ones = jnp.ones((8, tokens), BF)
        small[groups + 8 :, :] = jnp.zeros((8, width), F32)
        db = jnp.concatenate((mm(ones, d1[...], NT)[0:1], mm(ones, dqkv[...], NT)[0:1]), axis=1)
        small[pl.ds(groups + 8 + shard, 1), : cut + rows] = db
        hid = ins[7].ref.shape[1]
        up_v = ins[7].wait()
        for s in range(4):
            at = s * hid
            small[
                groups + 6 + at // width : groups + 7 + at // width, at % width : at % width + hid
            ] = up_v[pl.ds(jnp.bitwise_xor(shard, s), 1), :]
        gain = par[0:1, :]
        table = jnp.zeros((groups, width), F32)
        dgain = jnp.zeros((1, width), F32)
        dbias = jnp.zeros((1, width), F32)
        order = (3, 1, 2, 0)

        def product(j):
            at = slice(j * padded, (j + 1) * padded)
            return mm(d1[:, at], w_v[:cut, :], TN) + mm(dqkv[:, at], w_v[cut:, :], TN)

        da1 = product(order[0])
        for n, j in enumerate(order):
            later = product(order[n + 1]) if n < 3 else None
            at = slice(j * padded, (j + 1) * padded)
            normed, rstd = norm_rows(ins[5].wait()[at, :].astype(F32))
            back = norm_back(da1, normed, rstd, gain)
            (keep, send)[j % 2][j // 2 * padded : (j // 2 + 1) * padded, :] = back.astype(BF)
            dgain = dgain + jnp.sum(da1 * normed, axis=0, keepdims=True)
            dbias = dbias + jnp.sum(da1, axis=0, keepdims=True)
            table = table + onehot_sum(onehot_rows(raw_i[7 + j][0:1, :], groups), back)
            da1 = later
        first = ins[6].wait()
        small[0:groups, :] = table + first[0:groups, :]
        small[groups : groups + 4, :] = first[groups : groups + 4, :]
        small[groups + 4 : groups + 6, :] = jnp.concatenate((dgain, dbias), axis=0)
        both = two_parts(small[...])
        keep[2 * padded :, :] = both
        send[2 * padded :, :] = both

    return hbm_call(
        "back_2", body, (rl, a1, w_t, dqkv_1, params, h_all, small_own, db_up), (),
        near_outs=(
            SD((rows, width), BF), SD((2 * padded + 2 * groups + 32, width), BF),
            SD((2 * padded + 2 * groups + 32, width), BF),
        ),
        smem=(me,),
        raw_ins=(probs, qkv, o32),
        near_ins=(*dos, *ids),
        scratch=back_scratch(heads, tokens)
        + [pltpu.VMEM((rows, tokens), BF), pltpu.VMEM((groups + 16, width), F32)],
        limit=40, flops=10_000_000_000, nbytes=18_000_000, eager=False,
    )


def swap(arr, axis, bit):
    size = lax.axis_size(axis)
    return lax.ppermute(arr, axis, [(i, i ^ bit) for i in range(size)])


def add(a, b):
    return (a.astype(F32) + b.astype(F32)).astype(a.dtype)


def after(value, *others):
    return lax.optimization_barrier((value, others))[0]


def side_of(bit):
    return (lax.axis_index("dp") // bit) % 2


def dp_bits():
    bits, bit = [], 1
    while bit < lax.axis_size("dp"):
        bits.append(bit)
        bit *= 2
    return bits


def sync(*values):
    return lax.optimization_barrier(values)


def plus(a, b):
    return (a.astype(F32) + b.astype(F32)).astype(BF)


def stage(name, sides, ins, outs, body):
    near = pl.BlockSpec(memory_space=pltpu.VMEM)

    def kernel(side, *refs):
        body(side[0], side[1], refs[: len(ins)], refs[len(ins) :])

    return pl.pallas_call(
        kernel,
        out_shape=tuple(SD(shape, dtype) for shape, dtype in outs),
        in_specs=[pl.BlockSpec(memory_space=pltpu.SMEM)] + [near] * len(ins),
        out_specs=(near,) * len(outs),
        compiler_params=pltpu.CompilerParams(vmem_limit_bytes=16 * 2**20),
        name=name,
    )(sides, *ins)


def per_device(
    block_input, group_ids, intr_table, ln1_gain, ln1_bias, w_qkv, b_qv, w_out, b_out,
    ln2_gain, ln2_bias, w_up, b_up, w_down, b_down, cotangent,
):
    rows_own, width = block_input.shape
    padded = -(-rows_own // 128) * 128
    groups = intr_table.shape[0]
    feat, hid = w_out.shape[0], w_down.shape[0]
    heads = feat // HEAD
    me = lax.axis_index("mp")
    bits = dp_bits()

    id_row = jnp.pad(group_ids.astype(F32)[None, :], ((0, 7), (0, padded - rows_own)), constant_values=-1)
    x_x = swap(block_input, "mp", 2)
    x_c = swap(block_input, "mp", 1)
    ids_x = swap(id_row, "mp", 2)
    ids_c = swap(id_row, "mp", 1)

    zero_row = jnp.zeros((width,), F32)
    b_three = jnp.stack((b_qv[0], jnp.zeros((feat,), F32), b_qv[1]), axis=0)
    b_row = b_three.reshape(3, heads, HEAD).transpose(1, 0, 2).reshape(3 * feat)
    params = jnp.stack(
        (
            ln1_gain, ln1_bias, b_out, ln2_gain, ln2_bias, b_down,
            jnp.pad(b_row, (0, width - 3 * feat)), zero_row,
        ),
        axis=0,
    )
    w_t = (
        w_qkv.reshape(width, 3, heads, HEAD).transpose(2, 1, 3, 0).reshape(3 * feat, width)
    )
    b_rows = jnp.stack(three_parts(b_up), axis=0)
    pack = jnp.concatenate(
        (w_out, jnp.pad(b_rows, ((0, EXTRA - 3), (0, width - hid))), w_up.T, w_down), axis=0
    )
    up_at, down_at, half = feat + EXTRA, feat + EXTRA + hid, hid // 2
    side_u, side_d = side_of(bits[0]), side_of(bits[1])
    sides = jnp.stack((side_u, side_d))
    dy = jnp.pad(cotangent, ((0, padded - rows_own), (0, 0)))
    x_x, ids_x, first_rows, params, w_t, up_near, down_near, dy, _ = sync(
        x_x, ids_x, pack[:up_at], params, w_t,
        lax.dynamic_slice_in_dim(pack, up_at + side_u * half, half, 0),
        lax.dynamic_slice_in_dim(pack, down_at + side_d * half, half, 0), dy, mark(pack),
    )
    x_xc, ids_xc = swap(x_x, "mp", 1), swap(ids_x, "mp", 1)
    up_near, down_near = swap(up_near, "mp", 2), swap(down_near, "mp", 2)
    out_x = swap(first_rows, "mp", 2)
    pack_c = swap(after(pack, x_x), "mp", 1)
    ids = (id_row, ids_c, ids_x, ids_xc)
    a1, qkv, h_all, o32, rl, *o_ts, probs = attend(
        padded, block_input, (x_c, x_x, x_xc), ids, intr_table, params, w_t
    )

    o_own, o_c, o_two = o_ts
    up_near, down_near, out_x, o_own = sync(up_near, down_near, out_x, o_own)
    o_c, o_two, up_far, down_far, _ = sync(
        swap(o_c, "mp", 1), swap(o_two, "mp", 2),
        swap(up_near, "dp", bits[0]), swap(down_near, "dp", bits[1]), mark(rl),
    )
    o_ts = (o_own, o_c, o_two[0], swap(o_two[1], "mp", 1))
    pieces = (out_x, up_near, up_far, down_near, down_far)
    pieces = pieces + tuple(swap(p, "mp", 1) for p in pieces)
    part = feat // 2
    mixed, dh1, small_own, db_up, *do_ts, keep_a, send_a, keep_b, send_b = own_part(
        rows_own, groups, (hid, feat), part, sides, h_all, id_row, dy, params,
        (pack, pack_c), pieces, o_ts,
    )
    do_own = do_ts[0]
    first, second, full, *rest = bits
    do_c, do_x, do_xc, got_a, got_b, _ = sync(
        *(swap(do_ts[j], "mp", j) for j in (1, 2, 3)), swap(send_a, "mp", 1), swap(send_b, "mp", 1),
        mark(small_own),
    )

    w = width
    n_a, n_b, n_q, n_r = (hid + part) // 4, (hid + feat - part) // 4, 3 * feat * 2 // 3 // 4, feat // 4

    def stage_0(u, d, ins, outs):
        keep_a, got_a, keep_b, got_b = ins
        a_sent, a_kept, b_sent, b_kept = outs
        a_sent[...] = plus(keep_a[1], got_a[1])
        a_kept[...] = plus(keep_a[0], got_a[0])
        for out, at in ((b_sent, pl.ds(1 - u, 1)), (b_kept, pl.ds(u, 1))):
            out[...] = plus(keep_b[:, at], got_b[:, at])

    cut_b = (2, 2, 2, n_b, w)
    a_sent, a_kept, b_sent, b_kept = stage(
        "stage_0", sides, (keep_a, got_a, keep_b.reshape(cut_b), got_b.reshape(cut_b)),
        [((4 * n_a, w), BF)] * 2 + [((2, 1, 2, n_b, w), BF)] * 2, stage_0,
    )
    a_got, b_got = swap(a_sent, "mp", 2), swap(b_sent, "dp", first)
    do_own, do_c, do_x, do_xc, a_kept, b_kept = sync(do_own, do_c, do_x, do_xc, a_kept, b_kept)
    do_ts = (do_own, do_c, do_x, do_xc)
    dqkv_1, dw_1 = back_1(heads - 1, do_ts, a1, qkv, probs, o32, rl)

    def stage_1(u, d, ins, outs):
        a_kept, a_got, b_kept, b_got, q = ins
        for k, at in enumerate((pl.ds(1 - u, 1), pl.ds(u, 1))):
            outs[k][...] = plus(a_kept[at], a_got[at])
            outs[4 + k][...] = q[at]
        for k, at in enumerate((pl.ds(1 - d, 1), pl.ds(d, 1))):
            outs[2 + k][...] = plus(b_kept[:, :, at], b_got[:, :, at])

    cut_a, cut_q, cut_r = (2, 2, n_a, w), (2, 2, n_q, w), (2, 2, n_r, w)
    a_sent, a_kept, b_sent, b_kept, q_sent, q_kept = stage(
        "stage_1", sides,
        (a_kept.reshape(cut_a), a_got.reshape(cut_a), b_kept, b_got, dw_1.reshape(cut_q)),
        [((1, 2, n_a, w), BF)] * 2 + [((2, 1, 1, n_b, w), BF)] * 2 + [((1, 2, n_q, w), BF)] * 2,
        stage_1,
    )
    a_got, b_got, q_got = swap(a_sent, "dp", first), swap(b_sent, "dp", second), swap(q_sent, "dp", first)
    a_kept, b_kept, q_kept, dqkv_1 = sync(a_kept, b_kept, q_kept, dqkv_1)
    dw_2, send, keep = back_2(
        me.reshape(1), groups, 1, do_ts, ids, h_all, a1, qkv, probs, o32, rl, params, w_t, dqkv_1,
        small_own, db_up,
    )
    a_got, b_got, q_got, dw_2, send, keep = sync(a_got, b_got, q_got, dw_2, send, keep)

    def stage_2(u, d, ins, outs):
        a_kept, a_got, b_kept, b_got, q_kept, q_got, r = ins
        for k, at in enumerate((pl.ds(1 - d, 1), pl.ds(d, 1))):
            outs[k][...] = plus(a_kept[:, at], a_got[:, at])
            outs[4 + k][...] = plus(q_kept[:, at], q_got[:, at])
        for k in range(2):
            outs[2 + k][...] = plus(b_kept[1 - k], b_got[1 - k])
        for k, at in enumerate((pl.ds(1 - u, 1), pl.ds(u, 1))):
            outs[6 + k][...] = r[at]

    a_sent, a_kept, b_sent, b_kept, q_sent, q_kept, r_sent, r_kept = stage(
        "stage_2", sides, (a_kept, a_got, b_kept, b_got, q_kept, q_got, dw_2.reshape(cut_r)),
        [((1, 1, n_a, w), BF)] * 2 + [((1, 1, n_b, w), BF)] * 2 + [((1, 1, n_q, w), BF)] * 2
        + [((1, 2, n_r, w), BF)] * 2,
        stage_2,
    )
    a_got, b_got, q_got, r_got, t_got = (
        swap(a_sent, "dp", second), swap(b_sent, "mp", 2), swap(q_sent, "dp", second),
        swap(r_sent, "dp", first), swap(send, "mp", 1),
    )

    def stage_3(u, d, ins, outs):
        a_kept, a_got, b_kept, b_got, q_kept, q_got, r_kept, r_got, keep, t_got = ins
        outs[0][...] = plus(a_kept[...], a_got[...])
        outs[1][...] = plus(b_kept[...], b_got[...])
        outs[2][...] = plus(q_kept[...], q_got[...])
        for k, at in enumerate((pl.ds(1 - d, 1), pl.ds(d, 1))):
            outs[3 + k][...] = plus(r_kept[:, at], r_got[:, at])
        outs[5][:padded] = plus(keep[padded : 2 * padded], t_got[padded : 2 * padded])
        outs[5][padded:] = two_parts(joined(keep[2 * padded :]) + joined(t_got[2 * padded :]))
        outs[6][...] = plus(keep[:padded], t_got[:padded])

    one_a, one_b, one_q, one_r = ((1, 1, n, w) for n in (n_a, n_b, n_q, n_r))
    a, b, q, r_sent, r_kept, t_sent, t_kept = stage(
        "stage_3", sides,
        (a_kept, a_got, b_kept, b_got, q_kept, q_got, r_kept, r_got, keep, t_got),
        [(one_a, BF), (one_b, BF), (one_q, BF), (one_r, BF), (one_r, BF)]
        + [((send.shape[0] - padded, w), BF), ((padded, w), BF)],
        stage_3,
    )
    a_got, b_got, r_got, t_got = (
        swap(a, "dp", full), swap(b, "dp", full), swap(r_sent, "dp", second), swap(t_sent, "mp", 2)
    )

    def stage_4(u, d, ins, outs):
        a, a_got, b, b_got, q, r_kept, r_got, t_sent, t_got = ins
        outs[0][...] = plus(a[...], a_got[...])
        outs[1][...] = plus(b[...], b_got[...])
        outs[2][:, :, :n_q] = q[...]
        outs[2][:, :, n_q:] = plus(r_kept[...], r_got[...])
        outs[3][...] = joined(t_sent[padded:]) + joined(t_got[padded:])

    a, b, q, small = stage(
        "stage_4", sides, (a, a_got, b, b_got, q, r_kept, r_got, t_sent, t_got),
        [(one_a, BF), (one_b, BF), ((1, 1, n_q + n_r, w), BF), ((groups + 16, w), F32)], stage_4,
    )
    for bit in rest:
        a, b = plus(a, swap(a, "dp", bit)), plus(b, swap(b, "dp", bit))
    a_got, b_got, q_got, s_got = (
        swap(a, "dp", first), swap(b, "dp", second), swap(q, "dp", full), swap(small, "dp", first)
    )
    h = (n_q + n_r) // 2

    def stage_5(u, d, ins, outs):
        a, a_got, b, b_got, q, q_got, small, s_got = ins
        a_o, b_o, q_0, q_1, s_o = outs
        a_o[pl.ds(u, 1)] = a[...]
        a_o[pl.ds(1 - u, 1)] = a_got[...]
        b_o[:, pl.ds(d, 1)] = b[...]
        b_o[:, pl.ds(1 - d, 1)] = b_got[...]
        q_0[...] = plus(q[:, :, :h], q_got[:, :, :h])
        q_1[...] = plus(q[:, :, h:], q_got[:, :, h:])
        s_o[...] = small[...] + s_got[...]

    a, b, q_0, q_1, small = stage(
        "stage_5", sides, (a, a_got, b, b_got, q, q_got, small, s_got),
        [((2, 1, n_a, w), BF), ((1, 2, n_b, w), BF)] + [((1, 1, h, w), BF)] * 2
        + [(small.shape, F32)],
        stage_5,
    )
    for bit in rest:
        q_0, q_1 = plus(q_0, swap(q_0, "dp", bit)), plus(q_1, swap(q_1, "dp", bit))
    a_got, b_got, q_0_got, q_1_got, s_got = (
        swap(a, "dp", second), swap(b, "dp", first), swap(q_0, "dp", first), swap(q_1, "dp", second),
        swap(small, "dp", second),
    )

    def stage_6(u, d, ins, outs):
        q_0, q_0_got, q_1, q_1_got, small, s_got = ins
        q_0_o, q_1_o, s_o = outs
        q_0_o[pl.ds(u, 1)] = q_0[...]
        q_0_o[pl.ds(1 - u, 1)] = q_0_got[...]
        q_1_o[:, pl.ds(d, 1)] = q_1[...]
        q_1_o[:, pl.ds(1 - d, 1)] = q_1_got[...]
        s_o[...] = small[...] + s_got[...]

    a_got, b_got, q_0_got, q_1_got, s_got = sync(a_got, b_got, q_0_got, q_1_got, s_got)
    q_0, q_1, small = stage(
        "stage_6", sides, (q_0, q_0_got, q_1, q_1_got, small, s_got),
        [((2, 1, h, w), BF), ((1, 2, h, w), BF), (small.shape, F32)], stage_6,
    )
    q_0_got, q_1_got, s_got = sync(
        swap(q_0, "dp", second), swap(q_1, "dp", first), swap(small, "dp", full)
    )
    small = small + s_got
    for bit in rest:
        small = small + swap(small, "dp", bit)

    def doubled(cur, got, side, axis):
        return jnp.where(
            side == 0,
            jnp.concatenate((cur, got), axis=axis),
            jnp.concatenate((got, cur), axis=axis),
        )

    g_a = doubled(a, a_got, side_d, 1).reshape(-1, w)
    g_b = doubled(b, b_got, side_u, 0).reshape(-1, w)
    q_all = jnp.concatenate(
        (doubled(q_0, q_0_got, side_d, 1), doubled(q_1, q_1_got, side_u, 0)), axis=2
    )
    g_qkv = jnp.concatenate(
        (q_all[:, :, :n_q].reshape(-1, w), q_all[:, :, n_q:].reshape(-1, w)), axis=0
    )
    dh0 = dh1 + t_kept.astype(F32) + t_got[:padded].astype(F32)
    input_grad = dh0[:rows_own].astype(BF)
    at = groups
    up_at = at + 6
    qv_at = at + 8
    b_up_grad = lax.dynamic_slice(small[up_at:qv_at].reshape(4, hid), (me, 0), (1, hid))[0]
    db = lax.dynamic_slice(small, (qv_at + me, 0), (1, 3 * feat)).reshape(heads, 3, HEAD)
    b_qv_grad = jnp.stack((db[:, 0].reshape(feat), db[:, 2].reshape(feat)), axis=0)
    g_qkv = g_qkv.astype(F32)
    w_qkv_grad = (
        g_qkv.reshape(heads, 3, HEAD, width).transpose(3, 1, 0, 2).reshape(width, 3, feat)
    )
    return (
        mixed,
        input_grad,
        small[:groups],
        small[at + 4],
        small[at + 5],
        w_qkv_grad,
        b_qv_grad,
        jnp.concatenate((g_a[hid:], g_b[hid:]), axis=0).astype(F32),
        small[at],
        small[at + 1],
        small[at + 2],
        g_a[:hid].astype(F32).T,
        b_up_grad,
        g_b[:hid].astype(F32),
        small[at + 3],
    )


def solution(mesh):
    rows = P(("dp", "mp"), None)
    return jax.shard_map(
        per_device,
        mesh=mesh,
        in_specs=(
            rows, P(("dp", "mp")), P(), P(), P(), P(None, None, "mp"), P(None, "mp"), P("mp", None),
            P(), P(), P(), P(None, "mp"), P("mp"), P("mp", None), P(), rows,
        ),
        out_specs=(
            rows, rows, P(), P(), P(), P(None, None, "mp"), P(None, "mp"), P("mp", None),
            P(), P(), P(), P(None, "mp"), P("mp"), P("mp", None), P(),
        ),
        check_vma=False,
    )
```

```python
import jax
import jax.numpy as jnp
from jax import lax
from jax.experimental import pallas as pl
from jax.experimental.pallas import tpu as pltpu
from jax.sharding import PartitionSpec as P

HEAD = 64
BF = jnp.bfloat16
F32 = jnp.float32
LOG2E = 1.4426950408889634
NN = (((1,), (0,)), ((), ()))
NT = (((1,), (1,)), ((), ()))
TN = (((0,), (0,)), ((), ()))
QB = 256
SD = jax.ShapeDtypeStruct
SAFE = 3000.0
EXTRA = 32


def mm(a, b, dims):
    return lax.dot_general(a, b, dims, preferred_element_type=F32)


def three_parts(v):
    hi = v.astype(BF)
    rest = v - hi.astype(F32)
    mid = rest.astype(BF)
    low = (rest - mid.astype(F32)).astype(BF)
    return hi, mid, low


def norm_rows(rows):
    centre = rows - jnp.mean(rows, axis=-1, keepdims=True)
    var = jnp.mean(centre * centre, axis=-1, keepdims=True)
    rstd = lax.rsqrt(var + 1e-05)
    return centre * rstd, rstd


def norm_back(grad, normed, rstd, gain):
    scaled = grad * gain
    return rstd * (
        scaled
        - jnp.mean(scaled, axis=-1, keepdims=True)
        - normed * jnp.mean(scaled * normed, axis=-1, keepdims=True)
    )


def gelu_parts(u):
    square = u * u
    t = jnp.tanh(0.7978845608028654 * (u + 0.044715 * (u * square)))
    half = 0.5 * (1.0 + t)
    slope = half + 0.5 * u * (1.0 - t * t) * (
        0.7978845608028654 + (3 * 0.044715 * 0.7978845608028654) * square
    )
    return u * half, slope


def onehot_rows(ids_row, groups):
    levels = lax.broadcasted_iota(jnp.int32, (groups, ids_row.shape[1]), 0).astype(F32)
    return (levels == ids_row).astype(F32).astype(BF)


def onehot_sum(hot, rows):
    hi = rows.astype(BF)
    low = (rows - hi.astype(F32)).astype(BF)
    return mm(hot, hi, NN) + mm(hot, low, NN)


class Copy:
    def __init__(self, src, dst, sem, near):
        self.copy = pltpu.make_async_copy(src, dst, sem)
        self.ref = near
        self.begun = False
        self.ended = False

    def start(self):
        if not self.begun:
            self.begun = True
            self.copy.start()
        return self

    def wait(self):
        self.start()
        if not self.ended:
            self.ended = True
            self.copy.wait()
        return self.ref


def hbm_call(
    name, body, ins, outs, *, raw_ins=(), raw_outs=(), near_ins=(), near_outs=(), smem=(), scratch=(),
    limit, flops, nbytes, eager=True,
):
    hbm = pl.BlockSpec(memory_space=pltpu.HBM)
    n_i, n_o = len(ins), len(outs)

    def kernel(*refs):
        rest = list(refs)

        def take(n):
            got = rest[:n]
            del rest[:n]
            return got

        small = take(len(smem))
        far_i, raw_i = take(n_i), take(len(raw_ins))
        raw_i = raw_i + take(len(near_ins))
        far_o, raw_o = take(n_o), take(len(raw_outs) + len(near_outs))
        near_i, near_o = take(n_i), take(n_o)
        own = take(len(scratch))
        sem_i, sem_o = take(2)
        feeds = [Copy(f, n, sem_i.at[k], n) for k, (f, n) in enumerate(zip(far_i, near_i))]
        sinks = [Copy(n, f, sem_o.at[k], n) for k, (f, n) in enumerate(zip(far_o, near_o))]
        if eager:
            for feed in feeds:
                feed.start()
        body(small, feeds, raw_i, sinks, raw_o, own)
        for sink in sinks:
            sink.start()
        for sink in sinks:
            sink.wait()
        for feed in feeds:
            feed.wait()

    vmem = lambda a: pltpu.VMEM(a.shape, a.dtype)
    return pl.pallas_call(
        kernel,
        out_shape=tuple(pltpu.HBM(s.shape, s.dtype) for s in (*outs, *raw_outs)) + tuple(near_outs),
        in_specs=[pl.BlockSpec(memory_space=pltpu.SMEM)] * len(smem)
        + [hbm] * (n_i + len(raw_ins))
        + [pl.BlockSpec(memory_space=pltpu.VMEM)] * len(near_ins),
        out_specs=(hbm,) * (n_o + len(raw_outs))
        + (pl.BlockSpec(memory_space=pltpu.VMEM),) * len(near_outs),
        scratch_shapes=[vmem(a) for a in ins]
        + [vmem(a) for a in outs]
        + list(scratch)
        + [pltpu.SemaphoreType.DMA((n_i,)), pltpu.SemaphoreType.DMA((max(n_o, 1),))],
        compiler_params=pltpu.CompilerParams(vmem_limit_bytes=limit * 2**20),
        cost_estimate=pl.CostEstimate(flops=flops, bytes_accessed=nbytes, transcendentals=0),
        name=name,
    )(*smem, *[pltpu.with_memory_space_constraint(a, pltpu.HBM) for a in (*ins, *raw_ins)], *near_ins)


def forward_heads(heads, first, rows_own, qkv, probs, o32, rl, p_buf, p_sem):
    tokens = qkv.shape[1]
    padded = tokens // 4
    lane = lax.broadcasted_iota(jnp.int32, (16, tokens), 1)
    sub = lax.broadcasted_iota(jnp.int32, (16, tokens), 0)
    valid = jnp.zeros((16, tokens), jnp.bool_)
    for j in range(4):
        valid = valid | ((lane >= j * padded) & (lane < j * padded + rows_own))
    top_row = sub == 0
    mask = jnp.where(top_row & ~valid, -1e30, 0.0).astype(BF)
    ones = jnp.where(top_row, 1.0, 0.0).astype(BF)
    parts = []
    bound = jnp.float32(0.0)
    for h in range(heads):
        at = 3 * (first + h) * HEAD
        scaled = qkv[at : at + HEAD, :].astype(F32) * (0.125 * LOG2E)
        hi = scaled.astype(BF)
        low = (scaled - hi.astype(F32)).astype(BF)
        k_h = qkv[at + HEAD : at + 2 * HEAD, :]
        k_f = k_h.astype(F32)
        q_x = jnp.concatenate((hi, low, ones), axis=0)
        k_x = jnp.concatenate((k_h, k_h, mask), axis=0)
        v_x = jnp.concatenate((qkv[at + 2 * HEAD : at + 3 * HEAD, :], ones), axis=0)
        parts.append((q_x, k_x, v_x))
        bound = jnp.maximum(
            bound,
            jnp.max(jnp.sum(scaled * scaled, axis=0, keepdims=True))
            * jnp.max(jnp.sum(k_f * k_f, axis=0, keepdims=True)),
        )
    copies = [
        pltpu.make_async_copy(p_buf.at[h], probs.at[h], p_sem.at[h]) for h in range(heads)
    ]

    def run(exact):
        for h, (q_x, k_x, v_x) in enumerate(parts):
            for b in range(tokens // QB):
                cols = slice(b * QB, (b + 1) * QB)
                scores = mm(q_x[:, cols], k_x, TN)
                if exact:
                    scores = scores - jnp.max(scores, axis=-1, keepdims=True)
                p_block = jnp.exp2(scores).astype(BF)
                p_buf[h, cols, :] = p_block
                out = mm(v_x, p_block, NT)
                inv = 1.0 / out[HEAD : HEAD + 1, :]
                o32[h * HEAD : (h + 1) * HEAD, cols] = out[:HEAD, :] * inv
                rl[h : h + 1, cols] = inv
            copies[h].start()

    small = bound < SAFE

    @pl.when(small)
    def _():
        run(False)

    @pl.when(jnp.logical_not(small))
    def _():
        run(True)

    return copies


def attend(padded, x0, others, ids, table, params, w_t):
    rows_own, width = x0.shape
    tokens = 4 * padded
    rows = w_t.shape[0]
    feat = rows // 3
    heads = feat // HEAD
    groups = table.shape[0]

    def body(_, ins, raw_i, outs, raw_o, own):
        a1, qkv, h_all, o32, rl = outs[:5]
        p_buf, p_sem, x_v = own
        par = ins[2].wait()
        bias = jnp.transpose(par[...])[:rows, 6:7]
        table_v = ins[3].wait()[...]
        for pair in range(2):
            for j in (2 * pair, 2 * pair + 1):
                at = slice(j * padded, (j + 1) * padded)
                x = ins[0].wait() if j == 0 else raw_i[j - 1]
                x_v[j, padded - 16 :, :] = jnp.zeros((16, width), F32)
                x_v[j, :rows_own, :] = x[...].astype(F32)
                hot = onehot_rows(raw_i[3 + j][0:1, :], groups)
                h = (x_v[j] + mm(hot, table_v, TN)).astype(BF)
                h_all.ref[at, :] = h
                normed, _ = norm_rows(h.astype(F32))
                a1.ref[at, :] = (normed * par[0:1, :] + par[1:2, :]).astype(BF)
            cols = slice(2 * pair * padded, 2 * (pair + 1) * padded)
            qkv.ref[:, cols] = (mm(ins[1].wait()[...], a1.ref[cols, :], NT) + bias).astype(BF)
        for sink in (a1, qkv, h_all):
            sink.start()
        copies = forward_heads(heads, 0, rows_own, qkv.ref, raw_o[0], o32.ref, rl.ref, p_buf, p_sem)
        for j in range(4):
            o = o32.ref[:, j * padded : (j + 1) * padded].astype(BF)
            if j < 2:
                outs[5 + j].ref[...] = o
            else:
                outs[7].ref[j - 2] = o
        for sink in outs:
            sink.start()
        for copy in copies:
            copy.wait()

    return hbm_call(
        "attend", body, (x0, w_t, params, table),
        (
            SD((tokens, width), BF), SD((rows, tokens), BF), SD((tokens, width), BF),
            SD((feat, tokens), F32), SD((8, tokens), F32), SD((feat, padded), BF),
            SD((feat, padded), BF), SD((2, feat, padded), BF),
        ),
        raw_outs=(SD((heads, tokens, tokens), BF),),
        near_ins=(*others, *ids),
        scratch=[
            pltpu.VMEM((heads, tokens, tokens), BF), pltpu.SemaphoreType.DMA((heads,)),
            pltpu.VMEM((4, padded, width), F32),
        ],
        limit=40, flops=12_000_000_000, nbytes=25_000_000,
    )


def own_part(rows_own, groups, sizes, sides, h_all, ids, dy, params, packs, pieces, o_ts):
    hid, feat = sizes
    padded, width = dy.shape
    half = hid // 2
    both = SD((2, 2 * hid + feat, width), BF)
    blocks = 2
    step = padded // blocks

    def body(smem, ins, raw_i, outs, raw_o, own):
        w_v, w_sem, act_v, du_v, h_v, h_sem = own
        bufs = (raw_o[0], raw_o[1])
        get_h = pltpu.make_async_copy(raw_i[0].at[:padded, :], h_v, h_sem.at[0])
        get_h.start()
        packs_r, pieces_r, o_r = raw_i[1:3], raw_i[3:13], raw_i[13:17]
        ids_r, dy_r = raw_i[17], raw_i[18]
        up_at, down_at = feat + EXTRA, feat + EXTRA + hid
        loads = []
        for j in range(2):
            for k in range(4):
                s = smem[0][k // 2]
                at = (k // 2) * hid + ((1 - s) if k % 2 else s) * half
                copy = pltpu.make_async_copy(
                    pieces_r[5 * j + 1 + k], w_v.at[j, pl.ds(pl.multiple_of(at, 16), half), :],
                    w_sem.at[4 * j + k],
                )
                copy.start()
                loads.append(copy)
        heads_r = (packs_r[0], packs_r[1], pieces_r[0], pieces_r[5])
        out = slice(0, feat)

        def up_of(j):
            return packs_r[j][up_at:down_at, :] if j < 2 else w_v[j - 2, :hid, :]

        def down_of(j):
            return packs_r[j][down_at:, :] if j < 2 else w_v[j - 2, hid:, :]

        par = ins[0].wait()
        attn = par[2:3, :]
        for j in range(4):
            attn = attn + mm(o_r[j][...], heads_r[j][out, :], TN)
        get_h.wait()
        h1 = h_v[...].astype(F32) + attn
        normed, rstd = norm_rows(h1)
        a2 = (normed * par[3:4, :] + par[4:5, :]).astype(BF)
        mixed, dh1, small, db_up = outs[:4]
        dy_b = dy_r[...]
        acc = [h1[r * step : (r + 1) * step] + par[5:6, :] for r in range(blocks)]
        da2 = [jnp.zeros((step, width), F32) for _ in range(blocks)]
        parts = [slice(r * step, (r + 1) * step) for r in range(blocks)]

        def shard_grads(j):
            for at, left, right in ((0, du_v, a2), (hid, act_v, dy_b)):
                bufs[j % 2][j // 2, at : at + hid, :] = mm(left[j], right, TN).astype(BF)

        for copy in loads:
            copy.wait()
        for n, j in enumerate((1, 3, 0, 2)):
            b_rows = heads_r[j][feat : feat + 16, :].astype(F32)
            b_up = (b_rows[0:1] + b_rows[1:2] + b_rows[2:3])[:, :hid]
            us = [mm(a2[at], up_of(j), NT) + b_up for at in parts]
            dacts = [mm(dy_b[at], down_of(j), NT) for at in parts]
            if n:
                shard_grads((1, 3, 0)[n - 1])
            db = jnp.zeros((1, hid), F32)
            for r, at in enumerate(parts):
                value, slope = gelu_parts(us[r])
                act = value.astype(BF)
                acc[r] = acc[r] + mm(act, down_of(j), NN)
                du = (dacts[r] * slope).astype(BF)
                da2[r] = da2[r] + mm(du, up_of(j), NN)
                act_v[j, at, :] = act
                du_v[j, at, :] = du
                db = db + jnp.sum(du.astype(F32), axis=0, keepdims=True)
            db_up.ref[j : j + 1, :] = db
        shard_grads(2)
        da2 = jnp.concatenate(da2, axis=0)
        dyf = dy_b.astype(F32)
        total = dyf + norm_back(da2, normed, rstd, par[3:4, :])
        dattn = total.astype(BF)
        for j in range(4):
            outs[4 + j].ref[...] = mm(heads_r[j][out, :], dattn, NT).astype(BF)
            outs[4 + j].start()
        dh1.ref[...] = total
        dh1.start()
        mixed.ref[...] = jnp.concatenate(acc, axis=0)[:rows_own].astype(BF)
        mixed.start()
        for j in (1, 3, 0, 2):
            d_out = mm(o_r[j][...], dattn, NN).astype(BF)
            bufs[j % 2][j // 2, 2 * hid :, :] = d_out
        hot = onehot_rows(ids_r[0:1, :], groups)
        small.ref[0:groups, :] = onehot_sum(hot, total)
        small.ref[groups : groups + 8, :] = jnp.concatenate(
            (
                jnp.sum(dattn.astype(F32), axis=0, keepdims=True),
                jnp.sum(da2 * normed, axis=0, keepdims=True),
                jnp.sum(da2, axis=0, keepdims=True),
                jnp.sum(dyf, axis=0, keepdims=True),
                jnp.zeros((4, width), F32),
            ),
            axis=0,
        )
    return hbm_call(
        "own_part", body, (params,),
        (
            SD((rows_own, width), BF), SD((padded, width), F32), SD((groups + 8, width), F32),
            SD((8, hid), F32),
        )
        + (SD((feat, padded), BF),) * 4,
        raw_ins=(h_all,),
        near_ins=(*packs, *pieces, *o_ts, ids, dy),
        near_outs=(both, both),
        smem=(sides,),
        scratch=[
            pltpu.VMEM((2, 2 * hid, width), BF), pltpu.SemaphoreType.DMA((8,)),
            pltpu.VMEM((4, padded, hid), BF), pltpu.VMEM((4, padded, hid), BF),
            pltpu.VMEM((padded, width), BF), pltpu.SemaphoreType.DMA((1,)),
        ],
        limit=40, flops=10_000_000_000, nbytes=16_000_000,
    )


def mark(value):
    def body(_, ins, raw_i, outs, raw_o, own):
        outs[0].ref[...] = jnp.zeros_like(outs[0].ref)

    (out,) = hbm_call(
        "mark", body, (value[:8, :128].astype(F32),), (SD((8, 128), F32),),
        limit=4, flops=20_000_000_000, nbytes=1_000,
    )
    return out


def back_heads(heads, first, d_out, q_v, probs, o32, rl, dqkv, d_s, p_all, p_sem, ready, late):
    tokens = q_v.shape[1]
    spans = [(h, at) for h in range(heads) for at in ((slice(0, tokens),) if h == 0 else (slice(0, tokens),))]
    fetches = [
        pltpu.make_async_copy(probs.at[first + h, at, :], p_all.at[h, at, :], p_sem.at[i])
        for i, (h, at) in enumerate(spans)
    ]
    begins = {(h, at.start): f for (h, at), f in zip(spans, fetches)}
    fetches[0].start()
    ready(lambda: [f.start() for f in fetches[1:]])
    d_out = d_out()
    sub = lax.broadcasted_iota(jnp.int32, (16, tokens), 0)
    ones = jnp.where(sub < 3, 1.0, 0.0).astype(BF)
    zero = jnp.zeros((13, tokens), F32)
    for h in range(heads):
        at = h * 3 * HEAD
        do_s = (d_out[h * HEAD : (h + 1) * HEAD, :].astype(F32) * rl[first + h : first + h + 1, :]).astype(BF)
        delta = -jnp.sum(
            do_s.astype(F32) * o32[h * HEAD : (h + 1) * HEAD, :], axis=0, keepdims=True
        )
        d_hi = delta.astype(BF).astype(F32)
        d_mid = (delta - d_hi).astype(BF).astype(F32)
        d_low = delta - d_hi - d_mid
        tail = jnp.concatenate((d_hi, d_mid, d_low, zero), axis=0).astype(BF)
        do_x = jnp.concatenate((do_s, tail), axis=0)
        q_h = q_v[at : at + HEAD, :]
        k_h = q_v[at + HEAD : at + 2 * HEAD, :]
        v_x = jnp.concatenate((q_v[at + 2 * HEAD : at + 3 * HEAD, :], ones), axis=0)
        for b in range(tokens // QB):
            cols = slice(b * QB, (b + 1) * QB)
            if (h, b * QB) in begins:
                begins[h, b * QB].wait()
                if h == 0:
                    late()
            dp = mm(do_x[:, cols], v_x, TN)
            ds = (p_all[h, cols, :].astype(F32) * dp).astype(BF)
            d_s[cols, :] = ds
            dqkv[at : at + HEAD, cols] = (0.125 * mm(k_h, ds, NT)).astype(BF)
        dqkv[at + HEAD : at + 2 * HEAD, :] = (0.125 * mm(q_h, d_s[...], NN)).astype(BF)
        dqkv[at + 2 * HEAD : at + 3 * HEAD, :] = mm(do_s, p_all[h], NN).astype(BF)


def back_scratch(heads, tokens):
    return [
        pltpu.VMEM((tokens, tokens), BF),
        pltpu.VMEM((heads, tokens, tokens), BF),
        pltpu.SemaphoreType.DMA((heads + 1,)),
        pltpu.VMEM((3 * heads * HEAD, tokens), BF),
        pltpu.SemaphoreType.DMA((2,)),
        pltpu.VMEM((heads * HEAD, tokens), F32),
    ]


def back_1(heads, dos, a1, qkv, probs, o32, rl):
    tokens, width = a1.shape
    rows = heads * 3 * HEAD

    def body(_, ins, raw_i, outs, raw_o, own):
        d_s, p_all, p_sem, q_v, q_sem, o_v = own
        gets = (
            pltpu.make_async_copy(raw_i[1].at[:rows, :], q_v, q_sem.at[0]),
            pltpu.make_async_copy(raw_i[2].at[: heads * HEAD, :], o_v, q_sem.at[1]),
        )

        def ready(more):
            ins[0].start()
            for get in gets:
                get.start()
            more()
            ins[0].wait()
            for get in gets:
                get.wait()

        dqkv, do_rest, dw = outs[0], outs[1], raw_o[0]
        d_out = jnp.concatenate([d[...] for d in raw_i[3:]], axis=1)
        do_rest.ref[...] = d_out[heads * HEAD :, :]
        do_rest.start()
        back_heads(
            heads, 0, lambda: d_out, q_v, raw_i[0], o_v, ins[0].ref, dqkv.ref, d_s, p_all, p_sem, ready,
            ins[1].start,
        )
        dqkv.start()
        dw[...] = mm(dqkv.ref[...], ins[1].wait()[...], NN).astype(BF)

    return hbm_call(
        "back_1", body, (rl, a1),
        (SD((rows, tokens), BF), SD((dos[0].shape[0] - heads * HEAD, tokens), BF)),
        near_outs=(SD((rows, width), BF),),
        raw_ins=(probs, qkv, o32),
        near_ins=dos,
        scratch=back_scratch(heads, tokens),
        limit=32, flops=14_000_000_000, nbytes=18_000_000, eager=False,
    )


def back_2(me, groups, heads, do_rest, ids, h_all, a1, qkv, probs, o32, rl, params, w_t, dqkv_1, small_own, db_up):
    tokens, width = a1.shape
    padded = tokens // 4
    cut = dqkv_1.shape[0]
    rows = w_t.shape[0] - cut

    def body(smem, ins, raw_i, outs, raw_o, own):
        d_s, p_all, p_sem, q_v, q_sem, o_v, dqkv = own
        gets = (
            pltpu.make_async_copy(raw_i[1].at[cut:, :], q_v, q_sem.at[0]),
            pltpu.make_async_copy(raw_i[2].at[cut // 3 :, :], o_v, q_sem.at[1]),
        )

        def ready(more):
            ins[8].start()
            ins[0].start()
            for get in gets:
                get.start()
            more()
            ins[0].wait()
            for get in gets:
                get.wait()

        back_heads(
            heads, cut // (3 * HEAD), lambda: ins[8].wait()[...], q_v, raw_i[0], o_v, ins[0].ref, dqkv,
            d_s, p_all, p_sem, ready, lambda: [feed.start() for feed in ins[1:8]],
        )
        dw, send, keep, small = raw_o
        shard = smem[0][0]
        dw[...] = mm(dqkv[...], ins[1].wait()[...], NN).astype(BF)
        w_v, d1, par = ins[2].wait(), ins[3].wait(), ins[4].wait()
        ones = jnp.ones((8, tokens), BF)
        small[groups + 8 :, :] = jnp.zeros((8, width), F32)
        db = jnp.concatenate((mm(ones, d1[...], NT)[0:1], mm(ones, dqkv[...], NT)[0:1]), axis=1)
        small[pl.ds(groups + 8 + shard, 1), : cut + rows] = db
        hid = ins[7].ref.shape[1]
        up_v = ins[7].wait()
        for s in range(4):
            at = s * hid
            small[
                groups + 6 + at // width : groups + 7 + at // width, at % width : at % width + hid
            ] = up_v[pl.ds(jnp.bitwise_xor(shard, s), 1), :]
        gain = par[0:1, :]
        table = jnp.zeros((groups, width), F32)
        dgain = jnp.zeros((1, width), F32)
        dbias = jnp.zeros((1, width), F32)
        order = (3, 1, 2, 0)

        def product(j):
            at = slice(j * padded, (j + 1) * padded)
            return mm(d1[:, at], w_v[:cut, :], TN) + mm(dqkv[:, at], w_v[cut:, :], TN)

        da1 = product(order[0])
        for n, j in enumerate(order):
            later = product(order[n + 1]) if n < 3 else None
            at = slice(j * padded, (j + 1) * padded)
            normed, rstd = norm_rows(ins[5].wait()[at, :].astype(F32))
            back = norm_back(da1, normed, rstd, gain)
            (keep, send)[j % 2][j // 2 * padded : (j // 2 + 1) * padded, :] = back.astype(BF)
            dgain = dgain + jnp.sum(da1 * normed, axis=0, keepdims=True)
            dbias = dbias + jnp.sum(da1, axis=0, keepdims=True)
            table = table + onehot_sum(onehot_rows(raw_i[3 + j][0:1, :], groups), back)
            da1 = later
        first = ins[6].wait()
        small[0:groups, :] = table + first[0:groups, :]
        small[groups : groups + 4, :] = first[groups : groups + 4, :]
        small[groups + 4 : groups + 6, :] = jnp.concatenate((dgain, dbias), axis=0)

    return hbm_call(
        "back_2", body, (rl, a1, w_t, dqkv_1, params, h_all, small_own, db_up, do_rest), (),
        near_outs=(
            SD((rows, width), BF), SD((2 * padded, width), BF), SD((2 * padded, width), BF),
            SD((groups + 16, width), F32),
        ),
        smem=(me,),
        raw_ins=(probs, qkv, o32),
        near_ins=ids,
        scratch=back_scratch(heads, tokens)
        + [pltpu.VMEM((rows, tokens), BF)],
        limit=34, flops=10_000_000_000, nbytes=18_000_000, eager=False,
    )


def swap(arr, axis, bit):
    size = lax.axis_size(axis)
    return lax.ppermute(arr, axis, [(i, i ^ bit) for i in range(size)])


def add(a, b):
    return (a.astype(F32) + b.astype(F32)).astype(a.dtype)


def after(value, *others):
    return lax.optimization_barrier((value, others))[0]


def side_of(bit):
    return (lax.axis_index("dp") // bit) % 2


def dp_bits():
    bits, bit = [], 1
    while bit < lax.axis_size("dp"):
        bits.append(bit)
        bit *= 2
    return bits


def sync(*values):
    return lax.optimization_barrier(values)


def plus(a, b):
    return (a.astype(F32) + b.astype(F32)).astype(BF)


def stage(name, sides, ins, outs, body, scratch=(), flops=100_000):
    near = pl.BlockSpec(memory_space=pltpu.VMEM)

    def kernel(side, *refs):
        body(side[0], side[1], refs[: len(ins)], refs[len(ins) :])

    return pl.pallas_call(
        kernel,
        out_shape=tuple(SD(shape, dtype) for shape, dtype in outs),
        in_specs=[pl.BlockSpec(memory_space=pltpu.SMEM)] + [near] * len(ins),
        out_specs=(near,) * len(outs),
        scratch_shapes=[pltpu.VMEM(shape, dtype) for shape, dtype in scratch],
        compiler_params=pltpu.CompilerParams(vmem_limit_bytes=16 * 2**20),
        cost_estimate=pl.CostEstimate(flops=flops, bytes_accessed=1_000, transcendentals=0),
        name=name,
    )(sides, *ins)


def per_device(
    block_input, group_ids, intr_table, ln1_gain, ln1_bias, w_qkv, b_qv, w_out, b_out,
    ln2_gain, ln2_bias, w_up, b_up, w_down, b_down, cotangent,
):
    rows_own, width = block_input.shape
    padded = -(-rows_own // 128) * 128
    groups = intr_table.shape[0]
    feat, hid = w_out.shape[0], w_down.shape[0]
    heads = feat // HEAD
    me = lax.axis_index("mp")
    bits = dp_bits()

    id_row = jnp.pad(group_ids.astype(F32)[None, :], ((0, 7), (0, padded - rows_own)), constant_values=-1)
    x_x = swap(block_input, "mp", 2)
    x_c = swap(block_input, "mp", 1)
    ids_x = swap(id_row, "mp", 2)
    ids_c = swap(id_row, "mp", 1)

    zero_row = jnp.zeros((width,), F32)
    b_three = jnp.stack((b_qv[0], jnp.zeros((feat,), F32), b_qv[1]), axis=0)
    b_row = b_three.reshape(3, heads, HEAD).transpose(1, 0, 2).reshape(3 * feat)
    params = jnp.stack(
        (
            ln1_gain, ln1_bias, b_out, ln2_gain, ln2_bias, b_down,
            jnp.pad(b_row, (0, width - 3 * feat)), zero_row,
        ),
        axis=0,
    )
    w_t = (
        w_qkv.reshape(width, 3, heads, HEAD).transpose(2, 1, 3, 0).reshape(3 * feat, width)
    )
    b_rows = jnp.stack(three_parts(b_up), axis=0)
    pack = jnp.concatenate(
        (w_out, jnp.pad(b_rows, ((0, EXTRA - 3), (0, width - hid))), w_up.T, w_down), axis=0
    )
    up_at, down_at, half = feat + EXTRA, feat + EXTRA + hid, hid // 2
    side_u, side_d = side_of(bits[0]), side_of(bits[1])
    sides = jnp.stack((side_u, side_d))
    dy = jnp.pad(cotangent, ((0, padded - rows_own), (0, 0)))
    x_x, ids_x, first_rows, params, w_t, up_near, down_near, dy, _ = sync(
        x_x, ids_x, pack[:up_at], params, w_t,
        lax.dynamic_slice_in_dim(pack, up_at + side_u * half, half, 0),
        lax.dynamic_slice_in_dim(pack, down_at + side_d * half, half, 0), dy, mark(pack),
    )
    x_xc, ids_xc = swap(x_x, "mp", 1), swap(ids_x, "mp", 1)
    up_near, down_near = swap(up_near, "mp", 2), swap(down_near, "mp", 2)
    out_x = swap(first_rows, "mp", 2)
    pack_c = swap(after(pack, x_x), "mp", 1)
    ids = (id_row, ids_c, ids_x, ids_xc)
    a1, qkv, h_all, o32, rl, *o_ts, probs = attend(
        padded, block_input, (x_c, x_x, x_xc), ids, intr_table, params, w_t
    )

    o_own, o_c, o_two = o_ts
    up_near, down_near, out_x, o_own = sync(up_near, down_near, out_x, o_own)
    o_c, o_two, up_far, down_far, _ = sync(
        swap(o_c, "mp", 1), swap(o_two, "mp", 2),
        swap(up_near, "dp", bits[0]), swap(down_near, "dp", bits[1]), mark(rl),
    )
    o_ts = (o_own, o_c, o_two[0], swap(o_two[1], "mp", 1))
    pieces = (out_x, up_near, up_far, down_near, down_far)
    pieces = pieces + tuple(swap(p, "mp", 1) for p in pieces)
    mixed, dh1, small_own, db_up, *do_ts, keep_g, send_g = own_part(
        rows_own, groups, (hid, feat), sides, h_all, id_row, dy, params,
        (pack, pack_c), pieces, o_ts,
    )
    do_own = do_ts[0]
    first, second, full, *rest = bits
    do_c, do_x, do_xc, got_g, _ = sync(
        *(swap(do_ts[j], "mp", j) for j in (1, 2, 3)), swap(send_g, "mp", 1), mark(small_own)
    )

    w = width
    n_a, n_b, n_c, n_q, n_r = hid // 4, hid // 4, feat // 4, 2 * feat // 4, feat // 4

    def stage_0(u, d, ins, outs):
        keep, got = ins
        a_sent, a_kept, b_sent, b_kept, c_sent, c_kept = outs
        a_sent[...] = plus(keep[1, :hid], got[1, :hid])
        a_kept[...] = plus(keep[0, :hid], got[0, :hid])
        for out, side in ((b_sent, 1 - u), (b_kept, u)):
            for z in range(2):
                rows = pl.ds(pl.multiple_of(hid + (2 * side + z) * n_b, 16), n_b)
                out[:, 0, z] = plus(keep[:, rows], got[:, rows])
        for out, side in ((c_sent, 1 - d), (c_kept, d)):
            for y in range(2):
                rows = pl.ds(pl.multiple_of(2 * hid + (2 * y + side) * n_c, 16), n_c)
                out[:, y, 0] = plus(keep[:, rows], got[:, rows])

    a_sent, a_kept, b_sent, b_kept, c_sent, c_kept = stage(
        "stage_0", sides, (keep_g, got_g),
        [((hid, w), BF)] * 2 + [((2, 1, 2, n_b, w), BF)] * 2 + [((2, 2, 1, n_c, w), BF)] * 2, stage_0,
    )
    a_got, b_got, c_got = swap(a_sent, "mp", 2), swap(b_sent, "dp", first), swap(c_sent, "dp", second)
    do_own, do_c, do_x, do_xc, a_kept, b_kept, c_kept = sync(
        do_own, do_c, do_x, do_xc, a_kept, b_kept, c_kept
    )
    do_ts = (do_own, do_c, do_x, do_xc)
    dqkv_1, do_rest, dw_1 = back_1(heads - 1, do_ts, a1, qkv, probs, o32, rl)

    def stage_1(u, d, ins, outs):
        a_kept, a_got, b_kept, b_got, q, c_kept, c_got = ins
        for k, at in enumerate((pl.ds(1 - u, 1), pl.ds(u, 1))):
            outs[k][...] = plus(a_kept[at], a_got[at])
            outs[4 + k][...] = q[at]
        for k, at in enumerate((pl.ds(1 - d, 1), pl.ds(d, 1))):
            outs[2 + k][...] = plus(b_kept[:, :, at], b_got[:, :, at])
            outs[6 + k][...] = plus(c_kept[1 - k], c_got[1 - k])

    cut_a, cut_q, cut_r = (2, 2, n_a, w), (2, 2, n_q, w), (2, 2, n_r, w)
    a_sent, a_kept, b_sent, b_kept, q_sent, q_kept, c_sent, c_kept = stage(
        "stage_1", sides,
        (a_kept.reshape(cut_a), a_got.reshape(cut_a), b_kept, b_got, dw_1.reshape(cut_q), c_kept, c_got),
        [((1, 2, n_a, w), BF)] * 2 + [((2, 1, 1, n_b, w), BF)] * 2 + [((1, 2, n_q, w), BF)] * 2
        + [((2, 1, n_c, w), BF)] * 2,
        stage_1,
    )
    a_got, b_got, q_got = swap(a_sent, "dp", first), swap(b_sent, "dp", second), swap(q_sent, "dp", first)
    c_got = swap(c_sent, "mp", 2)
    a_kept, b_kept, q_kept, c_kept, dqkv_1 = sync(a_kept, b_kept, q_kept, c_kept, dqkv_1)
    dw_2, send, keep, small = back_2(
        me.reshape(1), groups, 1, do_rest, ids, h_all, a1, qkv, probs, o32, rl, params, w_t, dqkv_1,
        small_own, db_up,
    )
    a_got, b_got, q_got, c_got, dw_2, send, keep, small = sync(
        a_got, b_got, q_got, c_got, dw_2, send, keep, small
    )

    def stage_2(u, d, ins, outs):
        a_kept, a_got, b_kept, b_got, q_kept, q_got, r, c_kept, c_got = ins
        for k, at in enumerate((pl.ds(1 - d, 1), pl.ds(d, 1))):
            outs[k][...] = plus(a_kept[:, at], a_got[:, at])
            outs[4 + k][...] = plus(q_kept[:, at], q_got[:, at])
        for k in range(2):
            outs[2 + k][...] = plus(b_kept[1 - k], b_got[1 - k])
        for k, at in enumerate((pl.ds(1 - u, 1), pl.ds(u, 1))):
            outs[6 + k][...] = r[at]
            outs[8 + k][...] = plus(c_kept[at], c_got[at])

    a_sent, a_kept, b_sent, b_kept, q_sent, q_kept, r_sent, r_kept, c_sent, c_kept = stage(
        "stage_2", sides, (a_kept, a_got, b_kept, b_got, q_kept, q_got, dw_2.reshape(cut_r), c_kept, c_got),
        [((1, 1, n_a, w), BF)] * 2 + [((1, 1, n_b, w), BF)] * 2 + [((1, 1, n_q, w), BF)] * 2
        + [((1, 2, n_r, w), BF)] * 2 + [((1, 1, n_c, w), BF)] * 2,
        stage_2,
    )
    a_got, b_got, q_got, r_got, t_got = (
        swap(a_sent, "dp", second), swap(b_sent, "mp", 2), swap(q_sent, "dp", second),
        swap(r_sent, "dp", first), swap(send, "mp", 1),
    )
    s_got = [swap(small, "mp", bit) for bit in (1, 2, 3)]

    def stage_3(u, d, ins, outs):
        a_kept, a_got, b_kept, b_got, q_kept, q_got, r_kept, r_got, keep, t_got = ins[:10]
        s_0, s_1, s_2, s_3, c_sent = ins[10:]
        outs[8][...] = c_sent[...]
        outs[0][...] = plus(a_kept[...], a_got[...])
        outs[1][...] = plus(b_kept[...], b_got[...])
        outs[2][...] = plus(q_kept[...], q_got[...])
        for k, at in enumerate((pl.ds(1 - d, 1), pl.ds(d, 1))):
            outs[3 + k][...] = plus(r_kept[:, at], r_got[:, at])
        outs[5][...] = plus(keep[padded:], t_got[padded:])
        outs[6][...] = plus(keep[:padded], t_got[:padded])
        outs[7][...] = (s_0[...] + s_1[...]) + (s_2[...] + s_3[...])

    one_a, one_b, one_c, one_q, one_r = ((1, 1, n, w) for n in (n_a, n_b, n_c, n_q, n_r))
    a, b, q, r_sent, r_kept, t_sent, t_kept, small, c_sent = stage(
        "stage_3", sides,
        (a_kept, a_got, b_kept, b_got, q_kept, q_got, r_kept, r_got, keep, t_got,
         small, *s_got, c_sent),
        [(one_a, BF), (one_b, BF), (one_q, BF), (one_r, BF), (one_r, BF)]
        + [((padded, w), BF)] * 2 + [(small.shape, F32), (one_c, BF)],
        stage_3,
    )
    a_got, b_got, r_got, t_got, s_got = (
        swap(a, "dp", full), swap(b, "dp", full), swap(r_sent, "dp", second), swap(t_sent, "mp", 2),
        swap(small, "dp", first),
    )
    c_got = swap(c_sent, "dp", first)

    def stage_4(u, d, ins, outs):
        a, a_got, b, b_got, q, r_kept, r_got, small, s_got, c_kept, c_got, _ = ins
        outs[0][...] = plus(a[...], a_got[...])
        outs[1][...] = plus(b[...], b_got[...])
        outs[2][:, :, :n_q] = q[...]
        outs[2][:, :, n_q : n_q + n_r] = plus(r_kept[...], r_got[...])
        outs[2][:, :, n_q + n_r :] = plus(c_kept[...], c_got[...])
        outs[3][...] = small[...] + s_got[...]

    a, b, q, small = stage(
        "stage_4", sides, (a, a_got, b, b_got, q, r_kept, r_got, small, s_got, c_kept, c_got, t_got),
        [(one_a, BF), (one_b, BF), ((1, 1, n_q + n_r + n_c, w), BF), ((groups + 16, w), F32)], stage_4,
    )
    for bit in rest:
        small = small + swap(small, "dp", bit)
        a, b = plus(a, swap(a, "dp", bit)), plus(b, swap(b, "dp", bit))
    a_got, b_got, q_got, s_got = (
        swap(a, "dp", first), swap(b, "dp", second), swap(q, "dp", full), swap(small, "dp", second)
    )
    dh0 = dh1 + t_kept.astype(F32) + t_got.astype(F32)
    input_grad = dh0[:rows_own].astype(BF)
    q_got = after(q_got, input_grad)
    h = (n_q + n_r + n_c) // 32 * 16
    h_1 = n_q + n_r + n_c - h

    def stage_5(u, d, ins, outs):
        a, a_got, b, b_got, q, q_got, small, s_got = ins
        a_o, b_o, q_0, q_1, s_o = outs
        a_o[pl.ds(u, 1)] = a[...]
        a_o[pl.ds(1 - u, 1)] = a_got[...]
        b_o[:, pl.ds(d, 1)] = b[...]
        b_o[:, pl.ds(1 - d, 1)] = b_got[...]
        q_0[...] = plus(q[:, :, :h], q_got[:, :, :h])
        q_1[...] = plus(q[:, :, h:], q_got[:, :, h:])
        s_o[...] = small[...] + s_got[...]

    a, b, q_0, q_1, small = stage(
        "stage_5", sides, (a, a_got, b, b_got, q, q_got, small, s_got),
        [((2, 1, n_a, w), BF), ((1, 2, n_b, w), BF), ((1, 1, h, w), BF), ((1, 1, h_1, w), BF),
         (small.shape, F32)],
        stage_5,
    )
    for bit in rest:
        q_0, q_1 = plus(q_0, swap(q_0, "dp", bit)), plus(q_1, swap(q_1, "dp", bit))
    a_got, b_got, q_0_got, q_1_got, s_got = (
        swap(a, "dp", second), swap(b, "dp", first), swap(q_0, "dp", first), swap(q_1, "dp", second),
        swap(small, "dp", full),
    )

    def stage_6(u, d, ins, outs):
        q_0, q_0_got, q_1, q_1_got, small, s_got = ins
        q_0_o, q_1_o, s_o = outs
        s_o[...] = small[...] + s_got[...]
        q_0_o[pl.ds(u, 1)] = q_0[...]
        q_0_o[pl.ds(1 - u, 1)] = q_0_got[...]
        q_1_o[:, pl.ds(d, 1)] = q_1[...]
        q_1_o[:, pl.ds(1 - d, 1)] = q_1_got[...]

    q_0, q_1, small = stage(
        "stage_6", sides, (q_0, q_0_got, q_1, q_1_got, small, s_got),
        [((2, 1, h, w), BF), ((1, 2, h_1, w), BF), (small.shape, F32)], stage_6,
    )
    q_0_got, q_1_got = swap(q_0, "dp", second), swap(q_1, "dp", first)

    def stage_7(u, d, ins, outs):
        a, a_got, b, b_got = ins[:4]
        up_o, down_o, chunk_a = outs
        for y in range(2):
            for z, src in ((d, a), (1 - d, a_got)):
                at = pl.multiple_of((2 * y + z) * n_a, 16)
                chunk_a[pl.ds(at, n_a), :] = src[y, 0].astype(F32)
        for z in range(2):
            for y, src in ((u, b), (1 - u, b_got)):
                at = pl.multiple_of((2 * y + z) * n_b, 16)
                down_o[pl.ds(at, n_b), :] = src[0, z].astype(F32)
        up_o[...] = jnp.transpose(chunk_a[...])

    g_up, g_down = stage(
        "stage_7", sides, (a, a_got, b, b_got, q_0),
        [((w, hid), F32), ((hid, w), F32)], stage_7, [((hid, w), F32)], 20_000_000_000,
    )

    def doubled(cur, got, side, axis):
        return jnp.where(
            side == 0,
            jnp.concatenate((cur, got), axis=axis),
            jnp.concatenate((got, cur), axis=axis),
        )

    q_all = jnp.concatenate(
        (doubled(q_0, q_0_got, side_d, 1), doubled(q_1, q_1_got, side_u, 0)), axis=2
    )
    g_qkv = jnp.concatenate(
        (q_all[:, :, :n_q].reshape(-1, w), q_all[:, :, n_q : n_q + n_r].reshape(-1, w)), axis=0
    )
    g_out = q_all[:, :, n_q + n_r :].reshape(-1, w).astype(F32)
    at = groups
    up_at = at + 6
    qv_at = at + 8
    b_up_grad = lax.dynamic_slice(small[up_at:qv_at].reshape(4, hid), (me, 0), (1, hid))[0]
    db = lax.dynamic_slice(small, (qv_at + me, 0), (1, 3 * feat)).reshape(heads, 3, HEAD)
    b_qv_grad = jnp.stack((db[:, 0].reshape(feat), db[:, 2].reshape(feat)), axis=0)
    g_qkv = g_qkv.astype(F32)
    w_qkv_grad = (
        g_qkv.reshape(heads, 3, HEAD, width).transpose(3, 1, 0, 2).reshape(width, 3, feat)
    )
    return (
        mixed,
        input_grad,
        small[:groups],
        small[at + 4],
        small[at + 5],
        w_qkv_grad,
        b_qv_grad,
        g_out,
        small[at],
        small[at + 1],
        small[at + 2],
        g_up,
        b_up_grad,
        g_down,
        small[at + 3],
    )


def solution(mesh):
    rows = P(("dp", "mp"), None)
    return jax.shard_map(
        per_device,
        mesh=mesh,
        in_specs=(
            rows, P(("dp", "mp")), P(), P(), P(), P(None, None, "mp"), P(None, "mp"), P("mp", None),
            P(), P(), P(), P(None, "mp"), P("mp"), P("mp", None), P(), rows,
        ),
        out_specs=(
            rows, rows, P(), P(), P(), P(None, None, "mp"), P(None, "mp"), P("mp", None),
            P(), P(), P(), P(None, "mp"), P("mp"), P("mp", None), P(),
        ),
        check_vma=False,
    )
```

```python
import jax
import jax.numpy as jnp
from jax import lax
from jax.experimental import pallas as pl
from jax.experimental.pallas import tpu as pltpu
from jax.sharding import PartitionSpec as P

HEAD = 64
BF = jnp.bfloat16
F32 = jnp.float32
LOG2E = 1.4426950408889634
NN = (((1,), (0,)), ((), ()))
NT = (((1,), (1,)), ((), ()))
TN = (((0,), (0,)), ((), ()))
QB = 256
SD = jax.ShapeDtypeStruct
SAFE = 3000.0
EXTRA = 32


def mm(a, b, dims):
    return lax.dot_general(a, b, dims, preferred_element_type=F32)


def three_parts(v):
    hi = v.astype(BF)
    rest = v - hi.astype(F32)
    mid = rest.astype(BF)
    low = (rest - mid.astype(F32)).astype(BF)
    return hi, mid, low


def norm_rows(rows):
    centre = rows - jnp.mean(rows, axis=-1, keepdims=True)
    var = jnp.mean(centre * centre, axis=-1, keepdims=True)
    rstd = lax.rsqrt(var + 1e-05)
    return centre * rstd, rstd


def norm_back(grad, normed, rstd, gain):
    scaled = grad * gain
    return rstd * (
        scaled
        - jnp.mean(scaled, axis=-1, keepdims=True)
        - normed * jnp.mean(scaled * normed, axis=-1, keepdims=True)
    )


def gelu_parts(u):
    square = u * u
    t = jnp.tanh(0.7978845608028654 * (u + 0.044715 * (u * square)))
    half = 0.5 * (1.0 + t)
    slope = half + 0.5 * u * (1.0 - t * t) * (
        0.7978845608028654 + (3 * 0.044715 * 0.7978845608028654) * square
    )
    return u * half, slope


def onehot_rows(ids_row, groups):
    levels = lax.broadcasted_iota(jnp.int32, (groups, ids_row.shape[1]), 0).astype(F32)
    return (levels == ids_row).astype(F32).astype(BF)


def onehot_sum(hot, rows):
    hi = rows.astype(BF)
    low = (rows - hi.astype(F32)).astype(BF)
    return mm(hot, hi, NN) + mm(hot, low, NN)


class Copy:
    def __init__(self, src, dst, sem, near):
        self.copy = pltpu.make_async_copy(src, dst, sem)
        self.ref = near
        self.begun = False
        self.ended = False

    def start(self):
        if not self.begun:
            self.begun = True
            self.copy.start()
        return self

    def wait(self):
        self.start()
        if not self.ended:
            self.ended = True
            self.copy.wait()
        return self.ref


def hbm_call(
    name, body, ins, outs, *, raw_ins=(), raw_outs=(), near_ins=(), near_outs=(), smem=(), scratch=(),
    limit, flops, nbytes, eager=True,
):
    hbm = pl.BlockSpec(memory_space=pltpu.HBM)
    n_i, n_o = len(ins), len(outs)

    def kernel(*refs):
        rest = list(refs)

        def take(n):
            got = rest[:n]
            del rest[:n]
            return got

        small = take(len(smem))
        far_i, raw_i = take(n_i), take(len(raw_ins))
        raw_i = raw_i + take(len(near_ins))
        far_o, raw_o = take(n_o), take(len(raw_outs) + len(near_outs))
        near_i, near_o = take(n_i), take(n_o)
        own = take(len(scratch))
        sem_i, sem_o = take(2)
        feeds = [Copy(f, n, sem_i.at[k], n) for k, (f, n) in enumerate(zip(far_i, near_i))]
        sinks = [Copy(n, f, sem_o.at[k], n) for k, (f, n) in enumerate(zip(far_o, near_o))]
        if eager:
            for feed in feeds:
                feed.start()
        body(small, feeds, raw_i, sinks, raw_o, own)
        for sink in sinks:
            sink.start()
        for sink in sinks:
            sink.wait()
        for feed in feeds:
            feed.wait()

    vmem = lambda a: pltpu.VMEM(a.shape, a.dtype)
    return pl.pallas_call(
        kernel,
        out_shape=tuple(pltpu.HBM(s.shape, s.dtype) for s in (*outs, *raw_outs)) + tuple(near_outs),
        in_specs=[pl.BlockSpec(memory_space=pltpu.SMEM)] * len(smem)
        + [hbm] * (n_i + len(raw_ins))
        + [pl.BlockSpec(memory_space=pltpu.VMEM)] * len(near_ins),
        out_specs=(hbm,) * (n_o + len(raw_outs))
        + (pl.BlockSpec(memory_space=pltpu.VMEM),) * len(near_outs),
        scratch_shapes=[vmem(a) for a in ins]
        + [vmem(a) for a in outs]
        + list(scratch)
        + [pltpu.SemaphoreType.DMA((n_i,)), pltpu.SemaphoreType.DMA((max(n_o, 1),))],
        compiler_params=pltpu.CompilerParams(vmem_limit_bytes=limit * 2**20),
        cost_estimate=pl.CostEstimate(flops=flops, bytes_accessed=nbytes, transcendentals=0),
        name=name,
    )(*smem, *[pltpu.with_memory_space_constraint(a, pltpu.HBM) for a in (*ins, *raw_ins)], *near_ins)


def forward_heads(heads, first, rows_own, qkv, probs, o32, rl, p_buf, p_sem):
    tokens = qkv.shape[1]
    padded = tokens // 4
    lane = lax.broadcasted_iota(jnp.int32, (16, tokens), 1)
    sub = lax.broadcasted_iota(jnp.int32, (16, tokens), 0)
    valid = jnp.zeros((16, tokens), jnp.bool_)
    for j in range(4):
        valid = valid | ((lane >= j * padded) & (lane < j * padded + rows_own))
    top_row = sub == 0
    mask = jnp.where(top_row & ~valid, -1e30, 0.0).astype(BF)
    ones = jnp.where(top_row, 1.0, 0.0).astype(BF)
    parts = []
    bound = jnp.float32(0.0)
    for h in range(heads):
        at = 3 * (first + h) * HEAD
        scaled = qkv[at : at + HEAD, :].astype(F32) * (0.125 * LOG2E)
        hi = scaled.astype(BF)
        low = (scaled - hi.astype(F32)).astype(BF)
        k_h = qkv[at + HEAD : at + 2 * HEAD, :]
        k_f = k_h.astype(F32)
        q_x = jnp.concatenate((hi, low, ones), axis=0)
        k_x = jnp.concatenate((k_h, k_h, mask), axis=0)
        v_x = jnp.concatenate((qkv[at + 2 * HEAD : at + 3 * HEAD, :], ones), axis=0)
        parts.append((q_x, k_x, v_x))
        bound = jnp.maximum(
            bound,
            jnp.max(jnp.sum(scaled * scaled, axis=0, keepdims=True))
            * jnp.max(jnp.sum(k_f * k_f, axis=0, keepdims=True)),
        )
    copies = [
        pltpu.make_async_copy(p_buf.at[h], probs.at[h], p_sem.at[h]) for h in range(heads)
    ]

    def run(exact):
        for h, (q_x, k_x, v_x) in enumerate(parts):
            for b in range(tokens // QB):
                cols = slice(b * QB, (b + 1) * QB)
                scores = mm(q_x[:, cols], k_x, TN)
                if exact:
                    scores = scores - jnp.max(scores, axis=-1, keepdims=True)
                p_block = jnp.exp2(scores).astype(BF)
                p_buf[h, cols, :] = p_block
                out = mm(v_x, p_block, NT)
                inv = 1.0 / out[HEAD : HEAD + 1, :]
                o32[h * HEAD : (h + 1) * HEAD, cols] = out[:HEAD, :] * inv
                rl[h : h + 1, cols] = inv
            copies[h].start()

    small = bound < SAFE

    @pl.when(small)
    def _():
        run(False)

    @pl.when(jnp.logical_not(small))
    def _():
        run(True)

    return copies


def attend(padded, x0, others, ids, table, params, w_t):
    rows_own, width = x0.shape
    tokens = 4 * padded
    rows = w_t.shape[0]
    feat = rows // 3
    heads = feat // HEAD
    groups = table.shape[0]

    def body(_, ins, raw_i, outs, raw_o, own):
        a1, qkv, h_all, o32, rl = outs[:5]
        p_buf, p_sem, x_v = own
        par = ins[2].wait()
        bias = jnp.transpose(par[...])[:rows, 6:7]
        table_v = ins[3].wait()[...]
        for pair in range(2):
            for j in (2 * pair, 2 * pair + 1):
                at = slice(j * padded, (j + 1) * padded)
                x = ins[0].wait() if j == 0 else raw_i[j - 1]
                x_v[j, padded - 16 :, :] = jnp.zeros((16, width), F32)
                x_v[j, :rows_own, :] = x[...].astype(F32)
                hot = onehot_rows(raw_i[3 + j][0:1, :], groups)
                h = (x_v[j] + mm(hot, table_v, TN)).astype(BF)
                h_all.ref[at, :] = h
                normed, _ = norm_rows(h.astype(F32))
                a1.ref[at, :] = (normed * par[0:1, :] + par[1:2, :]).astype(BF)
            cols = slice(2 * pair * padded, 2 * (pair + 1) * padded)
            qkv.ref[:, cols] = (mm(ins[1].wait()[...], a1.ref[cols, :], NT) + bias).astype(BF)
        for sink in (a1, qkv, h_all):
            sink.start()
        copies = forward_heads(heads, 0, rows_own, qkv.ref, raw_o[0], o32.ref, rl.ref, p_buf, p_sem)
        for j in range(4):
            o = o32.ref[:, j * padded : (j + 1) * padded].astype(BF)
            if j < 2:
                outs[5 + j].ref[...] = o
            else:
                outs[7].ref[j - 2] = o
        for sink in outs:
            sink.start()
        for copy in copies:
            copy.wait()

    return hbm_call(
        "attend", body, (x0, w_t, params, table),
        (
            SD((tokens, width), BF), SD((rows, tokens), BF), SD((tokens, width), BF),
            SD((feat, tokens), F32), SD((8, tokens), F32), SD((feat, padded), BF),
            SD((feat, padded), BF), SD((2, feat, padded), BF),
        ),
        raw_outs=(SD((heads, tokens, tokens), BF),),
        near_ins=(*others, *ids),
        scratch=[
            pltpu.VMEM((heads, tokens, tokens), BF), pltpu.SemaphoreType.DMA((heads,)),
            pltpu.VMEM((4, padded, width), F32),
        ],
        limit=40, flops=12_000_000_000, nbytes=25_000_000,
    )


def own_part(rows_own, groups, sizes, sides, h_all, ids, dy, params, packs, pieces, o_ts):
    hid, feat = sizes
    padded, width = dy.shape
    half = hid // 2
    both = SD((2, 2 * hid + feat, width), BF)
    blocks = 2
    step = padded // blocks

    def body(smem, ins, raw_i, outs, raw_o, own):
        w_v, w_sem, act_v, du_v, h_v, h_sem = own
        bufs = (raw_o[0], raw_o[1])
        get_h = pltpu.make_async_copy(raw_i[0].at[:padded, :], h_v, h_sem.at[0])
        get_h.start()
        packs_r, pieces_r, o_r = raw_i[1:3], raw_i[3:13], raw_i[13:17]
        ids_r, dy_r = raw_i[17], raw_i[18]
        up_at, down_at = feat + EXTRA, feat + EXTRA + hid
        loads = []
        for j in range(2):
            for k in range(4):
                s = smem[0][k // 2]
                at = (k // 2) * hid + ((1 - s) if k % 2 else s) * half
                copy = pltpu.make_async_copy(
                    pieces_r[5 * j + 1 + k], w_v.at[j, pl.ds(pl.multiple_of(at, 16), half), :],
                    w_sem.at[4 * j + k],
                )
                copy.start()
                loads.append(copy)
        heads_r = (packs_r[0], packs_r[1], pieces_r[0], pieces_r[5])
        out = slice(0, feat)

        def up_of(j):
            return packs_r[j][up_at:down_at, :] if j < 2 else w_v[j - 2, :hid, :]

        def down_of(j):
            return packs_r[j][down_at:, :] if j < 2 else w_v[j - 2, hid:, :]

        par = ins[0].wait()
        attn = par[2:3, :]
        for j in range(4):
            attn = attn + mm(o_r[j][...], heads_r[j][out, :], TN)
        get_h.wait()
        h1 = h_v[...].astype(F32) + attn
        normed, rstd = norm_rows(h1)
        a2 = (normed * par[3:4, :] + par[4:5, :]).astype(BF)
        mixed, dh1, small, db_up = outs[:4]
        dy_b = dy_r[...]
        acc = [h1[r * step : (r + 1) * step] + par[5:6, :] for r in range(blocks)]
        da2 = [jnp.zeros((step, width), F32) for _ in range(blocks)]
        parts = [slice(r * step, (r + 1) * step) for r in range(blocks)]

        def shard_grads(j):
            for at, left, right in ((0, du_v, a2), (hid, act_v, dy_b)):
                bufs[j % 2][j // 2, at : at + hid, :] = mm(left[j], right, TN).astype(BF)

        for copy in loads:
            copy.wait()
        for n, j in enumerate((1, 3, 0, 2)):
            b_rows = heads_r[j][feat : feat + 16, :].astype(F32)
            b_up = (b_rows[0:1] + b_rows[1:2] + b_rows[2:3])[:, :hid]
            us = [mm(a2[at], up_of(j), NT) + b_up for at in parts]
            dacts = [mm(dy_b[at], down_of(j), NT) for at in parts]
            if n:
                shard_grads((1, 3, 0)[n - 1])
            db = jnp.zeros((1, hid), F32)
            for r, at in enumerate(parts):
                value, slope = gelu_parts(us[r])
                act = value.astype(BF)
                acc[r] = acc[r] + mm(act, down_of(j), NN)
                du = (dacts[r] * slope).astype(BF)
                da2[r] = da2[r] + mm(du, up_of(j), NN)
                act_v[j, at, :] = act
                du_v[j, at, :] = du
                db = db + jnp.sum(du.astype(F32), axis=0, keepdims=True)
            db_up.ref[j : j + 1, :] = db
        shard_grads(2)
        da2 = jnp.concatenate(da2, axis=0)
        dyf = dy_b.astype(F32)
        total = dyf + norm_back(da2, normed, rstd, par[3:4, :])
        dattn = total.astype(BF)
        for j in range(4):
            outs[4 + j].ref[...] = mm(heads_r[j][out, :], dattn, NT).astype(BF)
            outs[4 + j].start()
        dh1.ref[...] = total
        dh1.start()
        mixed.ref[...] = jnp.concatenate(acc, axis=0)[:rows_own].astype(BF)
        mixed.start()
        for j in (1, 3, 0, 2):
            d_out = mm(o_r[j][...], dattn, NN).astype(BF)
            bufs[j % 2][j // 2, 2 * hid :, :] = d_out
        hot = onehot_rows(ids_r[0:1, :], groups)
        small.ref[0:groups, :] = onehot_sum(hot, total)
        small.ref[groups : groups + 8, :] = jnp.concatenate(
            (
                jnp.sum(dattn.astype(F32), axis=0, keepdims=True),
                jnp.sum(da2 * normed, axis=0, keepdims=True),
                jnp.sum(da2, axis=0, keepdims=True),
                jnp.sum(dyf, axis=0, keepdims=True),
                jnp.zeros((4, width), F32),
            ),
            axis=0,
        )
    return hbm_call(
        "own_part", body, (params,),
        (
            SD((rows_own, width), BF), SD((padded, width), F32), SD((groups + 8, width), F32),
            SD((8, hid), F32),
        )
        + (SD((feat, padded), BF),) * 4,
        raw_ins=(h_all,),
        near_ins=(*packs, *pieces, *o_ts, ids, dy),
        near_outs=(both, both),
        smem=(sides,),
        scratch=[
            pltpu.VMEM((2, 2 * hid, width), BF), pltpu.SemaphoreType.DMA((8,)),
            pltpu.VMEM((4, padded, hid), BF), pltpu.VMEM((4, padded, hid), BF),
            pltpu.VMEM((padded, width), BF), pltpu.SemaphoreType.DMA((1,)),
        ],
        limit=40, flops=10_000_000_000, nbytes=16_000_000,
    )


def mark(value):
    def body(_, ins, raw_i, outs, raw_o, own):
        outs[0].ref[...] = jnp.zeros_like(outs[0].ref)

    (out,) = hbm_call(
        "mark", body, (value[:8, :128].astype(F32),), (SD((8, 128), F32),),
        limit=4, flops=20_000_000_000, nbytes=1_000,
    )
    return out


def back_heads(heads, first, d_out, q_v, probs, o32, rl, dqkv, d_s, p_all, p_sem, ready, late):
    tokens = q_v.shape[1]
    spans = [(h, at) for h in range(heads) for at in ((slice(0, tokens),) if h == 0 else (slice(0, tokens),))]
    fetches = [
        pltpu.make_async_copy(probs.at[first + h, at, :], p_all.at[h, at, :], p_sem.at[i])
        for i, (h, at) in enumerate(spans)
    ]
    begins = {(h, at.start): f for (h, at), f in zip(spans, fetches)}
    fetches[0].start()
    ready(lambda: [f.start() for f in fetches[1:]])
    d_out = d_out()
    sub = lax.broadcasted_iota(jnp.int32, (16, tokens), 0)
    ones = jnp.where(sub < 3, 1.0, 0.0).astype(BF)
    zero = jnp.zeros((13, tokens), F32)
    for h in range(heads):
        at = h * 3 * HEAD
        do_s = (d_out[h * HEAD : (h + 1) * HEAD, :].astype(F32) * rl[first + h : first + h + 1, :]).astype(BF)
        delta = -jnp.sum(
            do_s.astype(F32) * o32[h * HEAD : (h + 1) * HEAD, :], axis=0, keepdims=True
        )
        d_hi = delta.astype(BF).astype(F32)
        d_mid = (delta - d_hi).astype(BF).astype(F32)
        d_low = delta - d_hi - d_mid
        tail = jnp.concatenate((d_hi, d_mid, d_low, zero), axis=0).astype(BF)
        do_x = jnp.concatenate((do_s, tail), axis=0)
        q_h = q_v[at : at + HEAD, :]
        k_h = q_v[at + HEAD : at + 2 * HEAD, :]
        v_x = jnp.concatenate((q_v[at + 2 * HEAD : at + 3 * HEAD, :], ones), axis=0)
        for b in range(tokens // QB):
            cols = slice(b * QB, (b + 1) * QB)
            if (h, b * QB) in begins:
                begins[h, b * QB].wait()
                if h == 0:
                    late()
            dp = mm(do_x[:, cols], v_x, TN)
            ds = (p_all[h, cols, :].astype(F32) * dp).astype(BF)
            d_s[cols, :] = ds
            dqkv[at : at + HEAD, cols] = (0.125 * mm(k_h, ds, NT)).astype(BF)
        dqkv[at + HEAD : at + 2 * HEAD, :] = (0.125 * mm(q_h, d_s[...], NN)).astype(BF)
        dqkv[at + 2 * HEAD : at + 3 * HEAD, :] = mm(do_s, p_all[h], NN).astype(BF)


def back_scratch(heads, tokens):
    return [
        pltpu.VMEM((tokens, tokens), BF),
        pltpu.VMEM((heads, tokens, tokens), BF),
        pltpu.SemaphoreType.DMA((heads + 1,)),
        pltpu.VMEM((3 * heads * HEAD, tokens), BF),
        pltpu.SemaphoreType.DMA((2,)),
        pltpu.VMEM((heads * HEAD, tokens), F32),
    ]


def back_1(heads, d_out, a1, qkv, probs, o32, rl):
    tokens, width = a1.shape
    rows = heads * 3 * HEAD

    def body(_, ins, raw_i, outs, raw_o, own):
        d_s, p_all, p_sem, q_v, q_sem, o_v = own
        gets = (
            pltpu.make_async_copy(raw_i[1].at[:rows, :], q_v, q_sem.at[0]),
            pltpu.make_async_copy(raw_i[2].at[: heads * HEAD, :], o_v, q_sem.at[1]),
        )

        def ready(more):
            ins[0].start()
            for get in gets:
                get.start()
            more()
            ins[0].wait()
            for get in gets:
                get.wait()

        dqkv, do_rest, dw = outs[0], outs[1], raw_o[0]
        do_rest.ref[...] = raw_i[3][heads * HEAD :, :]
        do_rest.start()
        back_heads(
            heads, 0, lambda: raw_i[3], q_v, raw_i[0], o_v, ins[0].ref, dqkv.ref, d_s, p_all, p_sem, ready,
            ins[1].start,
        )
        dqkv.start()
        dw[...] = mm(dqkv.ref[...], ins[1].wait()[...], NN).astype(BF)

    return hbm_call(
        "back_1", body, (rl, a1),
        (SD((rows, tokens), BF), SD((d_out.shape[0] - heads * HEAD, tokens), BF)),
        near_outs=(SD((rows, width), BF),),
        raw_ins=(probs, qkv, o32),
        near_ins=(d_out,),
        scratch=back_scratch(heads, tokens),
        limit=32, flops=14_000_000_000, nbytes=18_000_000, eager=False,
    )


def back_2(me, groups, heads, do_rest, ids, h_all, a1, qkv, probs, o32, rl, params, w_t, dqkv_1, small_own, db_up):
    tokens, width = a1.shape
    padded = tokens // 4
    cut = dqkv_1.shape[0]
    rows = w_t.shape[0] - cut

    def body(smem, ins, raw_i, outs, raw_o, own):
        d_s, p_all, p_sem, q_v, q_sem, o_v, dqkv = own
        gets = (
            pltpu.make_async_copy(raw_i[1].at[cut:, :], q_v, q_sem.at[0]),
            pltpu.make_async_copy(raw_i[2].at[cut // 3 :, :], o_v, q_sem.at[1]),
        )

        def ready(more):
            ins[8].start()
            ins[0].start()
            for get in gets:
                get.start()
            more()
            ins[0].wait()
            for get in gets:
                get.wait()

        back_heads(
            heads, cut // (3 * HEAD), lambda: ins[8].wait()[...], q_v, raw_i[0], o_v, ins[0].ref, dqkv,
            d_s, p_all, p_sem, ready, lambda: [feed.start() for feed in ins[1:8]],
        )
        dw, send, keep, small = raw_o
        shard = smem[0][0]
        dw[...] = mm(dqkv[...], ins[1].wait()[...], NN).astype(BF)
        w_v, d1, par = ins[2].wait(), ins[3].wait(), ins[4].wait()
        ones = jnp.ones((8, tokens), BF)
        small[groups + 8 :, :] = jnp.zeros((8, width), F32)
        db = jnp.concatenate((mm(ones, d1[...], NT)[0:1], mm(ones, dqkv[...], NT)[0:1]), axis=1)
        small[pl.ds(groups + 8 + shard, 1), : cut + rows] = db
        hid = ins[7].ref.shape[1]
        up_v = ins[7].wait()
        for s in range(4):
            at = s * hid
            small[
                groups + 6 + at // width : groups + 7 + at // width, at % width : at % width + hid
            ] = up_v[pl.ds(jnp.bitwise_xor(shard, s), 1), :]
        gain = par[0:1, :]
        table = jnp.zeros((groups, width), F32)
        dgain = jnp.zeros((1, width), F32)
        dbias = jnp.zeros((1, width), F32)
        order = (3, 1, 2, 0)

        def product(j):
            at = slice(j * padded, (j + 1) * padded)
            return mm(d1[:, at], w_v[:cut, :], TN) + mm(dqkv[:, at], w_v[cut:, :], TN)

        da1 = product(order[0])
        for n, j in enumerate(order):
            later = product(order[n + 1]) if n < 3 else None
            at = slice(j * padded, (j + 1) * padded)
            normed, rstd = norm_rows(ins[5].wait()[at, :].astype(F32))
            back = norm_back(da1, normed, rstd, gain)
            (keep, send)[j % 2][j // 2 * padded : (j // 2 + 1) * padded, :] = back.astype(BF)
            dgain = dgain + jnp.sum(da1 * normed, axis=0, keepdims=True)
            dbias = dbias + jnp.sum(da1, axis=0, keepdims=True)
            table = table + onehot_sum(onehot_rows(raw_i[3 + j][0:1, :], groups), back)
            da1 = later
        first = ins[6].wait()
        small[0:groups, :] = table + first[0:groups, :]
        small[groups : groups + 4, :] = first[groups : groups + 4, :]
        small[groups + 4 : groups + 6, :] = jnp.concatenate((dgain, dbias), axis=0)

    return hbm_call(
        "back_2", body, (rl, a1, w_t, dqkv_1, params, h_all, small_own, db_up, do_rest), (),
        near_outs=(
            SD((rows, width), BF), SD((2 * padded, width), BF), SD((2 * padded, width), BF),
            SD((groups + 16, width), F32),
        ),
        smem=(me,),
        raw_ins=(probs, qkv, o32),
        near_ins=ids,
        scratch=back_scratch(heads, tokens)
        + [pltpu.VMEM((rows, tokens), BF)],
        limit=34, flops=10_000_000_000, nbytes=18_000_000, eager=False,
    )


def swap(arr, axis, bit):
    size = lax.axis_size(axis)
    return lax.ppermute(arr, axis, [(i, i ^ bit) for i in range(size)])


def add(a, b):
    return (a.astype(F32) + b.astype(F32)).astype(a.dtype)


def after(value, *others):
    return lax.optimization_barrier((value, others))[0]


def side_of(bit):
    return (lax.axis_index("dp") // bit) % 2


def dp_bits():
    bits, bit = [], 1
    while bit < lax.axis_size("dp"):
        bits.append(bit)
        bit *= 2
    return bits


def sync(*values):
    return lax.optimization_barrier(values)


def plus(a, b):
    return (a.astype(F32) + b.astype(F32)).astype(BF)


def stage(name, sides, ins, outs, body, scratch=(), flops=100_000):
    near = pl.BlockSpec(memory_space=pltpu.VMEM)

    def kernel(side, *refs):
        body(side[0], side[1], refs[: len(ins)], refs[len(ins) :])

    return pl.pallas_call(
        kernel,
        out_shape=tuple(SD(shape, dtype) for shape, dtype in outs),
        in_specs=[pl.BlockSpec(memory_space=pltpu.SMEM)] + [near] * len(ins),
        out_specs=(near,) * len(outs),
        scratch_shapes=[pltpu.VMEM(shape, dtype) for shape, dtype in scratch],
        compiler_params=pltpu.CompilerParams(vmem_limit_bytes=16 * 2**20),
        cost_estimate=pl.CostEstimate(flops=flops, bytes_accessed=1_000, transcendentals=0),
        name=name,
    )(sides, *ins)


def per_device(
    block_input, group_ids, intr_table, ln1_gain, ln1_bias, w_qkv, b_qv, w_out, b_out,
    ln2_gain, ln2_bias, w_up, b_up, w_down, b_down, cotangent,
):
    rows_own, width = block_input.shape
    padded = -(-rows_own // 128) * 128
    groups = intr_table.shape[0]
    feat, hid = w_out.shape[0], w_down.shape[0]
    heads = feat // HEAD
    me = lax.axis_index("mp")
    bits = dp_bits()

    id_row = jnp.pad(group_ids.astype(F32)[None, :], ((0, 7), (0, padded - rows_own)), constant_values=-1)
    x_x = swap(block_input, "mp", 2)
    x_c = swap(block_input, "mp", 1)
    ids_x = swap(id_row, "mp", 2)
    ids_c = swap(id_row, "mp", 1)

    zero_row = jnp.zeros((width,), F32)
    b_three = jnp.stack((b_qv[0], jnp.zeros((feat,), F32), b_qv[1]), axis=0)
    b_row = b_three.reshape(3, heads, HEAD).transpose(1, 0, 2).reshape(3 * feat)
    params = jnp.stack(
        (
            ln1_gain, ln1_bias, b_out, ln2_gain, ln2_bias, b_down,
            jnp.pad(b_row, (0, width - 3 * feat)), zero_row,
        ),
        axis=0,
    )
    w_t = (
        w_qkv.reshape(width, 3, heads, HEAD).transpose(2, 1, 3, 0).reshape(3 * feat, width)
    )
    b_rows = jnp.stack(three_parts(b_up), axis=0)
    pack = jnp.concatenate(
        (w_out, jnp.pad(b_rows, ((0, EXTRA - 3), (0, width - hid))), w_up.T, w_down), axis=0
    )
    up_at, down_at, half = feat + EXTRA, feat + EXTRA + hid, hid // 2
    side_u, side_d = side_of(bits[0]), side_of(bits[1])
    sides = jnp.stack((side_u, side_d))
    dy = jnp.pad(cotangent, ((0, padded - rows_own), (0, 0)))
    x_x, ids_x, first_rows, params, w_t, up_near, down_near, dy, _ = sync(
        x_x, ids_x, pack[:up_at], params, w_t,
        lax.dynamic_slice_in_dim(pack, up_at + side_u * half, half, 0),
        lax.dynamic_slice_in_dim(pack, down_at + side_d * half, half, 0), dy, mark(pack),
    )
    x_xc, ids_xc = swap(x_x, "mp", 1), swap(ids_x, "mp", 1)
    up_near, down_near = swap(up_near, "mp", 2), swap(down_near, "mp", 2)
    out_x = swap(first_rows, "mp", 2)
    pack_c = swap(after(pack, x_x), "mp", 1)
    ids = (id_row, ids_c, ids_x, ids_xc)
    a1, qkv, h_all, o32, rl, *o_ts, probs = attend(
        padded, block_input, (x_c, x_x, x_xc), ids, intr_table, params, w_t
    )

    o_own, o_c, o_two = o_ts
    up_near, down_near, out_x, o_own = sync(up_near, down_near, out_x, o_own)
    o_c, o_two, up_far, down_far, _ = sync(
        swap(o_c, "mp", 1), swap(o_two, "mp", 2),
        swap(up_near, "dp", bits[0]), swap(down_near, "dp", bits[1]), mark(rl),
    )
    o_ts = (o_own, o_c, o_two[0], swap(o_two[1], "mp", 1))
    pieces = (out_x, up_near, up_far, down_near, down_far)
    pieces = pieces + tuple(swap(p, "mp", 1) for p in pieces)
    mixed, dh1, small_own, db_up, *do_ts, keep_g, send_g = own_part(
        rows_own, groups, (hid, feat), sides, h_all, id_row, dy, params,
        (pack, pack_c), pieces, o_ts,
    )
    do_own = do_ts[0]
    first, second, full, *rest = bits
    do_c, do_x, do_xc, got_g, _ = sync(
        *(swap(do_ts[j], "mp", j) for j in (1, 2, 3)), swap(send_g, "mp", 1), mark(small_own)
    )

    w = width
    n_a, n_b, n_c, n_q, n_r = hid // 4, hid // 4, feat // 4, 2 * feat // 4, feat // 4

    def stage_0(u, d, ins, outs):
        keep, got = ins[:2]
        a_sent, a_kept, b_sent, b_kept, c_sent, c_kept, d_out = outs
        for j in range(4):
            d_out[:, j * padded : (j + 1) * padded] = ins[2 + j][...]
        a_sent[...] = plus(keep[1, :hid], got[1, :hid])
        a_kept[...] = plus(keep[0, :hid], got[0, :hid])
        for out, side in ((b_sent, 1 - u), (b_kept, u)):
            for z in range(2):
                rows = pl.ds(pl.multiple_of(hid + (2 * side + z) * n_b, 16), n_b)
                out[:, 0, z] = plus(keep[:, rows], got[:, rows])
        for out, side in ((c_sent, 1 - d), (c_kept, d)):
            for y in range(2):
                rows = pl.ds(pl.multiple_of(2 * hid + (2 * y + side) * n_c, 16), n_c)
                out[:, y, 0] = plus(keep[:, rows], got[:, rows])

    a_sent, a_kept, b_sent, b_kept, c_sent, c_kept, d_out = stage(
        "stage_0", sides, (keep_g, got_g, do_own, do_c, do_x, do_xc),
        [((hid, w), BF)] * 2 + [((2, 1, 2, n_b, w), BF)] * 2 + [((2, 2, 1, n_c, w), BF)] * 2
        + [((feat, 4 * padded), BF)],
        stage_0,
    )
    a_got, b_got, c_got = swap(a_sent, "mp", 2), swap(b_sent, "dp", first), swap(c_sent, "dp", second)
    d_out, a_kept, b_kept, c_kept = sync(d_out, a_kept, b_kept, c_kept)
    dqkv_1, do_rest, dw_1 = back_1(heads - 1, d_out, a1, qkv, probs, o32, rl)

    def stage_1(u, d, ins, outs):
        a_kept, a_got, b_kept, b_got, q, c_kept, c_got = ins
        for k, at in enumerate((pl.ds(1 - u, 1), pl.ds(u, 1))):
            outs[k][:, :, :n_a] = plus(a_kept[at], a_got[at])
            outs[k][:, :, n_a:] = q[at]
        for k, at in enumerate((pl.ds(1 - d, 1), pl.ds(d, 1))):
            outs[2 + k][...] = plus(b_kept[:, :, at], b_got[:, :, at])
            outs[4 + k][...] = plus(c_kept[1 - k], c_got[1 - k])

    cut_a, cut_q, cut_r = (2, 2, n_a, w), (2, 2, n_q, w), (2, 2, n_r, w)
    n_aq = n_a + n_q
    aq_sent, aq_kept, b_sent, b_kept, c_sent, c_kept = stage(
        "stage_1", sides,
        (a_kept.reshape(cut_a), a_got.reshape(cut_a), b_kept, b_got, dw_1.reshape(cut_q), c_kept, c_got),
        [((1, 2, n_aq, w), BF)] * 2 + [((2, 1, 1, n_b, w), BF)] * 2 + [((2, 1, n_c, w), BF)] * 2,
        stage_1,
    )
    aq_got, b_got, c_got = swap(aq_sent, "dp", first), swap(b_sent, "dp", second), swap(c_sent, "mp", 2)
    aq_kept, b_kept, c_kept, dqkv_1 = sync(aq_kept, b_kept, c_kept, dqkv_1)
    dw_2, send, keep, small = back_2(
        me.reshape(1), groups, 1, do_rest, ids, h_all, a1, qkv, probs, o32, rl, params, w_t, dqkv_1,
        small_own, db_up,
    )
    aq_got, b_got, c_got, dw_2, send, keep, small = sync(
        aq_got, b_got, c_got, dw_2, send, keep, small
    )

    def stage_2(u, d, ins, outs):
        aq_kept, aq_got, b_kept, b_got, r, c_kept, c_got = ins
        for k, at in enumerate((pl.ds(1 - d, 1), pl.ds(d, 1))):
            outs[k][...] = plus(aq_kept[:, at], aq_got[:, at])
        for k in range(2):
            outs[2 + k][...] = plus(b_kept[1 - k], b_got[1 - k])
        for k, at in enumerate((pl.ds(1 - u, 1), pl.ds(u, 1))):
            outs[4 + k][...] = r[at]
            outs[6 + k][...] = plus(c_kept[at], c_got[at])

    aq_sent, aq_kept, b_sent, b_kept, r_sent, r_kept, c_sent, c_kept = stage(
        "stage_2", sides, (aq_kept, aq_got, b_kept, b_got, dw_2.reshape(cut_r), c_kept, c_got),
        [((1, 1, n_aq, w), BF)] * 2 + [((1, 1, n_b, w), BF)] * 2 + [((1, 2, n_r, w), BF)] * 2
        + [((1, 1, n_c, w), BF)] * 2,
        stage_2,
    )
    aq_got, b_got, r_got, t_got = (
        swap(aq_sent, "dp", second), swap(b_sent, "mp", 2), swap(r_sent, "dp", first),
        swap(send, "mp", 1),
    )
    s_got = [swap(small, "mp", bit) for bit in (1, 2, 3)]

    def stage_3(u, d, ins, outs):
        aq_kept, aq_got, b_kept, b_got, r_kept, r_got, keep, t_got = ins[:8]
        s_0, s_1, s_2, s_3, c_sent = ins[8:]
        outs[7][...] = c_sent[...]
        outs[0][:, :, :n_a] = plus(aq_kept[:, :, :n_a], aq_got[:, :, :n_a])
        outs[0][:, :, n_a:] = plus(b_kept[...], b_got[...])
        outs[1][...] = plus(aq_kept[:, :, n_a:], aq_got[:, :, n_a:])
        for k, at in enumerate((pl.ds(1 - d, 1), pl.ds(d, 1))):
            outs[2 + k][...] = plus(r_kept[:, at], r_got[:, at])
        outs[4][...] = plus(keep[padded:], t_got[padded:])
        outs[5][...] = plus(keep[:padded], t_got[:padded])
        outs[6][...] = (s_0[...] + s_1[...]) + (s_2[...] + s_3[...])

    one_a, one_b, one_c, one_q, one_r = ((1, 1, n, w) for n in (n_a, n_b, n_c, n_q, n_r))
    ab, q, r_sent, r_kept, t_sent, t_kept, small, c_sent = stage(
        "stage_3", sides,
        (aq_kept, aq_got, b_kept, b_got, r_kept, r_got, keep, t_got,
         small, *s_got, c_sent),
        [((1, 1, n_a + n_b, w), BF), (one_q, BF), (one_r, BF), (one_r, BF)]
        + [((padded, w), BF)] * 2 + [(small.shape, F32), (one_c, BF)],
        stage_3,
    )
    ab_got, r_got, t_got, s_got = (
        swap(ab, "dp", full), swap(r_sent, "dp", second), swap(t_sent, "mp", 2),
        swap(small, "dp", first),
    )
    c_got = swap(c_sent, "dp", first)

    def stage_4(u, d, ins, outs):
        ab, ab_got, q, r_kept, r_got, small, s_got, c_kept, c_got, _ = ins
        outs[0][...] = plus(ab[:, :, :n_a], ab_got[:, :, :n_a])
        outs[1][...] = plus(ab[:, :, n_a:], ab_got[:, :, n_a:])
        outs[2][:, :, :n_q] = q[...]
        outs[2][:, :, n_q : n_q + n_r] = plus(r_kept[...], r_got[...])
        outs[2][:, :, n_q + n_r :] = plus(c_kept[...], c_got[...])
        outs[3][...] = small[...] + s_got[...]

    a, b, q, small = stage(
        "stage_4", sides, (ab, ab_got, q, r_kept, r_got, small, s_got, c_kept, c_got, t_got),
        [(one_a, BF), (one_b, BF), ((1, 1, n_q + n_r + n_c, w), BF), ((groups + 16, w), F32)], stage_4,
    )
    for bit in rest:
        small = small + swap(small, "dp", bit)
        a, b = plus(a, swap(a, "dp", bit)), plus(b, swap(b, "dp", bit))
    a_got, b_got, q_got, s_got = (
        swap(a, "dp", first), swap(b, "dp", second), swap(q, "dp", full), swap(small, "dp", second)
    )
    dh0 = dh1 + t_kept.astype(F32) + t_got.astype(F32)
    input_grad = dh0[:rows_own].astype(BF)
    q_got = after(q_got, input_grad)
    h = (n_q + n_r + n_c) // 32 * 16
    h_1 = n_q + n_r + n_c - h

    def stage_5(u, d, ins, outs):
        a, a_got, b, b_got, q, q_got, small, s_got = ins
        a_o, b_o, q_0, q_1, s_o = outs
        a_o[pl.ds(u, 1)] = a[...]
        a_o[pl.ds(1 - u, 1)] = a_got[...]
        b_o[:, pl.ds(d, 1)] = b[...]
        b_o[:, pl.ds(1 - d, 1)] = b_got[...]
        q_0[...] = plus(q[:, :, :h], q_got[:, :, :h])
        q_1[...] = plus(q[:, :, h:], q_got[:, :, h:])
        s_o[...] = small[...] + s_got[...]

    a, b, q_0, q_1, small = stage(
        "stage_5", sides, (a, a_got, b, b_got, q, q_got, small, s_got),
        [((2, 1, n_a, w), BF), ((1, 2, n_b, w), BF), ((1, 1, h, w), BF), ((1, 1, h_1, w), BF),
         (small.shape, F32)],
        stage_5,
    )
    for bit in rest:
        q_0, q_1 = plus(q_0, swap(q_0, "dp", bit)), plus(q_1, swap(q_1, "dp", bit))
    a_got, b_got, q_0_got, q_1_got, s_got = (
        swap(a, "dp", second), swap(b, "dp", first), swap(q_0, "dp", first), swap(q_1, "dp", second),
        swap(small, "dp", full),
    )

    def stage_6(u, d, ins, outs):
        q_0, q_0_got, q_1, q_1_got, small, s_got = ins
        q_0_o, q_1_o, s_o = outs
        s_o[...] = small[...] + s_got[...]
        q_0_o[pl.ds(u, 1)] = q_0[...]
        q_0_o[pl.ds(1 - u, 1)] = q_0_got[...]
        q_1_o[:, pl.ds(d, 1)] = q_1[...]
        q_1_o[:, pl.ds(1 - d, 1)] = q_1_got[...]

    q_0, q_1, small = stage(
        "stage_6", sides, (q_0, q_0_got, q_1, q_1_got, small, s_got),
        [((2, 1, h, w), BF), ((1, 2, h_1, w), BF), (small.shape, F32)], stage_6,
    )
    q_0_got, q_1_got = swap(q_0, "dp", second), swap(q_1, "dp", first)

    def stage_7(u, d, ins, outs):
        a, a_got, b, b_got = ins[:4]
        up_o, down_o, chunk_a = outs
        for y in range(2):
            for z, src in ((d, a), (1 - d, a_got)):
                at = pl.multiple_of((2 * y + z) * n_a, 16)
                chunk_a[pl.ds(at, n_a), :] = src[y, 0].astype(F32)
        for z in range(2):
            for y, src in ((u, b), (1 - u, b_got)):
                at = pl.multiple_of((2 * y + z) * n_b, 16)
                down_o[pl.ds(at, n_b), :] = src[0, z].astype(F32)
        up_o[...] = jnp.transpose(chunk_a[...])

    g_up, g_down = stage(
        "stage_7", sides, (a, a_got, b, b_got, q_0),
        [((w, hid), F32), ((hid, w), F32)], stage_7, [((hid, w), F32)], 20_000_000_000,
    )

    def doubled(cur, got, side, axis):
        return jnp.where(
            side == 0,
            jnp.concatenate((cur, got), axis=axis),
            jnp.concatenate((got, cur), axis=axis),
        )

    q_all = jnp.concatenate(
        (doubled(q_0, q_0_got, side_d, 1), doubled(q_1, q_1_got, side_u, 0)), axis=2
    )
    g_qkv = jnp.concatenate(
        (q_all[:, :, :n_q].reshape(-1, w), q_all[:, :, n_q : n_q + n_r].reshape(-1, w)), axis=0
    )
    g_out = q_all[:, :, n_q + n_r :].reshape(-1, w).astype(F32)
    at = groups
    up_at = at + 6
    qv_at = at + 8
    b_up_grad = lax.dynamic_slice(small[up_at:qv_at].reshape(4, hid), (me, 0), (1, hid))[0]
    db = lax.dynamic_slice(small, (qv_at + me, 0), (1, 3 * feat)).reshape(heads, 3, HEAD)
    b_qv_grad = jnp.stack((db[:, 0].reshape(feat), db[:, 2].reshape(feat)), axis=0)
    g_qkv = g_qkv.astype(F32)
    w_qkv_grad = (
        g_qkv.reshape(heads, 3, HEAD, width).transpose(3, 1, 0, 2).reshape(width, 3, feat)
    )
    return (
        mixed,
        input_grad,
        small[:groups],
        small[at + 4],
        small[at + 5],
        w_qkv_grad,
        b_qv_grad,
        g_out,
        small[at],
        small[at + 1],
        small[at + 2],
        g_up,
        b_up_grad,
        g_down,
        small[at + 3],
    )


def solution(mesh):
    rows = P(("dp", "mp"), None)
    return jax.shard_map(
        per_device,
        mesh=mesh,
        in_specs=(
            rows, P(("dp", "mp")), P(), P(), P(), P(None, None, "mp"), P(None, "mp"), P("mp", None),
            P(), P(), P(), P(None, "mp"), P("mp"), P("mp", None), P(), rows,
        ),
        out_specs=(
            rows, rows, P(), P(), P(), P(None, None, "mp"), P(None, "mp"), P("mp", None),
            P(), P(), P(), P(None, "mp"), P("mp"), P("mp", None), P(),
        ),
        check_vma=False,
    )
```

```python
import jax
import jax.numpy as jnp
from jax import lax
from jax.experimental import pallas as pl
from jax.experimental.pallas import tpu as pltpu
from jax.sharding import PartitionSpec as P

HEAD = 64
BF = jnp.bfloat16
F32 = jnp.float32
LOG2E = 1.4426950408889634
NN = (((1,), (0,)), ((), ()))
NT = (((1,), (1,)), ((), ()))
TN = (((0,), (0,)), ((), ()))
QB = 256
SD = jax.ShapeDtypeStruct
SAFE = 3000.0
EXTRA = 32


def mm(a, b, dims):
    return lax.dot_general(a, b, dims, preferred_element_type=F32)


def three_parts(v):
    hi = v.astype(BF)
    rest = v - hi.astype(F32)
    mid = rest.astype(BF)
    low = (rest - mid.astype(F32)).astype(BF)
    return hi, mid, low


def norm_rows(rows):
    centre = rows - jnp.mean(rows, axis=-1, keepdims=True)
    var = jnp.mean(centre * centre, axis=-1, keepdims=True)
    rstd = lax.rsqrt(var + 1e-05)
    return centre * rstd, rstd


def norm_back(grad, normed, rstd, gain):
    scaled = grad * gain
    return rstd * (
        scaled
        - jnp.mean(scaled, axis=-1, keepdims=True)
        - normed * jnp.mean(scaled * normed, axis=-1, keepdims=True)
    )


def gelu_parts(u):
    square = u * u
    t = jnp.tanh(0.7978845608028654 * (u + 0.044715 * (u * square)))
    half = 0.5 * (1.0 + t)
    slope = half + 0.5 * u * (1.0 - t * t) * (
        0.7978845608028654 + (3 * 0.044715 * 0.7978845608028654) * square
    )
    return u * half, slope


def onehot_rows(ids_row, groups):
    levels = lax.broadcasted_iota(jnp.int32, (groups, ids_row.shape[1]), 0).astype(F32)
    return (levels == ids_row).astype(F32).astype(BF)


def onehot_sum(hot, rows):
    hi = rows.astype(BF)
    low = (rows - hi.astype(F32)).astype(BF)
    return mm(hot, hi, NN) + mm(hot, low, NN)


class Copy:
    def __init__(self, src, dst, sem, near):
        self.copy = pltpu.make_async_copy(src, dst, sem)
        self.ref = near
        self.begun = False
        self.ended = False

    def start(self):
        if not self.begun:
            self.begun = True
            self.copy.start()
        return self

    def wait(self):
        self.start()
        if not self.ended:
            self.ended = True
            self.copy.wait()
        return self.ref


def hbm_call(
    name, body, ins, outs, *, raw_ins=(), raw_outs=(), near_ins=(), near_outs=(), smem=(), scratch=(),
    limit, flops, nbytes, eager=True,
):
    hbm = pl.BlockSpec(memory_space=pltpu.HBM)
    n_i, n_o = len(ins), len(outs)

    def kernel(*refs):
        rest = list(refs)

        def take(n):
            got = rest[:n]
            del rest[:n]
            return got

        small = take(len(smem))
        far_i, raw_i = take(n_i), take(len(raw_ins))
        raw_i = raw_i + take(len(near_ins))
        far_o, raw_o = take(n_o), take(len(raw_outs) + len(near_outs))
        near_i, near_o = take(n_i), take(n_o)
        own = take(len(scratch))
        sem_i, sem_o = take(2)
        feeds = [Copy(f, n, sem_i.at[k], n) for k, (f, n) in enumerate(zip(far_i, near_i))]
        sinks = [Copy(n, f, sem_o.at[k], n) for k, (f, n) in enumerate(zip(far_o, near_o))]
        if eager:
            for feed in feeds:
                feed.start()
        body(small, feeds, raw_i, sinks, raw_o, own)
        for sink in sinks:
            sink.start()
        for sink in sinks:
            sink.wait()
        for feed in feeds:
            feed.wait()

    vmem = lambda a: pltpu.VMEM(a.shape, a.dtype)
    return pl.pallas_call(
        kernel,
        out_shape=tuple(pltpu.HBM(s.shape, s.dtype) for s in (*outs, *raw_outs)) + tuple(near_outs),
        in_specs=[pl.BlockSpec(memory_space=pltpu.SMEM)] * len(smem)
        + [hbm] * (n_i + len(raw_ins))
        + [pl.BlockSpec(memory_space=pltpu.VMEM)] * len(near_ins),
        out_specs=(hbm,) * (n_o + len(raw_outs))
        + (pl.BlockSpec(memory_space=pltpu.VMEM),) * len(near_outs),
        scratch_shapes=[vmem(a) for a in ins]
        + [vmem(a) for a in outs]
        + list(scratch)
        + [pltpu.SemaphoreType.DMA((n_i,)), pltpu.SemaphoreType.DMA((max(n_o, 1),))],
        compiler_params=pltpu.CompilerParams(vmem_limit_bytes=limit * 2**20),
        cost_estimate=pl.CostEstimate(flops=flops, bytes_accessed=nbytes, transcendentals=0),
        name=name,
    )(*smem, *[pltpu.with_memory_space_constraint(a, pltpu.HBM) for a in (*ins, *raw_ins)], *near_ins)


def forward_heads(heads, first, rows_own, qkv, probs, o32, rl, p_buf, p_sem):
    tokens = qkv.shape[1]
    padded = tokens // 4
    lane = lax.broadcasted_iota(jnp.int32, (16, tokens), 1)
    sub = lax.broadcasted_iota(jnp.int32, (16, tokens), 0)
    valid = jnp.zeros((16, tokens), jnp.bool_)
    for j in range(4):
        valid = valid | ((lane >= j * padded) & (lane < j * padded + rows_own))
    top_row = sub == 0
    mask = jnp.where(top_row & ~valid, -1e30, 0.0).astype(BF)
    ones = jnp.where(top_row, 1.0, 0.0).astype(BF)
    parts = []
    bound = jnp.float32(0.0)
    for h in range(heads):
        at = 3 * (first + h) * HEAD
        scaled = qkv[at : at + HEAD, :].astype(F32) * (0.125 * LOG2E)
        hi = scaled.astype(BF)
        low = (scaled - hi.astype(F32)).astype(BF)
        k_h = qkv[at + HEAD : at + 2 * HEAD, :]
        k_f = k_h.astype(F32)
        q_x = jnp.concatenate((hi, low, ones), axis=0)
        k_x = jnp.concatenate((k_h, k_h, mask), axis=0)
        v_x = jnp.concatenate((qkv[at + 2 * HEAD : at + 3 * HEAD, :], ones), axis=0)
        parts.append((q_x, k_x, v_x))
        bound = jnp.maximum(
            bound,
            jnp.max(jnp.sum(scaled * scaled, axis=0, keepdims=True))
            * jnp.max(jnp.sum(k_f * k_f, axis=0, keepdims=True)),
        )
    copies = [
        pltpu.make_async_copy(p_buf.at[h], probs.at[h], p_sem.at[h]) for h in range(heads)
    ]

    def run(exact):
        for h, (q_x, k_x, v_x) in enumerate(parts):
            for b in range(tokens // QB):
                cols = slice(b * QB, (b + 1) * QB)
                scores = mm(q_x[:, cols], k_x, TN)
                if exact:
                    scores = scores - jnp.max(scores, axis=-1, keepdims=True)
                p_block = jnp.exp2(scores).astype(BF)
                p_buf[h, cols, :] = p_block
                out = mm(v_x, p_block, NT)
                inv = 1.0 / out[HEAD : HEAD + 1, :]
                o32[h * HEAD : (h + 1) * HEAD, cols] = out[:HEAD, :] * inv
                rl[h : h + 1, cols] = inv
            copies[h].start()

    small = bound < SAFE

    @pl.when(small)
    def _():
        run(False)

    @pl.when(jnp.logical_not(small))
    def _():
        run(True)

    return copies


def attend(padded, x0, others, ids, table, params, w_t):
    rows_own, width = x0.shape
    tokens = 4 * padded
    rows = w_t.shape[0]
    feat = rows // 3
    heads = feat // HEAD
    groups = table.shape[0]

    def body(_, ins, raw_i, outs, raw_o, own):
        a1, qkv, h_all, o32, rl = outs[:5]
        p_buf, p_sem, x_v = own
        par = ins[2].wait()
        bias = jnp.transpose(par[...])[:rows, 6:7]
        table_v = ins[3].wait()[...]
        for pair in range(2):
            for j in (2 * pair, 2 * pair + 1):
                at = slice(j * padded, (j + 1) * padded)
                x = ins[0].wait() if j == 0 else raw_i[j - 1]
                x_v[j, padded - 16 :, :] = jnp.zeros((16, width), F32)
                x_v[j, :rows_own, :] = x[...].astype(F32)
                hot = onehot_rows(raw_i[3 + j][0:1, :], groups)
                h = (x_v[j] + mm(hot, table_v, TN)).astype(BF)
                h_all.ref[at, :] = h
                normed, _ = norm_rows(h.astype(F32))
                a1.ref[at, :] = (normed * par[0:1, :] + par[1:2, :]).astype(BF)
            cols = slice(2 * pair * padded, 2 * (pair + 1) * padded)
            qkv.ref[:, cols] = (mm(ins[1].wait()[...], a1.ref[cols, :], NT) + bias).astype(BF)
        for sink in (a1, qkv, h_all):
            sink.start()
        copies = forward_heads(heads, 0, rows_own, qkv.ref, raw_o[0], o32.ref, rl.ref, p_buf, p_sem)
        for j in range(4):
            o = o32.ref[:, j * padded : (j + 1) * padded].astype(BF)
            if j < 2:
                outs[5 + j].ref[...] = o
            else:
                outs[7].ref[j - 2] = o
        for sink in outs:
            sink.start()
        for copy in copies:
            copy.wait()

    return hbm_call(
        "attend", body, (x0, w_t, params, table),
        (
            SD((tokens, width), BF), SD((rows, tokens), BF), SD((tokens, width), BF),
            SD((feat, tokens), F32), SD((8, tokens), F32), SD((feat, padded), BF),
            SD((feat, padded), BF), SD((2, feat, padded), BF),
        ),
        raw_outs=(SD((heads, tokens, tokens), BF),),
        near_ins=(*others, *ids),
        scratch=[
            pltpu.VMEM((heads, tokens, tokens), BF), pltpu.SemaphoreType.DMA((heads,)),
            pltpu.VMEM((4, padded, width), F32),
        ],
        limit=40, flops=12_000_000_000, nbytes=25_000_000,
    )


def own_part(rows_own, groups, sizes, sides, h_all, ids, dy, params, packs, pieces, o_ts):
    hid, feat = sizes
    padded, width = dy.shape
    half = hid // 2
    both = SD((2, 2 * hid + feat, width), BF)
    blocks = 1
    step = padded // blocks

    def body(smem, ins, raw_i, outs, raw_o, own):
        w_v, w_sem, act_v, du_v, h_v, h_sem = own
        bufs = (raw_o[0], raw_o[1])
        get_h = pltpu.make_async_copy(raw_i[0].at[:padded, :], h_v, h_sem.at[0])
        get_h.start()
        packs_r, pieces_r, o_r = raw_i[1:3], raw_i[3:13], raw_i[13:17]
        ids_r, dy_r = raw_i[17], raw_i[18]
        up_at, down_at = feat + EXTRA, feat + EXTRA + hid
        loads = []
        for j in range(2):
            for k in range(4):
                s = smem[0][k // 2]
                at = (k // 2) * hid + ((1 - s) if k % 2 else s) * half
                copy = pltpu.make_async_copy(
                    pieces_r[5 * j + 1 + k], w_v.at[j, pl.ds(pl.multiple_of(at, 16), half), :],
                    w_sem.at[4 * j + k],
                )
                copy.start()
                loads.append(copy)
        heads_r = (packs_r[0], packs_r[1], pieces_r[0], pieces_r[5])
        out = slice(0, feat)

        def up_of(j):
            return packs_r[j][up_at:down_at, :] if j < 2 else w_v[j - 2, :hid, :]

        def down_of(j):
            return packs_r[j][down_at:, :] if j < 2 else w_v[j - 2, hid:, :]

        par = ins[0].wait()
        attn = par[2:3, :]
        for j in range(4):
            attn = attn + mm(o_r[j][...], heads_r[j][out, :], TN)
        get_h.wait()
        h1 = h_v[...].astype(F32) + attn
        normed, rstd = norm_rows(h1)
        a2 = (normed * par[3:4, :] + par[4:5, :]).astype(BF)
        mixed, dh1, small, db_up = outs[:4]
        dy_b = dy_r[...]
        acc = [h1[r * step : (r + 1) * step] + par[5:6, :] for r in range(blocks)]
        da2 = [jnp.zeros((step, width), F32) for _ in range(blocks)]
        parts = [slice(r * step, (r + 1) * step) for r in range(blocks)]

        def shard_grads(j):
            for at, left, right in ((0, du_v, a2), (hid, act_v, dy_b)):
                bufs[j % 2][j // 2, at : at + hid, :] = mm(left[j], right, TN).astype(BF)

        for copy in loads:
            copy.wait()
        for n, j in enumerate((1, 3, 0, 2)):
            b_rows = heads_r[j][feat : feat + 16, :].astype(F32)
            b_up = (b_rows[0:1] + b_rows[1:2] + b_rows[2:3])[:, :hid]
            us = [mm(a2[at], up_of(j), NT) + b_up for at in parts]
            dacts = [mm(dy_b[at], down_of(j), NT) for at in parts]
            if n:
                shard_grads((1, 3, 0)[n - 1])
            db = jnp.zeros((1, hid), F32)
            for r, at in enumerate(parts):
                value, slope = gelu_parts(us[r])
                act = value.astype(BF)
                acc[r] = acc[r] + mm(act, down_of(j), NN)
                du = (dacts[r] * slope).astype(BF)
                da2[r] = da2[r] + mm(du, up_of(j), NN)
                act_v[j, at, :] = act
                du_v[j, at, :] = du
                db = db + jnp.sum(du.astype(F32), axis=0, keepdims=True)
            db_up.ref[j : j + 1, :] = db
        shard_grads(2)
        da2 = jnp.concatenate(da2, axis=0)
        dyf = dy_b.astype(F32)
        total = dyf + norm_back(da2, normed, rstd, par[3:4, :])
        dattn = total.astype(BF)
        for j in range(4):
            outs[4 + j].ref[...] = mm(heads_r[j][out, :], dattn, NT).astype(BF)
            outs[4 + j].start()
        dh1.ref[...] = total
        dh1.start()
        mixed.ref[...] = jnp.concatenate(acc, axis=0)[:rows_own].astype(BF)
        mixed.start()
        for j in (1, 3, 0, 2):
            d_out = mm(o_r[j][...], dattn, NN).astype(BF)
            bufs[j % 2][j // 2, 2 * hid :, :] = d_out
        hot = onehot_rows(ids_r[0:1, :], groups)
        small.ref[0:groups, :] = onehot_sum(hot, total)
        small.ref[groups : groups + 8, :] = jnp.concatenate(
            (
                jnp.sum(dattn.astype(F32), axis=0, keepdims=True),
                jnp.sum(da2 * normed, axis=0, keepdims=True),
                jnp.sum(da2, axis=0, keepdims=True),
                jnp.sum(dyf, axis=0, keepdims=True),
                jnp.zeros((4, width), F32),
            ),
            axis=0,
        )
    return hbm_call(
        "own_part", body, (params,),
        (
            SD((rows_own, width), BF), SD((padded, width), F32), SD((groups + 8, width), F32),
            SD((8, hid), F32),
        )
        + (SD((feat, padded), BF),) * 4,
        raw_ins=(h_all,),
        near_ins=(*packs, *pieces, *o_ts, ids, dy),
        near_outs=(both, both),
        smem=(sides,),
        scratch=[
            pltpu.VMEM((2, 2 * hid, width), BF), pltpu.SemaphoreType.DMA((8,)),
            pltpu.VMEM((4, padded, hid), BF), pltpu.VMEM((4, padded, hid), BF),
            pltpu.VMEM((padded, width), BF), pltpu.SemaphoreType.DMA((1,)),
        ],
        limit=40, flops=10_000_000_000, nbytes=16_000_000,
    )


def mark(value):
    def body(_, ins, raw_i, outs, raw_o, own):
        outs[0].ref[...] = jnp.zeros_like(outs[0].ref)

    (out,) = hbm_call(
        "mark", body, (value[:8, :128].astype(F32),), (SD((8, 128), F32),),
        limit=4, flops=20_000_000_000, nbytes=1_000,
    )
    return out


def back_heads(heads, first, d_out, q_v, probs, o32, rl, dqkv, d_s, p_all, p_sem, ready, late):
    tokens = q_v.shape[1]
    spans = [(h, at) for h in range(heads) for at in ((slice(0, tokens),) if h == 0 else (slice(0, tokens),))]
    fetches = [
        pltpu.make_async_copy(probs.at[first + h, at, :], p_all.at[h, at, :], p_sem.at[i])
        for i, (h, at) in enumerate(spans)
    ]
    begins = {(h, at.start): f for (h, at), f in zip(spans, fetches)}
    fetches[0].start()
    ready(lambda: [f.start() for f in fetches[1:]])
    d_out = d_out()
    sub = lax.broadcasted_iota(jnp.int32, (16, tokens), 0)
    ones = jnp.where(sub < 3, 1.0, 0.0).astype(BF)
    zero = jnp.zeros((13, tokens), F32)
    for h in range(heads):
        at = h * 3 * HEAD
        do_s = (d_out[h * HEAD : (h + 1) * HEAD, :].astype(F32) * rl[first + h : first + h + 1, :]).astype(BF)
        delta = -jnp.sum(
            do_s.astype(F32) * o32[h * HEAD : (h + 1) * HEAD, :], axis=0, keepdims=True
        )
        d_hi = delta.astype(BF).astype(F32)
        d_mid = (delta - d_hi).astype(BF).astype(F32)
        d_low = delta - d_hi - d_mid
        tail = jnp.concatenate((d_hi, d_mid, d_low, zero), axis=0).astype(BF)
        do_x = jnp.concatenate((do_s, tail), axis=0)
        q_h = q_v[at : at + HEAD, :]
        k_h = q_v[at + HEAD : at + 2 * HEAD, :]
        v_x = jnp.concatenate((q_v[at + 2 * HEAD : at + 3 * HEAD, :], ones), axis=0)
        for b in range(tokens // QB):
            cols = slice(b * QB, (b + 1) * QB)
            if (h, b * QB) in begins:
                begins[h, b * QB].wait()
                if h == 0:
                    late()
            dp = mm(do_x[:, cols], v_x, TN)
            ds = (p_all[h, cols, :].astype(F32) * dp).astype(BF)
            d_s[cols, :] = ds
            dqkv[at : at + HEAD, cols] = (0.125 * mm(k_h, ds, NT)).astype(BF)
        dqkv[at + HEAD : at + 2 * HEAD, :] = (0.125 * mm(q_h, d_s[...], NN)).astype(BF)
        dqkv[at + 2 * HEAD : at + 3 * HEAD, :] = mm(do_s, p_all[h], NN).astype(BF)


def back_scratch(heads, tokens):
    return [
        pltpu.VMEM((tokens, tokens), BF),
        pltpu.VMEM((heads, tokens, tokens), BF),
        pltpu.SemaphoreType.DMA((heads + 1,)),
        pltpu.VMEM((3 * heads * HEAD, tokens), BF),
        pltpu.SemaphoreType.DMA((2,)),
        pltpu.VMEM((heads * HEAD, tokens), F32),
    ]


def back_1(heads, d_out, a1, qkv, probs, o32, rl):
    tokens, width = a1.shape
    rows = heads * 3 * HEAD

    def body(_, ins, raw_i, outs, raw_o, own):
        d_s, p_all, p_sem, q_v, q_sem, o_v = own
        gets = (
            pltpu.make_async_copy(raw_i[1].at[:rows, :], q_v, q_sem.at[0]),
            pltpu.make_async_copy(raw_i[2].at[: heads * HEAD, :], o_v, q_sem.at[1]),
        )

        def ready(more):
            ins[0].start()
            for get in gets:
                get.start()
            more()
            ins[0].wait()
            for get in gets:
                get.wait()

        dqkv, do_rest, dw = outs[0], outs[1], raw_o[0]
        do_rest.ref[...] = raw_i[3][heads * HEAD :, :]
        do_rest.start()
        back_heads(
            heads, 0, lambda: raw_i[3], q_v, raw_i[0], o_v, ins[0].ref, dqkv.ref, d_s, p_all, p_sem, ready,
            ins[1].start,
        )
        dqkv.start()
        dw[...] = mm(dqkv.ref[...], ins[1].wait()[...], NN).astype(BF)

    return hbm_call(
        "back_1", body, (rl, a1),
        (SD((rows, tokens), BF), SD((d_out.shape[0] - heads * HEAD, tokens), BF)),
        near_outs=(SD((rows, width), BF),),
        raw_ins=(probs, qkv, o32),
        near_ins=(d_out,),
        scratch=back_scratch(heads, tokens),
        limit=32, flops=14_000_000_000, nbytes=18_000_000, eager=False,
    )


def back_2(me, groups, heads, do_rest, ids, h_all, a1, qkv, probs, o32, rl, params, w_t, dqkv_1, small_own, db_up):
    tokens, width = a1.shape
    padded = tokens // 4
    cut = dqkv_1.shape[0]
    rows = w_t.shape[0] - cut

    def body(smem, ins, raw_i, outs, raw_o, own):
        d_s, p_all, p_sem, q_v, q_sem, o_v, dqkv = own
        gets = (
            pltpu.make_async_copy(raw_i[1].at[cut:, :], q_v, q_sem.at[0]),
            pltpu.make_async_copy(raw_i[2].at[cut // 3 :, :], o_v, q_sem.at[1]),
        )

        def ready(more):
            ins[8].start()
            ins[0].start()
            for get in gets:
                get.start()
            more()
            ins[0].wait()
            for get in gets:
                get.wait()

        back_heads(
            heads, cut // (3 * HEAD), lambda: ins[8].wait()[...], q_v, raw_i[0], o_v, ins[0].ref, dqkv,
            d_s, p_all, p_sem, ready, lambda: [feed.start() for feed in ins[1:8]],
        )
        dw, send, keep, small = raw_o
        shard = smem[0][0]
        dw[...] = mm(dqkv[...], ins[1].wait()[...], NN).astype(BF)
        w_v, d1, par = ins[2].wait(), ins[3].wait(), ins[4].wait()
        ones = jnp.ones((8, tokens), BF)
        small[groups + 8 :, :] = jnp.zeros((8, width), F32)
        db = jnp.concatenate((mm(ones, d1[...], NT)[0:1], mm(ones, dqkv[...], NT)[0:1]), axis=1)
        small[pl.ds(groups + 8 + shard, 1), : cut + rows] = db
        hid = ins[7].ref.shape[1]
        up_v = ins[7].wait()
        for s in range(4):
            at = s * hid
            small[
                groups + 6 + at // width : groups + 7 + at // width, at % width : at % width + hid
            ] = up_v[pl.ds(jnp.bitwise_xor(shard, s), 1), :]
        gain = par[0:1, :]
        table = jnp.zeros((groups, width), F32)
        dgain = jnp.zeros((1, width), F32)
        dbias = jnp.zeros((1, width), F32)
        order = (3, 1, 2, 0)

        def product(j):
            at = slice(j * padded, (j + 1) * padded)
            return mm(d1[:, at], w_v[:cut, :], TN) + mm(dqkv[:, at], w_v[cut:, :], TN)

        da1 = product(order[0])
        for n, j in enumerate(order):
            later = product(order[n + 1]) if n < 3 else None
            at = slice(j * padded, (j + 1) * padded)
            normed, rstd = norm_rows(ins[5].wait()[at, :].astype(F32))
            back = norm_back(da1, normed, rstd, gain)
            (keep, send)[j % 2][j // 2 * padded : (j // 2 + 1) * padded, :] = back.astype(BF)
            dgain = dgain + jnp.sum(da1 * normed, axis=0, keepdims=True)
            dbias = dbias + jnp.sum(da1, axis=0, keepdims=True)
            table = table + onehot_sum(onehot_rows(raw_i[3 + j][0:1, :], groups), back)
            da1 = later
        first = ins[6].wait()
        small[0:groups, :] = table + first[0:groups, :]
        small[groups : groups + 4, :] = first[groups : groups + 4, :]
        small[groups + 4 : groups + 6, :] = jnp.concatenate((dgain, dbias), axis=0)

    return hbm_call(
        "back_2", body, (rl, a1, w_t, dqkv_1, params, h_all, small_own, db_up, do_rest), (),
        near_outs=(
            SD((rows, width), BF), SD((2 * padded, width), BF), SD((2 * padded, width), BF),
            SD((groups + 16, width), F32),
        ),
        smem=(me,),
        raw_ins=(probs, qkv, o32),
        near_ins=ids,
        scratch=back_scratch(heads, tokens)
        + [pltpu.VMEM((rows, tokens), BF)],
        limit=34, flops=10_000_000_000, nbytes=18_000_000, eager=False,
    )


def swap(arr, axis, bit):
    size = lax.axis_size(axis)
    return lax.ppermute(arr, axis, [(i, i ^ bit) for i in range(size)])


def add(a, b):
    return (a.astype(F32) + b.astype(F32)).astype(a.dtype)


def after(value, *others):
    return lax.optimization_barrier((value, others))[0]


def side_of(bit):
    return (lax.axis_index("dp") // bit) % 2


def dp_bits():
    bits, bit = [], 1
    while bit < lax.axis_size("dp"):
        bits.append(bit)
        bit *= 2
    return bits


def sync(*values):
    return lax.optimization_barrier(values)


def plus(a, b):
    return (a.astype(F32) + b.astype(F32)).astype(BF)


def stage(name, sides, ins, outs, body, scratch=(), flops=100_000):
    near = pl.BlockSpec(memory_space=pltpu.VMEM)

    def kernel(side, *refs):
        body(side[0], side[1], refs[: len(ins)], refs[len(ins) :])

    return pl.pallas_call(
        kernel,
        out_shape=tuple(SD(shape, dtype) for shape, dtype in outs),
        in_specs=[pl.BlockSpec(memory_space=pltpu.SMEM)] + [near] * len(ins),
        out_specs=(near,) * len(outs),
        scratch_shapes=[pltpu.VMEM(shape, dtype) for shape, dtype in scratch],
        compiler_params=pltpu.CompilerParams(vmem_limit_bytes=16 * 2**20),
        cost_estimate=pl.CostEstimate(flops=flops, bytes_accessed=1_000, transcendentals=0),
        name=name,
    )(sides, *ins)


def per_device(
    block_input, group_ids, intr_table, ln1_gain, ln1_bias, w_qkv, b_qv, w_out, b_out,
    ln2_gain, ln2_bias, w_up, b_up, w_down, b_down, cotangent,
):
    rows_own, width = block_input.shape
    padded = -(-rows_own // 128) * 128
    groups = intr_table.shape[0]
    feat, hid = w_out.shape[0], w_down.shape[0]
    heads = feat // HEAD
    me = lax.axis_index("mp")
    bits = dp_bits()

    id_row = jnp.pad(group_ids.astype(F32)[None, :], ((0, 7), (0, padded - rows_own)), constant_values=-1)
    x_x = swap(block_input, "mp", 2)
    x_c = swap(block_input, "mp", 1)
    ids_x = swap(id_row, "mp", 2)
    ids_c = swap(id_row, "mp", 1)

    zero_row = jnp.zeros((width,), F32)
    b_three = jnp.stack((b_qv[0], jnp.zeros((feat,), F32), b_qv[1]), axis=0)
    b_row = b_three.reshape(3, heads, HEAD).transpose(1, 0, 2).reshape(3 * feat)
    params = jnp.stack(
        (
            ln1_gain, ln1_bias, b_out, ln2_gain, ln2_bias, b_down,
            jnp.pad(b_row, (0, width - 3 * feat)), zero_row,
        ),
        axis=0,
    )
    w_t = (
        w_qkv.reshape(width, 3, heads, HEAD).transpose(2, 1, 3, 0).reshape(3 * feat, width)
    )
    b_rows = jnp.stack(three_parts(b_up), axis=0)
    pack = jnp.concatenate(
        (w_out, jnp.pad(b_rows, ((0, EXTRA - 3), (0, width - hid))), w_up.T, w_down), axis=0
    )
    up_at, down_at, half = feat + EXTRA, feat + EXTRA + hid, hid // 2
    side_u, side_d = side_of(bits[0]), side_of(bits[1])
    sides = jnp.stack((side_u, side_d))
    dy = jnp.pad(cotangent, ((0, padded - rows_own), (0, 0)))
    x_x, ids_x, first_rows, params, w_t, up_near, down_near, dy, _ = sync(
        x_x, ids_x, pack[:up_at], params, w_t,
        lax.dynamic_slice_in_dim(pack, up_at + side_u * half, half, 0),
        lax.dynamic_slice_in_dim(pack, down_at + side_d * half, half, 0), dy, mark(pack),
    )
    x_xc, ids_xc = swap(x_x, "mp", 1), swap(ids_x, "mp", 1)
    up_near, down_near = swap(up_near, "mp", 2), swap(down_near, "mp", 2)
    out_x = swap(first_rows, "mp", 2)
    pack_c = swap(after(pack, x_x), "mp", 1)
    ids = (id_row, ids_c, ids_x, ids_xc)
    a1, qkv, h_all, o32, rl, *o_ts, probs = attend(
        padded, block_input, (x_c, x_x, x_xc), ids, intr_table, params, w_t
    )

    o_own, o_c, o_two = o_ts
    up_near, down_near, out_x, o_own = sync(up_near, down_near, out_x, o_own)
    o_c, o_two, up_far, down_far, _ = sync(
        swap(o_c, "mp", 1), swap(o_two, "mp", 2),
        swap(up_near, "dp", bits[0]), swap(down_near, "dp", bits[1]), mark(rl),
    )
    o_ts = (o_own, o_c, o_two[0], swap(o_two[1], "mp", 1))
    pieces = (out_x, up_near, up_far, down_near, down_far)
    pieces = pieces + tuple(swap(p, "mp", 1) for p in pieces)
    mixed, dh1, small_own, db_up, *do_ts, keep_g, send_g = own_part(
        rows_own, groups, (hid, feat), sides, h_all, id_row, dy, params,
        (pack, pack_c), pieces, o_ts,
    )
    do_own = do_ts[0]
    first, second, full, *rest = bits
    do_c, do_x, do_xc, got_g, _ = sync(
        *(swap(do_ts[j], "mp", j) for j in (1, 2, 3)), swap(send_g, "mp", 1), mark(small_own)
    )

    w = width
    n_a, n_b, n_c, n_q, n_r = hid // 4, hid // 4, feat // 4, 2 * feat // 4, feat // 4

    def stage_0(u, d, ins, outs):
        keep, got = ins[:2]
        a_sent, a_kept, b_sent, b_kept, c_sent, c_kept, d_out = outs
        for j in range(4):
            d_out[:, j * padded : (j + 1) * padded] = ins[2 + j][...]
        a_sent[...] = plus(keep[1, :hid], got[1, :hid])
        a_kept[...] = plus(keep[0, :hid], got[0, :hid])
        for out, side in ((b_sent, 1 - u), (b_kept, u)):
            for z in range(2):
                rows = pl.ds(pl.multiple_of(hid + (2 * side + z) * n_b, 16), n_b)
                out[:, 0, z] = plus(keep[:, rows], got[:, rows])
        for out, side in ((c_sent, 1 - d), (c_kept, d)):
            for y in range(2):
                rows = pl.ds(pl.multiple_of(2 * hid + (2 * y + side) * n_c, 16), n_c)
                out[:, y, 0] = plus(keep[:, rows], got[:, rows])

    a_sent, a_kept, b_sent, b_kept, c_sent, c_kept, d_out = stage(
        "stage_0", sides, (keep_g, got_g, do_own, do_c, do_x, do_xc),
        [((hid, w), BF)] * 2 + [((2, 1, 2, n_b, w), BF)] * 2 + [((2, 2, 1, n_c, w), BF)] * 2
        + [((feat, 4 * padded), BF)],
        stage_0,
    )
    a_got, b_got, c_got = swap(a_sent, "mp", 2), swap(b_sent, "dp", first), swap(c_sent, "dp", second)
    d_out, a_kept, b_kept, c_kept = sync(d_out, a_kept, b_kept, c_kept)
    dqkv_1, do_rest, dw_1 = back_1(heads - 1, d_out, a1, qkv, probs, o32, rl)

    def stage_1(u, d, ins, outs):
        a_kept, a_got, b_kept, b_got, q, c_kept, c_got = ins
        for k, at in enumerate((pl.ds(1 - u, 1), pl.ds(u, 1))):
            outs[k][:, :, :n_a] = plus(a_kept[at], a_got[at])
            outs[k][:, :, n_a:] = q[at]
        for k, at in enumerate((pl.ds(1 - d, 1), pl.ds(d, 1))):
            outs[2 + k][...] = plus(b_kept[:, :, at], b_got[:, :, at])
            outs[4 + k][...] = plus(c_kept[1 - k], c_got[1 - k])

    cut_a, cut_q, cut_r = (2, 2, n_a, w), (2, 2, n_q, w), (2, 2, n_r, w)
    n_aq = n_a + n_q
    aq_sent, aq_kept, b_sent, b_kept, c_sent, c_kept = stage(
        "stage_1", sides,
        (a_kept.reshape(cut_a), a_got.reshape(cut_a), b_kept, b_got, dw_1.reshape(cut_q), c_kept, c_got),
        [((1, 2, n_aq, w), BF)] * 2 + [((2, 1, 1, n_b, w), BF)] * 2 + [((2, 1, n_c, w), BF)] * 2,
        stage_1,
    )
    aq_got, b_got, c_got = swap(aq_sent, "dp", first), swap(b_sent, "dp", second), swap(c_sent, "mp", 2)
    aq_kept, b_kept, c_kept, dqkv_1 = sync(aq_kept, b_kept, c_kept, dqkv_1)
    dw_2, send, keep, small = back_2(
        me.reshape(1), groups, 1, do_rest, ids, h_all, a1, qkv, probs, o32, rl, params, w_t, dqkv_1,
        small_own, db_up,
    )
    aq_got, b_got, c_got, dw_2, send, keep, small = sync(
        aq_got, b_got, c_got, dw_2, send, keep, small
    )

    def stage_2(u, d, ins, outs):
        aq_kept, aq_got, b_kept, b_got, r, c_kept, c_got = ins
        for k, at in enumerate((pl.ds(1 - d, 1), pl.ds(d, 1))):
            outs[k][...] = plus(aq_kept[:, at], aq_got[:, at])
        for k in range(2):
            outs[2 + k][...] = plus(b_kept[1 - k], b_got[1 - k])
        for k, at in enumerate((pl.ds(1 - u, 1), pl.ds(u, 1))):
            outs[4 + k][...] = r[at]
            outs[6 + k][...] = plus(c_kept[at], c_got[at])

    aq_sent, aq_kept, b_sent, b_kept, r_sent, r_kept, c_sent, c_kept = stage(
        "stage_2", sides, (aq_kept, aq_got, b_kept, b_got, dw_2.reshape(cut_r), c_kept, c_got),
        [((1, 1, n_aq, w), BF)] * 2 + [((1, 1, n_b, w), BF)] * 2 + [((1, 2, n_r, w), BF)] * 2
        + [((1, 1, n_c, w), BF)] * 2,
        stage_2,
    )
    aq_got, b_got, r_got, t_got = (
        swap(aq_sent, "dp", second), swap(b_sent, "mp", 2), swap(r_sent, "dp", first),
        swap(send, "mp", 1),
    )
    s_got = [swap(small, "mp", bit) for bit in (1, 2, 3)]

    def stage_3(u, d, ins, outs):
        aq_kept, aq_got, b_kept, b_got, r_kept, r_got, keep, t_got = ins[:8]
        s_0, s_1, s_2, s_3, c_sent = ins[8:]
        outs[7][...] = c_sent[...]
        outs[0][:, :, :n_a] = plus(aq_kept[:, :, :n_a], aq_got[:, :, :n_a])
        outs[0][:, :, n_a:] = plus(b_kept[...], b_got[...])
        outs[1][...] = plus(aq_kept[:, :, n_a:], aq_got[:, :, n_a:])
        for k, at in enumerate((pl.ds(1 - d, 1), pl.ds(d, 1))):
            outs[2 + k][...] = plus(r_kept[:, at], r_got[:, at])
        outs[4][...] = plus(keep[padded:], t_got[padded:])
        outs[5][...] = plus(keep[:padded], t_got[:padded])
        outs[6][...] = (s_0[...] + s_1[...]) + (s_2[...] + s_3[...])

    one_a, one_b, one_c, one_q, one_r = ((1, 1, n, w) for n in (n_a, n_b, n_c, n_q, n_r))
    ab, q, r_sent, r_kept, t_sent, t_kept, small, c_sent = stage(
        "stage_3", sides,
        (aq_kept, aq_got, b_kept, b_got, r_kept, r_got, keep, t_got,
         small, *s_got, c_sent),
        [((1, 1, n_a + n_b, w), BF), (one_q, BF), (one_r, BF), (one_r, BF)]
        + [((padded, w), BF)] * 2 + [(small.shape, F32), (one_c, BF)],
        stage_3,
    )
    ab_got, r_got, t_got, s_got = (
        swap(ab, "dp", full), swap(r_sent, "dp", second), swap(t_sent, "mp", 2),
        swap(small, "dp", first),
    )
    c_got = swap(c_sent, "dp", first)

    def stage_4(u, d, ins, outs):
        ab, ab_got, q, r_kept, r_got, small, s_got, c_kept, c_got, _ = ins
        outs[0][...] = plus(ab[:, :, :n_a], ab_got[:, :, :n_a])
        outs[1][...] = plus(ab[:, :, n_a:], ab_got[:, :, n_a:])
        outs[2][:, :, :n_q] = q[...]
        outs[2][:, :, n_q : n_q + n_r] = plus(r_kept[...], r_got[...])
        outs[2][:, :, n_q + n_r :] = plus(c_kept[...], c_got[...])
        outs[3][...] = small[...] + s_got[...]

    a, b, q, small = stage(
        "stage_4", sides, (ab, ab_got, q, r_kept, r_got, small, s_got, c_kept, c_got, t_got),
        [(one_a, BF), (one_b, BF), ((1, 1, n_q + n_r + n_c, w), BF), ((groups + 16, w), F32)], stage_4,
    )
    for bit in rest:
        small = small + swap(small, "dp", bit)
        a, b = plus(a, swap(a, "dp", bit)), plus(b, swap(b, "dp", bit))
    a_got, b_got, q_got, s_got = (
        swap(a, "dp", first), swap(b, "dp", second), swap(q, "dp", full), swap(small, "dp", second)
    )
    dh0 = dh1 + t_kept.astype(F32) + t_got.astype(F32)
    input_grad = dh0[:rows_own].astype(BF)
    q_got = after(q_got, input_grad)
    h = (n_q + n_r + n_c) // 32 * 16
    h_1 = n_q + n_r + n_c - h

    def stage_5(u, d, ins, outs):
        a, a_got, b, b_got, q, q_got, small, s_got = ins
        a_o, b_o, q_0, q_1, s_o = outs
        a_o[pl.ds(u, 1)] = a[...]
        a_o[pl.ds(1 - u, 1)] = a_got[...]
        b_o[:, pl.ds(d, 1)] = b[...]
        b_o[:, pl.ds(1 - d, 1)] = b_got[...]
        q_0[...] = plus(q[:, :, :h], q_got[:, :, :h])
        q_1[...] = plus(q[:, :, h:], q_got[:, :, h:])
        s_o[...] = small[...] + s_got[...]

    a, b, q_0, q_1, small = stage(
        "stage_5", sides, (a, a_got, b, b_got, q, q_got, small, s_got),
        [((2, 1, n_a, w), BF), ((1, 2, n_b, w), BF), ((1, 1, h, w), BF), ((1, 1, h_1, w), BF),
         (small.shape, F32)],
        stage_5,
    )
    for bit in rest:
        q_0, q_1 = plus(q_0, swap(q_0, "dp", bit)), plus(q_1, swap(q_1, "dp", bit))
    a_got, b_got, q_0_got, q_1_got, s_got = (
        swap(a, "dp", second), swap(b, "dp", first), swap(q_0, "dp", first), swap(q_1, "dp", second),
        swap(small, "dp", full),
    )

    def stage_6(u, d, ins, outs):
        q_0, q_0_got, q_1, q_1_got, small, s_got = ins
        q_0_o, q_1_o, s_o = outs
        s_o[...] = small[...] + s_got[...]
        q_0_o[pl.ds(u, 1)] = q_0[...]
        q_0_o[pl.ds(1 - u, 1)] = q_0_got[...]
        q_1_o[:, pl.ds(d, 1)] = q_1[...]
        q_1_o[:, pl.ds(1 - d, 1)] = q_1_got[...]

    q_0, q_1, small = stage(
        "stage_6", sides, (q_0, q_0_got, q_1, q_1_got, small, s_got),
        [((2, 1, h, w), BF), ((1, 2, h_1, w), BF), (small.shape, F32)], stage_6,
    )
    q_0_got, q_1_got = swap(q_0, "dp", second), swap(q_1, "dp", first)

    def stage_7(u, d, ins, outs):
        a, a_got, b, b_got = ins[:4]
        up_o, down_o, chunk_a = outs
        for y in range(2):
            for z, src in ((d, a), (1 - d, a_got)):
                at = pl.multiple_of((2 * y + z) * n_a, 16)
                chunk_a[pl.ds(at, n_a), :] = src[y, 0].astype(F32)
        for z in range(2):
            for y, src in ((u, b), (1 - u, b_got)):
                at = pl.multiple_of((2 * y + z) * n_b, 16)
                down_o[pl.ds(at, n_b), :] = src[0, z].astype(F32)
        up_o[...] = jnp.transpose(chunk_a[...])

    g_up, g_down = stage(
        "stage_7", sides, (a, a_got, b, b_got, q_0),
        [((w, hid), F32), ((hid, w), F32)], stage_7, [((hid, w), F32)], 20_000_000_000,
    )

    def doubled(cur, got, side, axis):
        return jnp.where(
            side == 0,
            jnp.concatenate((cur, got), axis=axis),
            jnp.concatenate((got, cur), axis=axis),
        )

    q_all = jnp.concatenate(
        (doubled(q_0, q_0_got, side_d, 1), doubled(q_1, q_1_got, side_u, 0)), axis=2
    )
    g_qkv = jnp.concatenate(
        (q_all[:, :, :n_q].reshape(-1, w), q_all[:, :, n_q : n_q + n_r].reshape(-1, w)), axis=0
    )
    g_out = q_all[:, :, n_q + n_r :].reshape(-1, w).astype(F32)
    at = groups
    up_at = at + 6
    qv_at = at + 8
    b_up_grad = lax.dynamic_slice(small[up_at:qv_at].reshape(4, hid), (me, 0), (1, hid))[0]
    db = lax.dynamic_slice(small, (qv_at + me, 0), (1, 3 * feat)).reshape(heads, 3, HEAD)
    b_qv_grad = jnp.stack((db[:, 0].reshape(feat), db[:, 2].reshape(feat)), axis=0)
    g_qkv = g_qkv.astype(F32)
    w_qkv_grad = (
        g_qkv.reshape(heads, 3, HEAD, width).transpose(3, 1, 0, 2).reshape(width, 3, feat)
    )
    return (
        mixed,
        input_grad,
        small[:groups],
        small[at + 4],
        small[at + 5],
        w_qkv_grad,
        b_qv_grad,
        g_out,
        small[at],
        small[at + 1],
        small[at + 2],
        g_up,
        b_up_grad,
        g_down,
        small[at + 3],
    )


def solution(mesh):
    rows = P(("dp", "mp"), None)
    return jax.shard_map(
        per_device,
        mesh=mesh,
        in_specs=(
            rows, P(("dp", "mp")), P(), P(), P(), P(None, None, "mp"), P(None, "mp"), P("mp", None),
            P(), P(), P(), P(None, "mp"), P("mp"), P("mp", None), P(), rows,
        ),
        out_specs=(
            rows, rows, P(), P(), P(), P(None, None, "mp"), P(None, "mp"), P("mp", None),
            P(), P(), P(), P(None, "mp"), P("mp"), P("mp", None), P(),
        ),
        check_vma=False,
    )
```
